32 devices in a mesh: rep: 4 (over z), fsdp: 8 (over y, x, core).
Axes of the slice: x: 2, y: 2, z: 4, core: 2. Of those that a mesh axis runs over, the one named last changes fastest.
Arguments:
- enc_in: bfloat16 [8192, 768], P(('rep', 'fsdp')), may hold values from -6 to 6
- dec_in: bfloat16 [8192, 768], P(('rep', 'fsdp')), may hold values from -6 to 6
- bucket: int32 [32], P(('rep', 'fsdp')), may hold values from 0 to 1, as said below
- enc_lengths: int32 [32, 4], P(('rep', 'fsdp')), may hold values from 0 to 256, as said below
- dec_lengths: int32 [32, 4], P(('rep', 'fsdp')), may hold values from 0 to 256, as said below
- enc_attn: bfloat16 [768, 3072], P('fsdp'), may hold values from -3 to 3
- enc_vec: bfloat16 [9216], P('fsdp'), may hold values from -1.2 to 1.6
- enc_w1: bfloat16 [768, 3072], P('fsdp'), may hold values from -0.21875 to 0.21875
- enc_w2: bfloat16 [3072, 768], P('fsdp'), may hold values from -0.109375 to 0.109375
- dec_attn: bfloat16 [768, 6144], P('fsdp'), may hold values from -3 to 3
- dec_vec: bfloat16 [13056], P('fsdp'), may hold values from -1.2 to 1.6
- dec_w1: bfloat16 [768, 3072], P('fsdp'), may hold values from -0.21875 to 0.21875
- dec_w2: bfloat16 [3072, 768], P('fsdp'), may hold values from -0.109375 to 0.109375
- enc_cot: bfloat16 [8192, 768], P(('rep', 'fsdp')), may hold values from -6 to 6
- dec_cot: bfloat16 [8192, 768], P(('rep', 'fsdp')), may hold values from -6 to 6
Outputs:
- enc_out: bfloat16 [8192, 768], P(('rep', 'fsdp'))
- dec_out: bfloat16 [8192, 768], P(('rep', 'fsdp'))
- enc_in_grad: float32 [8192, 768], P(('rep', 'fsdp'))
- dec_in_grad: float32 [8192, 768], P(('rep', 'fsdp'))
- enc_attn_grad: float32 [768, 3072], P('fsdp')
- enc_vec_grad: float32 [9216], P('fsdp')
- enc_w1_grad: float32 [768, 3072], P('fsdp')
- enc_w2_grad: float32 [3072, 768], P('fsdp')
- dec_attn_grad: float32 [768, 6144], P('fsdp')
- dec_vec_grad: float32 [13056], P('fsdp')
- dec_w1_grad: float32 [768, 3072], P('fsdp')
- dec_w2_grad: float32 [3072, 768], P('fsdp')
The draws below stay inside these ranges and needn't reach their ends.
Inputs may be any that keep to these rules, and one draw needn't show every extreme that they name: Some block has bucket 1 in every draw. In a block with bucket 1, entry 0 is the length of its one sequence, half of 256 or more, and the other entries are 0; with bucket 0 all 4 entries are lengths between a quarter of 64 (rounded down) and 64. Some block with bucket 1 has length 256 in every draw, in enc_lengths and dec_lengths alike. `dec_lengths`: as for enc_lengths.
All inputs are finite; a program needn't handle non-finite values.
Results may differ from the reference program's by a relative error of at most 0.03.
Values may be sent and summed in bfloat16 or wider, within the bound.
No kernel may reach another device: no remote copies, remote signals or barrier semaphores. Data moves between devices by JAX's collectives and lax.ppermute only.
A program may use at most 256 MiB of HBM per device.

```python
import math
import jax
import jax.numpy as jnp
from jax import lax

D = 768
FF = 3072
HEAD = 64
TOK_DEV = 256
SEGS = 4
SEG_LEN = 64
SLABS = 32
TOKENS = 8192
N_REP = 4
N_FSDP = 8


def layout(source):
    chosen = jax.random.randint(jax.random.fold_in(source, 101), (), 0, SLABS)
    bucket = jax.random.randint(jax.random.fold_in(source, 102), (SLABS,), 0, 2)
    bucket = jnp.where(jnp.arange(SLABS) == chosen, 1, bucket).astype(jnp.int32)
    return (bucket, chosen)


def lengths_for(shared, own_key):
    bucket, chosen = shared
    full_len = jax.random.randint(jax.random.fold_in(own_key, 1), (SLABS,), TOK_DEV // 2, TOK_DEV + 1)
    full_len = jnp.where(jnp.arange(SLABS) == chosen, TOK_DEV, full_len)
    short_len = jax.random.randint(jax.random.fold_in(own_key, 2), (SLABS, SEGS), SEG_LEN // 4, SEG_LEN + 1)
    lead_slot = (jnp.arange(SEGS) == 0)[None, :]
    long_rows = jnp.where(lead_slot, full_len[:, None], 0)
    return jnp.where(bucket[:, None] == 1, long_rows, short_len).astype(jnp.int32)


def attention_draw(source, blocks):
    normal = jnp.clip(jax.random.normal(source, (D, blocks, 4, D), jnp.float32), -6.0, 6.0)
    scales = jnp.array([1.5, 1.5, 1.0, 5.0], jnp.float32) / math.sqrt(D)
    return (normal * scales[None, None, :, None]).reshape(D, blocks * 4 * D).astype(jnp.bfloat16)


def vector_draw(source, row_count, gain_rows):
    length_all = row_count * D + FF
    normal = jnp.clip(jax.random.normal(source, (length_all,), jnp.float32), -6.0, 6.0)
    row_id = jnp.arange(length_all) // D
    is_gain = jnp.zeros((length_all,), jnp.bool_)
    for gain_row in gain_rows:
        is_gain = is_gain | (row_id == gain_row)
    return jnp.where(is_gain, 1.0 + 0.1 * normal, 0.2 * normal).astype(jnp.bfloat16)


def draw_bucket(key, part):
    shared = layout(key)
    return shared[0]


def draw_enc_lengths(key, part):
    shared = layout(key)
    key = jax.random.fold_in(key, 8)
    return lengths_for(shared, key)


def draw_dec_lengths(key, part):
    shared = layout(key)
    key = jax.random.fold_in(key, 9)
    return lengths_for(shared, key)


def draw_enc_attn(key, part):
    key = jax.random.fold_in(key, 11)
    return attention_draw(key, 1)


def draw_dec_attn(key, part):
    key = jax.random.fold_in(key, 12)
    return attention_draw(key, 2)


def draw_enc_vec(key, part):
    key = jax.random.fold_in(key, 13)
    return vector_draw(key, 8, (3, 6))


def draw_dec_vec(key, part):
    key = jax.random.fold_in(key, 14)
    return vector_draw(key, 13, (3, 8, 11))


def steps_of(key, extent, shards, low, top_value):
    def one(position, parts):
        draws = jax.random.uniform(jax.random.fold_in(jax.random.fold_in(key, 6), position), (parts,), jnp.float32, low / len(shards), top_value / len(shards))
        return jnp.repeat(jnp.exp(draws), extent[position] // parts).reshape((-1,) + (1,) * (len(extent) - position - 1))

    level = one(*shards[0])
    for cut in shards[1:]:
        level = level * one(*cut)
    return level


def noise(key, dims, deviation, bound, cuts=(), kind=jnp.bfloat16):
    entries = jax.random.normal(key, dims, jnp.float32) * deviation
    if len(cuts) > 0:
        entries = steps_of(key, dims, cuts, -0.22, 0.18) * entries
    return jnp.clip(entries, min=-bound, max=bound).astype(kind)


def setup_inputs(seed: int = 0) -> dict:
    streams_of = jax.random.split(jax.random.key(seed), 16)
    return {
        "enc_in": noise(streams_of[0], (TOKENS, D), 1.0, 6.0, ((0, 32),)),
        "dec_in": noise(streams_of[1], (TOKENS, D), 1.0, 6.0, ((0, 32),)),
        "bucket": draw_bucket(jax.random.fold_in(streams_of[15], 71), 0),
        "enc_lengths": draw_enc_lengths(jax.random.fold_in(streams_of[15], 71), 0),
        "dec_lengths": draw_dec_lengths(jax.random.fold_in(streams_of[15], 71), 0),
        "enc_attn": draw_enc_attn(jax.random.fold_in(streams_of[15], 71), 0),
        "enc_vec": draw_enc_vec(jax.random.fold_in(streams_of[15], 71), 0),
        "enc_w1": noise(streams_of[7], (D, FF), D ** -0.5, 0.21875, ((0, 8),)),
        "enc_w2": noise(streams_of[8], (FF, D), FF ** -0.5, 0.109375, ((0, 8),)),
        "dec_attn": draw_dec_attn(jax.random.fold_in(streams_of[15], 71), 0),
        "dec_vec": draw_dec_vec(jax.random.fold_in(streams_of[15], 71), 0),
        "dec_w1": noise(streams_of[11], (D, FF), D ** -0.5, 0.21875, ((0, 8),)),
        "dec_w2": noise(streams_of[12], (FF, D), FF ** -0.5, 0.109375, ((0, 8),)),
        "enc_cot": noise(streams_of[13], (TOKENS, D), 1.0, 6.0, ((0, 32),)),
        "dec_cot": noise(streams_of[14], (TOKENS, D), 1.0, 6.0, ((0, 32),)),
    }


EPSILON = 1e-05
NEG_FILL = -1e+30
SCORE_SCALE = 0.125

@jax.custom_vjp
def low(v):
    return lax.optimization_barrier(v.astype(jnp.bfloat16)).astype(jnp.float32)

@jax.custom_vjp
def low_back(v):
    return v

def low_keep(v):
    return (low(v), None)

def low_pass(kept, grad):
    return (grad,)

def back_keep(v):
    return (v, None)

def back_low(kept, grad):
    return (low(grad),)
low.defvjp(low_keep, low_pass)
low_back.defvjp(back_keep, back_low)

def matmul(first_op, second_op):
    return jnp.dot(first_op, second_op, precision=lax.Precision.HIGHEST)

def norm_rows(hidden, gain_row, shift_row):
    row_mean = lax.optimization_barrier(jnp.mean(hidden, axis=-1, keepdims=True))
    centred = hidden - row_mean
    variance = lax.optimization_barrier(jnp.mean(centred * centred, axis=-1, keepdims=True))
    return centred * lax.rsqrt(variance + EPSILON) * gain_row + shift_row

def build_masks(one_long, enc_len, dec_len, row_total, seg_count):
    span_rows = jnp.where(one_long == 1, row_total, row_total // seg_count).astype(jnp.int32)
    row_index = jnp.arange(row_total, dtype=jnp.int32)
    group_id = row_index // span_rows
    row_place = row_index - group_id * span_rows
    in_group = group_id[:, None] == jnp.arange(seg_count, dtype=jnp.int32)[None, :]
    enc_live = row_place < lax.optimization_barrier(jnp.sum(jnp.where(in_group, enc_len[None, :], 0), axis=1))
    dec_live = row_place < lax.optimization_barrier(jnp.sum(jnp.where(in_group, dec_len[None, :], 0), axis=1))
    same_group = group_id[:, None] == group_id[None, :]
    enc_mask = same_group & enc_live[None, :]
    self_mask = same_group & dec_live[None, :] & (row_index[None, :] <= row_index[:, None])
    return (enc_mask, self_mask, enc_mask)

def attention(q_in, kv_in, weights, bias_q, bias_v, bias_o, key_mask):
    row_total, feature = q_in.shape
    head_count = feature // HEAD
    queries = low(low_back(matmul(q_in, weights[:, :feature])) + bias_q).reshape(row_total, head_count, HEAD)
    keys_low = low(low_back(matmul(kv_in, weights[:, feature:2 * feature]))).reshape(row_total, head_count, HEAD)
    values = low(low_back(matmul(kv_in, weights[:, 2 * feature:3 * feature])) + bias_v).reshape(row_total, head_count, HEAD)
    raw_score = low_back(jnp.einsum('qhd,khd->hqk', queries, keys_low, precision=lax.Precision.HIGHEST))
    probs = jax.nn.softmax(jnp.where(key_mask[None], raw_score * SCORE_SCALE, NEG_FILL), axis=-1)
    mixed = jnp.einsum('hqk,khd->qhd', low(probs), values, precision=lax.Precision.HIGHEST).reshape(row_total, feature)
    mixed = low(low_back(mixed))
    return low_back(matmul(mixed, weights[:, 3 * feature:4 * feature])) + bias_o

def feed(rows_in, w_in, b_in, w_out, b_out):
    hidden = low_back(matmul(rows_in, w_in)) + b_in
    active = low(jax.nn.gelu(hidden, approximate=False))
    return low_back(matmul(active, w_out)) + b_out

def slab_forward(params, enc_rows, dec_rows, all_masks):
    e_attn, e_vec, e_in, e_out, d_attn, d_vec, d_in, d_out = params
    feature = enc_rows.shape[1]
    e_rows = e_vec[:8 * feature].reshape(8, feature)
    e_tail = e_vec[8 * feature:]
    d_rows = d_vec[:13 * feature].reshape(13, feature)
    d_tail = d_vec[13 * feature:]
    enc_mask, self_mask, cross_mask = all_masks
    hidden = enc_rows + attention(enc_rows, enc_rows, e_attn, e_rows[0], e_rows[1], e_rows[2], enc_mask)
    first_out = low(norm_rows(hidden, e_rows[3], e_rows[4]))
    hidden = first_out + feed(first_out, e_in, e_tail, e_out, e_rows[5])
    encoded = low(norm_rows(hidden, e_rows[6], e_rows[7]))
    hidden = dec_rows + attention(dec_rows, dec_rows, d_attn[:, :4 * feature], d_rows[0], d_rows[1], d_rows[2], self_mask)
    first_out = low(norm_rows(hidden, d_rows[3], d_rows[4]))
    hidden = first_out + attention(first_out, encoded, d_attn[:, 4 * feature:], d_rows[5], d_rows[6], d_rows[7], cross_mask)
    second = low(norm_rows(hidden, d_rows[8], d_rows[9]))
    hidden = second + feed(second, d_in, d_tail, d_out, d_rows[10])
    decoded = low(norm_rows(hidden, d_rows[11], d_rows[12]))
    return (encoded, decoded)

def reference(enc_in, dec_in, bucket, enc_lengths, dec_lengths, enc_attn, enc_vec, enc_w1, enc_w2, dec_attn, dec_vec, dec_w1, dec_w2, enc_cot, dec_cot):
    params = tuple((item.astype(jnp.float32) for item in (enc_attn, enc_vec, enc_w1, enc_w2, dec_attn, dec_vec, dec_w1, dec_w2)))
    slab_total = N_REP * N_FSDP
    feature = enc_in.shape[1]

    def by_slab(array):
        return array.reshape(slab_total, TOK_DEV, feature)

    def slab_step(totals, slab_items):
        enc_rows, dec_rows, one_long, enc_len, dec_len, enc_grad_in, dec_grad_in = slab_items
        all_masks = build_masks(one_long, enc_len, dec_len, TOK_DEV, SEGS)

        def forward(weights, enc_part, dec_part):
            return slab_forward(weights, enc_part, dec_part, all_masks)
        layer_outs, pullback = jax.vjp(forward, params, enc_rows.astype(jnp.float32), dec_rows.astype(jnp.float32))
        gradients, enc_back, dec_back = pullback((enc_grad_in.astype(jnp.float32), dec_grad_in.astype(jnp.float32)))
        totals = jax.tree.map(jnp.add, totals, gradients)
        return (totals, (layer_outs[0].astype(jnp.bfloat16), layer_outs[1].astype(jnp.bfloat16), enc_back, dec_back))
    empty_grads = jax.tree.map(jnp.zeros_like, params)
    totals, results = lax.scan(slab_step, empty_grads, (by_slab(enc_in), by_slab(dec_in), bucket, enc_lengths, dec_lengths, by_slab(enc_cot), by_slab(dec_cot)))
    enc_out, dec_out, enc_back, dec_back = results
    return (enc_out.reshape(-1, feature), dec_out.reshape(-1, feature), enc_back.reshape(-1, feature), dec_back.reshape(-1, feature), totals[0], totals[1], totals[2], totals[3], totals[4], totals[5], totals[6], totals[7])
```

```python
import functools

import jax
import jax.numpy as jnp
from jax import lax
from jax.experimental import pallas as pl
from jax.experimental.pallas import tpu as pltpu
from jax.sharding import PartitionSpec as P

HEAD = 64
ROW_TILE = 16


EPSILON = 1e-05
NEG_FILL = -1e30
SCORE_SCALE = 0.125


def norm_rows(hidden, gain_row, shift_row):
    row_mean = jnp.mean(hidden, axis=-1, keepdims=True)
    centred = hidden - row_mean
    variance = jnp.mean(centred * centred, axis=-1, keepdims=True)
    return centred * lax.rsqrt(variance + EPSILON) * gain_row + shift_row


def norm_back(hidden, gain_row, shift_row, gradient):
    unused, pullback = jax.vjp(norm_rows, hidden, gain_row, shift_row)
    return pullback(gradient)


def gelu_exact(hidden):
    return jax.nn.gelu(hidden, approximate=False)


def dot_plain(first_op, second_op):
    return jnp.dot(first_op, second_op, preferred_element_type=jnp.float32)


def dot_left(first_op, second_op):
    return lax.dot_general(
        first_op, second_op, (((0,), (0,)), ((), ())), preferred_element_type=jnp.float32
    )


def dot_right(first_op, second_op):
    return lax.dot_general(
        first_op, second_op, (((1,), (1,)), ((), ())), preferred_element_type=jnp.float32
    )


def build_masks(one_long, enc_len, dec_len, row_total, seg_count):
    span_rows = jnp.where(one_long == 1, row_total, row_total // seg_count).astype(jnp.int32)
    row_index = jnp.arange(row_total, dtype=jnp.int32)
    group_id = row_index // span_rows
    row_place = row_index - group_id * span_rows
    in_group = group_id[:, None] == jnp.arange(seg_count, dtype=jnp.int32)[None, :]
    enc_live = row_place < jnp.sum(jnp.where(in_group, enc_len[None, :], 0), axis=1)
    dec_live = row_place < jnp.sum(jnp.where(in_group, dec_len[None, :], 0), axis=1)
    same_group = group_id[:, None] == group_id[None, :]
    enc_mask = same_group & enc_live[None, :]
    self_mask = same_group & dec_live[None, :] & (row_index[None, :] <= row_index[:, None])
    return (enc_mask, self_mask, enc_mask)


def unpack(vector, row_count, feature):
    rows_part = vector[: row_count * feature].astype(jnp.float32).reshape(row_count, feature)
    return (rows_part, vector[row_count * feature :].astype(jnp.float32))


def fetch(attn_rows, vec_part, w_in, w_out):
    return (
        lax.all_gather(attn_rows, "fsdp", axis=0, tiled=True),
        lax.all_gather(vec_part, "fsdp", axis=0, tiled=True),
        lax.all_gather(w_in, "fsdp", axis=0, tiled=True),
        lax.all_gather(w_out, "fsdp", axis=0, tiled=True),
    )


def reduce_grads(grad_attn, grad_vec, grad_in, grad_out):
    shard = (
        lax.psum_scatter(
            grad_attn.astype(jnp.bfloat16), "fsdp", scatter_dimension=0, tiled=True
        ).astype(jnp.float32),
        lax.psum_scatter(
            grad_vec.astype(jnp.bfloat16), "fsdp", scatter_dimension=0, tiled=True
        ).astype(jnp.float32),
        lax.psum_scatter(
            grad_in.astype(jnp.bfloat16), "fsdp", scatter_dimension=0, tiled=True
        ).astype(jnp.float32),
        lax.psum_scatter(
            grad_out.astype(jnp.bfloat16), "fsdp", scatter_dimension=0, tiled=True
        ).astype(jnp.float32),
    )
    return (
        lax.psum(shard[0].astype(jnp.bfloat16), "rep").astype(jnp.float32),
        lax.psum(shard[1].astype(jnp.bfloat16), "rep").astype(jnp.float32),
        lax.psum(shard[2].astype(jnp.bfloat16), "rep").astype(jnp.float32),
        lax.psum(shard[3].astype(jnp.bfloat16), "rep").astype(jnp.float32),
    )


def swap(value, bit):
    return lax.ppermute(value, "fsdp", [(i, i ^ bit) for i in range(8)])


def tile_up(rows):
    return -(-rows // ROW_TILE) * ROW_TILE


def piece_plan(shards, feature):
    plan = []
    offset = 0
    for index, (rows, columns) in enumerate(shards):
        for block in range(columns // feature):
            plan.append((index, rows, block, offset))
            offset += rows
    return (plan, offset)


def pack_shards(shards, feature):
    parts = []
    for shard in shards:
        for block in range(shard.shape[1] // feature):
            parts.append(shard[:, block * feature : (block + 1) * feature])
    return jnp.concatenate(parts, axis=0)


def vec_rows(vec_part, feature):
    rows = tile_up(-(-vec_part.shape[0] // feature))
    padded = jnp.pad(vec_part, (0, rows * feature - vec_part.shape[0]))
    return padded.reshape(rows, feature)


def gather_piece(packed):
    cut = tile_up(packed.shape[0] // 2)
    from_x = swap(packed, 2)
    from_y = swap(packed, 4)
    corner_top = swap(from_x[:cut], 4)
    corner_low = swap(from_y[cut:], 2)
    mine = [packed, from_x, from_y, corner_top, corner_low]
    return mine + [swap(value, 1) for value in mine]


def unpack_body(plan, cut, table, *refs):
    sources, outs, sems = refs[:10], refs[10:-1], refs[-1]
    copies = []

    def add(source, first, count, out, row, column):
        feature = source.shape[1]
        copies.append(
            pltpu.make_async_copy(
                source.at[pl.ds(first, count), :],
                out.at[pl.ds(row, count), pl.ds(column * feature, feature)],
                sems.at[len(copies)],
            )
        )

    for core in range(2):
        group = sources[5 * core : 5 * core + 5]
        for chip in range(4):
            place = table[2 * chip + core]
            for index, rows, block, offset in plan:
                row = pl.multiple_of(place * rows, ROW_TILE)
                if chip < 3:
                    add(group[chip], offset, rows, outs[index], row, block)
                    continue
                top = max(0, min(cut - offset, rows))
                if top > 0:
                    add(group[3], offset, top, outs[index], row, block)
                if top < rows:
                    row = pl.multiple_of(row + top, ROW_TILE)
                    add(group[4], offset + top - cut, rows - top, outs[index], row, block)
    for copy in copies:
        copy.start()
    for copy in copies:
        copy.wait()


def unpack_piece(sources, table, shards, feature):
    plan, total = piece_plan(shards, feature)
    cut = tile_up(total // 2)
    return pl.pallas_call(
        functools.partial(unpack_body, plan, cut),
        out_shape=[
            jax.ShapeDtypeStruct((8 * rows, columns), jnp.bfloat16) for rows, columns in shards
        ],
        in_specs=[pl.BlockSpec(memory_space=pltpu.SMEM)] + [pl.BlockSpec(memory_space=pl.ANY)] * 10,
        out_specs=[pl.BlockSpec(memory_space=pl.ANY)] * len(shards),
        scratch_shapes=[pltpu.SemaphoreType.DMA((8 * len(plan) + 2,))],
    )(table, *sources)


def pack_body(plan, count, table, *refs):
    sources, keep, send, sems = refs[:count], refs[count], refs[count + 1], refs[-1]
    copies = []
    for core, out in ((1, send), (0, keep)):
        for chip in range(4):
            place = table[2 * chip + core]
            for index, rows, block, offset in plan:
                feature = out.shape[2]
                row = pl.multiple_of(place * rows, ROW_TILE)
                copies.append(
                    pltpu.make_async_copy(
                        sources[index].at[pl.ds(row, rows), pl.ds(block * feature, feature)],
                        out.at[chip, pl.ds(offset, rows), :],
                        sems.at[len(copies)],
                    )
                )
    for copy in copies:
        copy.start()
    for copy in copies:
        copy.wait()


def pack_piece(grads, table, feature):
    shards = [(grad.shape[0] // 8, grad.shape[1]) for grad in grads]
    plan, total = piece_plan(shards, feature)
    out = jax.ShapeDtypeStruct((4, total, feature), jnp.bfloat16)
    keep, send = pl.pallas_call(
        functools.partial(pack_body, plan, len(grads)),
        out_shape=[out, out],
        in_specs=[pl.BlockSpec(memory_space=pltpu.SMEM)]
        + [pl.BlockSpec(memory_space=pl.ANY)] * len(grads),
        out_specs=[pl.BlockSpec(memory_space=pl.ANY)] * 2,
        scratch_shapes=[pltpu.SemaphoreType.DMA((8 * len(plan),))],
    )(table, *grads)
    return (keep, send, plan)


def add_low(*terms):
    total = terms[0].astype(jnp.float32)
    for term in terms[1:]:
        total = total + term.astype(jnp.float32)
    return total.astype(jnp.bfloat16)


def line_sum(value):
    place = lax.axis_index("rep")
    inner = (place == 1) | (place == 2)
    inward = lax.ppermute(value, "rep", [(0, 1), (3, 2)])
    half = add_low(value, inward)
    total = add_low(half, lax.ppermute(half, "rep", [(1, 2), (2, 1)]))
    outward = lax.ppermute(total, "rep", [(1, 0), (2, 3)])
    return jnp.where(inner, total, outward)


def reduce_piece(grads, table, feature):
    keep, send, plan = pack_piece(grads, table, feature)
    full = add_low(keep, swap(send, 1))
    cut = tile_up(full.shape[1] // 2)
    low_x = swap(full[3, :cut], 2)
    low_y = swap(full[3, cut:], 4)
    to_x = jnp.concatenate([full[1, :cut], add_low(full[1, cut:], low_y)], axis=0)
    to_y = jnp.concatenate([add_low(full[2, :cut], low_x), full[2, cut:]], axis=0)
    own = add_low(full[0], swap(to_x, 2), swap(to_y, 4))
    own = line_sum(own).astype(jnp.float32)
    results = []
    for index in range(len(grads)):
        blocks = [own[offset : offset + rows] for which, rows, block, offset in plan if which == index]
        results.append(jnp.concatenate(blocks, axis=1))
    return results


def fetch_pieces(attn_rows, vec_part, w_in, w_out, table):
    feature = w_out.shape[1]
    vec_block = vec_rows(vec_part, feature)
    first = pack_shards([attn_rows, vec_block], feature)
    second = pack_shards([w_in, w_out], feature)
    attn, vec = unpack_piece(
        gather_piece(first), table, [attn_rows.shape, vec_block.shape], feature
    )
    w_in_all, w_out_all = unpack_piece(
        gather_piece(second), table, [w_in.shape, w_out.shape], feature
    )
    vec = vec.reshape(8, -1)[:, : vec_part.shape[0]].reshape(-1)
    return (attn, vec, w_in_all, w_out_all)


def reduce_vec(grad_vec, feature):
    parts = grad_vec.astype(jnp.bfloat16).reshape(8, -1)
    rows = tile_up(-(-parts.shape[1] // feature))
    return jnp.pad(parts, ((0, 0), (0, rows * feature - parts.shape[1]))).reshape(8 * rows, feature)


def reduce_pieces(grad_attn, grad_vec, grad_in, grad_out, table):
    feature = grad_out.shape[1]
    w_in, w_out = reduce_piece(
        [grad_in.astype(jnp.bfloat16), grad_out.astype(jnp.bfloat16)], table, feature
    )
    attn, vec = reduce_piece(
        [grad_attn.astype(jnp.bfloat16), reduce_vec(grad_vec, feature)], table, feature
    )
    vec = vec.reshape(-1)[: grad_vec.shape[0] // 8]
    return (attn, vec, w_in, w_out)


def attend(q_in, kv_in, weights, biases, key_mask, one_source):
    row_total, feature = q_in.shape
    head_count = feature // HEAD
    if one_source:
        packed = dot_plain(q_in, weights[:, : 3 * feature])
        q_pre = packed[:, :feature]
        k_pre = packed[:, feature : 2 * feature]
        v_pre = packed[:, 2 * feature :]
    else:
        q_pre = dot_plain(q_in, weights[:, :feature])
        packed = dot_plain(kv_in, weights[:, feature : 3 * feature])
        k_pre = packed[:, :feature]
        v_pre = packed[:, feature:]
    queries = (q_pre + biases[0]).astype(jnp.bfloat16).reshape(row_total, head_count, HEAD)
    keys_low = k_pre.astype(jnp.bfloat16).reshape(row_total, head_count, HEAD)
    values = (v_pre + biases[1]).astype(jnp.bfloat16).reshape(row_total, head_count, HEAD)
    raw_score = jnp.einsum("qhd,khd->hqk", queries, keys_low, preferred_element_type=jnp.float32)
    probs = jax.nn.softmax(jnp.where(key_mask[None], raw_score * SCORE_SCALE, NEG_FILL), axis=-1)
    probs_low = probs.astype(jnp.bfloat16)
    mixed = jnp.einsum("hqk,khd->qhd", probs_low, values, preferred_element_type=jnp.float32)
    mixed = mixed.reshape(row_total, feature).astype(jnp.bfloat16)
    branch = dot_plain(mixed, weights[:, 3 * feature :]) + biases[2]
    return (branch, (queries, keys_low, values, probs, probs_low, mixed))


def attend_back(gradient, q_in, kv_in, weights, saved, one_source):
    queries, keys_low, values, probs, probs_low, mixed = saved
    row_total, feature = q_in.shape
    head_count = feature // HEAD
    grad_bias_o = jnp.sum(gradient, axis=0)
    grad_low = gradient.astype(jnp.bfloat16)
    grad_w_o = dot_left(mixed, grad_low)
    grad_mixed = dot_right(grad_low, weights[:, 3 * feature :]).astype(jnp.bfloat16)
    grad_mixed = grad_mixed.reshape(row_total, head_count, HEAD)
    grad_probs = jnp.einsum("qhd,khd->hqk", grad_mixed, values, preferred_element_type=jnp.float32)
    grad_values = jnp.einsum(
        "hqk,qhd->khd", probs_low, grad_mixed, preferred_element_type=jnp.float32
    )
    grad_score = probs * (grad_probs - jnp.sum(grad_probs * probs, axis=-1, keepdims=True))
    grad_raw = (grad_score * SCORE_SCALE).astype(jnp.bfloat16)
    grad_query = jnp.einsum(
        "hqk,khd->qhd", grad_raw, keys_low, preferred_element_type=jnp.float32
    ).reshape(row_total, feature)
    grad_keys = jnp.einsum(
        "hqk,qhd->khd", grad_raw, queries, preferred_element_type=jnp.float32
    ).reshape(row_total, feature)
    grad_values = grad_values.reshape(row_total, feature)
    grad_bias_q = jnp.sum(grad_query, axis=0)
    grad_bias_v = jnp.sum(grad_values, axis=0)
    low_query = grad_query.astype(jnp.bfloat16)
    low_kv = jnp.concatenate(
        [grad_keys.astype(jnp.bfloat16), grad_values.astype(jnp.bfloat16)], axis=1
    )
    if one_source:
        packed = jnp.concatenate([low_query, low_kv], axis=1)
        grad_weights = jnp.concatenate([dot_left(q_in, packed), grad_w_o], axis=1)
        grad_q_in = dot_right(packed, weights[:, : 3 * feature])
        grad_kv_in = grad_q_in
    else:
        grad_weights = jnp.concatenate(
            [dot_left(q_in, low_query), dot_left(kv_in, low_kv), grad_w_o], axis=1
        )
        grad_q_in = dot_right(low_query, weights[:, :feature])
        grad_kv_in = dot_right(low_kv, weights[:, feature : 3 * feature])
    return (grad_q_in, grad_kv_in, grad_weights, (grad_bias_q, grad_bias_v, grad_bias_o))


def feed(rows_in, w_in, b_in, w_out, b_out):
    hidden = dot_plain(rows_in, w_in) + b_in
    active = gelu_exact(hidden).astype(jnp.bfloat16)
    return (dot_plain(active, w_out) + b_out, (hidden, active))


def feed_back(gradient, rows_in, w_in, w_out, saved):
    hidden, active = saved
    grad_b_out = jnp.sum(gradient, axis=0)
    grad_low = gradient.astype(jnp.bfloat16)
    grad_w_out = dot_left(active, grad_low)
    grad_active = dot_right(grad_low, w_out)
    unused, pullback = jax.vjp(gelu_exact, hidden)
    grad_hidden = pullback(grad_active)[0]
    grad_b_in = jnp.sum(grad_hidden, axis=0)
    hidden_low = grad_hidden.astype(jnp.bfloat16)
    grad_w_in = dot_left(rows_in, hidden_low)
    grad_rows = dot_right(hidden_low, w_in)
    return (grad_rows, grad_w_in, grad_b_in, grad_w_out, grad_b_out)


def per_device(
    fsdp_size,
    rep_size,
    enc_in,
    dec_in,
    bucket,
    enc_lengths,
    dec_lengths,
    enc_attn,
    enc_vec,
    enc_w1,
    enc_w2,
    dec_attn,
    dec_vec,
    dec_w1,
    dec_w2,
    enc_cot,
    dec_cot,
):
    row_total, feature = enc_in.shape
    enc_mask, self_mask, cross_mask = build_masks(
        bucket[0], enc_lengths[0], dec_lengths[0], row_total, enc_lengths.shape[1]
    )
    small = fsdp_size == 8 and rep_size == 4
    if small:
        table = lax.axis_index("fsdp").astype(jnp.int32) ^ jnp.arange(8, dtype=jnp.int32)
        enc_weights = fetch_pieces(enc_attn, enc_vec, enc_w1, enc_w2, table)
        dec_weights = fetch_pieces(dec_attn, dec_vec, dec_w1, dec_w2, table)
    else:
        enc_weights = fetch(enc_attn, enc_vec, enc_w1, enc_w2)
        dec_weights = fetch(dec_attn, dec_vec, dec_w1, dec_w2)
    e_attn, e_vec, e_in, e_out = enc_weights
    e_rows, e_tail = unpack(e_vec, 8, feature)
    branch, e_saved_a = attend(enc_in, enc_in, e_attn, e_rows[0:3], enc_mask, True)
    e_hid_a = enc_in.astype(jnp.float32) + branch
    e_first = norm_rows(e_hid_a, e_rows[3], e_rows[4]).astype(jnp.bfloat16)
    branch, e_saved_f = feed(e_first, e_in, e_tail, e_out, e_rows[5])
    e_hid_f = e_first.astype(jnp.float32) + branch
    encoded = norm_rows(e_hid_f, e_rows[6], e_rows[7]).astype(jnp.bfloat16)
    d_attn, d_vec, d_in, d_out = dec_weights
    d_rows, d_tail = unpack(d_vec, 13, feature)
    branch, d_saved_s = attend(
        dec_in, dec_in, d_attn[:, : 4 * feature], d_rows[0:3], self_mask, True
    )
    d_hid_s = dec_in.astype(jnp.float32) + branch
    d_first = norm_rows(d_hid_s, d_rows[3], d_rows[4]).astype(jnp.bfloat16)
    branch, d_saved_c = attend(
        d_first, encoded, d_attn[:, 4 * feature :], d_rows[5:8], cross_mask, False
    )
    d_hid_c = d_first.astype(jnp.float32) + branch
    d_second = norm_rows(d_hid_c, d_rows[8], d_rows[9]).astype(jnp.bfloat16)
    branch, d_saved_f = feed(d_second, d_in, d_tail, d_out, d_rows[10])
    d_hid_f = d_second.astype(jnp.float32) + branch
    decoded = norm_rows(d_hid_f, d_rows[11], d_rows[12]).astype(jnp.bfloat16)
    gradient, grad_g11, grad_n12 = norm_back(
        d_hid_f, d_rows[11], d_rows[12], dec_cot.astype(jnp.float32)
    )
    grad_rows, grad_d_in, grad_d_tail, grad_d_out, grad_b10 = feed_back(
        gradient, d_second, d_in, d_out, d_saved_f
    )
    gradient, grad_g8, grad_n9 = norm_back(d_hid_c, d_rows[8], d_rows[9], gradient + grad_rows)
    grad_q_in, grad_encoded, grad_cross, cross_bias = attend_back(
        gradient, d_first, encoded, d_attn[:, 4 * feature :], d_saved_c, False
    )
    gradient, grad_g3, grad_n4 = norm_back(d_hid_s, d_rows[3], d_rows[4], gradient + grad_q_in)
    grad_self_in, unused, grad_self, self_bias = attend_back(
        gradient, dec_in, dec_in, d_attn[:, : 4 * feature], d_saved_s, True
    )
    dec_in_grad = gradient + grad_self_in
    dec_stack = jnp.stack(
        [
            self_bias[0],
            self_bias[1],
            self_bias[2],
            grad_g3,
            grad_n4,
            cross_bias[0],
            cross_bias[1],
            cross_bias[2],
            grad_g8,
            grad_n9,
            grad_b10,
            grad_g11,
            grad_n12,
        ]
    )
    dec_vec_full = jnp.concatenate([dec_stack.reshape(-1), grad_d_tail])
    grad_d_attn = jnp.concatenate([grad_self, grad_cross], axis=1)
    if small:
        dec_shards = reduce_pieces(grad_d_attn, dec_vec_full, grad_d_in, grad_d_out, table)
    else:
        dec_shards = reduce_grads(grad_d_attn, dec_vec_full, grad_d_in, grad_d_out)
    gradient, grad_g6, grad_n7 = norm_back(
        e_hid_f, e_rows[6], e_rows[7], enc_cot.astype(jnp.float32) + grad_encoded
    )
    grad_rows, grad_e_in, grad_e_tail, grad_e_out, grad_b5 = feed_back(
        gradient, e_first, e_in, e_out, e_saved_f
    )
    gradient, grad_g3e, grad_n4e = norm_back(e_hid_a, e_rows[3], e_rows[4], gradient + grad_rows)
    grad_self_in, unused, grad_e_attn, enc_bias = attend_back(
        gradient, enc_in, enc_in, e_attn, e_saved_a, True
    )
    enc_in_grad = gradient + grad_self_in
    enc_stack = jnp.stack(
        [enc_bias[0], enc_bias[1], enc_bias[2], grad_g3e, grad_n4e, grad_b5, grad_g6, grad_n7]
    )
    enc_vec_full = jnp.concatenate([enc_stack.reshape(-1), grad_e_tail])
    if small:
        enc_shards = reduce_pieces(grad_e_attn, enc_vec_full, grad_e_in, grad_e_out, table)
    else:
        enc_shards = reduce_grads(grad_e_attn, enc_vec_full, grad_e_in, grad_e_out)
    return (
        encoded,
        decoded,
        enc_in_grad,
        dec_in_grad,
        enc_shards[0],
        enc_shards[1],
        enc_shards[2],
        enc_shards[3],
        dec_shards[0],
        dec_shards[1],
        dec_shards[2],
        dec_shards[3],
    )


def solution(mesh):
    in_specs = (
        P(("rep", "fsdp"), None),
        P(("rep", "fsdp"), None),
        P(("rep", "fsdp")),
        P(("rep", "fsdp"), None),
        P(("rep", "fsdp"), None),
        P("fsdp", None),
        P("fsdp"),
        P("fsdp", None),
        P("fsdp", None),
        P("fsdp", None),
        P("fsdp"),
        P("fsdp", None),
        P("fsdp", None),
        P(("rep", "fsdp"), None),
        P(("rep", "fsdp"), None),
    )
    out_specs = (
        P(("rep", "fsdp"), None),
        P(("rep", "fsdp"), None),
        P(("rep", "fsdp"), None),
        P(("rep", "fsdp"), None),
        P("fsdp", None),
        P("fsdp"),
        P("fsdp", None),
        P("fsdp", None),
        P("fsdp", None),
        P("fsdp"),
        P("fsdp", None),
        P("fsdp", None),
    )
    return jax.shard_map(
        functools.partial(per_device, mesh.shape["fsdp"], mesh.shape["rep"]), mesh=mesh, in_specs=in_specs, out_specs=out_specs, check_vma=False
    )
```

```python
import functools

import jax
import jax.numpy as jnp
from jax import lax
from jax.experimental import pallas as pl
from jax.experimental.pallas import tpu as pltpu
from jax.sharding import PartitionSpec as P

HEAD = 64
PAIR = 2 * HEAD
ROW_TILE = 16
VMEM_BYTES = 56 * 1024 * 1024
ANY = pl.BlockSpec(memory_space=pl.ANY)
SMEM = pl.BlockSpec(memory_space=pltpu.SMEM)
VMEM = pl.BlockSpec(memory_space=pltpu.VMEM)


EPSILON = 1e-05
NEG_FILL = -1e30
SCORE_SCALE = 0.125


def norm_rows(hidden, gain_row, shift_row):
    row_mean = jnp.mean(hidden, axis=-1, keepdims=True)
    centred = hidden - row_mean
    variance = jnp.mean(centred * centred, axis=-1, keepdims=True)
    return centred * lax.rsqrt(variance + EPSILON) * gain_row + shift_row


def norm_back(hidden, gain_row, shift_row, gradient):
    unused, pullback = jax.vjp(norm_rows, hidden, gain_row, shift_row)
    return pullback(gradient)


def gelu_exact(hidden):
    return jax.nn.gelu(hidden, approximate=False)


def dot_plain(first_op, second_op):
    return jnp.dot(first_op, second_op, preferred_element_type=jnp.float32)


def dot_left(first_op, second_op):
    return lax.dot_general(
        first_op, second_op, (((0,), (0,)), ((), ())), preferred_element_type=jnp.float32
    )


def dot_right(first_op, second_op):
    return lax.dot_general(
        first_op, second_op, (((1,), (1,)), ((), ())), preferred_element_type=jnp.float32
    )


def build_masks(one_long, enc_len, dec_len, row_total, seg_count):
    span_rows = jnp.where(one_long == 1, row_total, row_total // seg_count).astype(jnp.int32)
    row_index = jnp.arange(row_total, dtype=jnp.int32)
    group_id = row_index // span_rows
    row_place = row_index - group_id * span_rows
    in_group = group_id[:, None] == jnp.arange(seg_count, dtype=jnp.int32)[None, :]
    enc_live = row_place < jnp.sum(jnp.where(in_group, enc_len[None, :], 0), axis=1)
    dec_live = row_place < jnp.sum(jnp.where(in_group, dec_len[None, :], 0), axis=1)
    same_group = group_id[:, None] == group_id[None, :]
    enc_mask = same_group & enc_live[None, :]
    self_mask = same_group & dec_live[None, :] & (row_index[None, :] <= row_index[:, None])
    return (enc_mask, self_mask, enc_mask)


def unpack(vector, row_count, feature):
    rows_part = vector[: row_count * feature].astype(jnp.float32).reshape(row_count, feature)
    return (rows_part, vector[row_count * feature :].astype(jnp.float32))


def fetch(attn_rows, vec_part, w_in, w_out):
    return (
        lax.all_gather(attn_rows, "fsdp", axis=0, tiled=True),
        lax.all_gather(vec_part, "fsdp", axis=0, tiled=True),
        lax.all_gather(w_in, "fsdp", axis=0, tiled=True),
        lax.all_gather(w_out, "fsdp", axis=0, tiled=True),
    )


def fetch_again(attn_rows, vec_part, w_in, w_out):
    return (
        lax.all_gather(attn_rows, "fsdp", axis=0, tiled=True),
        lax.all_gather(vec_part, "fsdp", axis=0, tiled=True),
        lax.all_gather(w_in, "fsdp", axis=0, tiled=True),
        lax.all_gather(w_out, "fsdp", axis=0, tiled=True),
    )


def reduce_grads(grad_attn, grad_vec, grad_in, grad_out):
    shard = (
        lax.psum_scatter(
            grad_attn.astype(jnp.bfloat16), "fsdp", scatter_dimension=0, tiled=True
        ).astype(jnp.float32),
        lax.psum_scatter(
            grad_vec.astype(jnp.bfloat16), "fsdp", scatter_dimension=0, tiled=True
        ).astype(jnp.float32),
        lax.psum_scatter(
            grad_in.astype(jnp.bfloat16), "fsdp", scatter_dimension=0, tiled=True
        ).astype(jnp.float32),
        lax.psum_scatter(
            grad_out.astype(jnp.bfloat16), "fsdp", scatter_dimension=0, tiled=True
        ).astype(jnp.float32),
    )
    return (
        lax.psum(shard[0].astype(jnp.bfloat16), "rep").astype(jnp.float32),
        lax.psum(shard[1].astype(jnp.bfloat16), "rep").astype(jnp.float32),
        lax.psum(shard[2].astype(jnp.bfloat16), "rep").astype(jnp.float32),
        lax.psum(shard[3].astype(jnp.bfloat16), "rep").astype(jnp.float32),
    )


def attend(q_in, kv_in, weights, biases, key_mask, one_source):
    row_total, feature = q_in.shape
    head_count = feature // HEAD
    if one_source:
        packed = dot_plain(q_in, weights[:, : 3 * feature])
        q_pre = packed[:, :feature]
        k_pre = packed[:, feature : 2 * feature]
        v_pre = packed[:, 2 * feature :]
    else:
        q_pre = dot_plain(q_in, weights[:, :feature])
        packed = dot_plain(kv_in, weights[:, feature : 3 * feature])
        k_pre = packed[:, :feature]
        v_pre = packed[:, feature:]
    queries = (q_pre + biases[0]).astype(jnp.bfloat16).reshape(row_total, head_count, HEAD)
    keys_low = k_pre.astype(jnp.bfloat16).reshape(row_total, head_count, HEAD)
    values = (v_pre + biases[1]).astype(jnp.bfloat16).reshape(row_total, head_count, HEAD)
    raw_score = jnp.einsum("qhd,khd->hqk", queries, keys_low, preferred_element_type=jnp.float32)
    probs = jax.nn.softmax(jnp.where(key_mask[None], raw_score * SCORE_SCALE, NEG_FILL), axis=-1)
    probs_low = probs.astype(jnp.bfloat16)
    mixed = jnp.einsum("hqk,khd->qhd", probs_low, values, preferred_element_type=jnp.float32)
    mixed = mixed.reshape(row_total, feature).astype(jnp.bfloat16)
    branch = dot_plain(mixed, weights[:, 3 * feature :]) + biases[2]
    return (branch, (queries, keys_low, values, probs, probs_low, mixed))


def attend_back(gradient, q_in, kv_in, weights, saved, one_source):
    queries, keys_low, values, probs, probs_low, mixed = saved
    row_total, feature = q_in.shape
    head_count = feature // HEAD
    grad_bias_o = jnp.sum(gradient, axis=0)
    grad_low = gradient.astype(jnp.bfloat16)
    grad_w_o = dot_left(mixed, grad_low)
    grad_mixed = dot_right(grad_low, weights[:, 3 * feature :]).astype(jnp.bfloat16)
    grad_mixed = grad_mixed.reshape(row_total, head_count, HEAD)
    grad_probs = jnp.einsum("qhd,khd->hqk", grad_mixed, values, preferred_element_type=jnp.float32)
    grad_values = jnp.einsum(
        "hqk,qhd->khd", probs_low, grad_mixed, preferred_element_type=jnp.float32
    )
    grad_score = probs * (grad_probs - jnp.sum(grad_probs * probs, axis=-1, keepdims=True))
    grad_raw = (grad_score * SCORE_SCALE).astype(jnp.bfloat16)
    grad_query = jnp.einsum(
        "hqk,khd->qhd", grad_raw, keys_low, preferred_element_type=jnp.float32
    ).reshape(row_total, feature)
    grad_keys = jnp.einsum(
        "hqk,qhd->khd", grad_raw, queries, preferred_element_type=jnp.float32
    ).reshape(row_total, feature)
    grad_values = grad_values.reshape(row_total, feature)
    grad_bias_q = jnp.sum(grad_query, axis=0)
    grad_bias_v = jnp.sum(grad_values, axis=0)
    low_query = grad_query.astype(jnp.bfloat16)
    low_kv = jnp.concatenate(
        [grad_keys.astype(jnp.bfloat16), grad_values.astype(jnp.bfloat16)], axis=1
    )
    if one_source:
        packed = jnp.concatenate([low_query, low_kv], axis=1)
        grad_weights = jnp.concatenate([dot_left(q_in, packed), grad_w_o], axis=1)
        grad_q_in = dot_right(packed, weights[:, : 3 * feature])
        grad_kv_in = grad_q_in
    else:
        grad_weights = jnp.concatenate(
            [dot_left(q_in, low_query), dot_left(kv_in, low_kv), grad_w_o], axis=1
        )
        grad_q_in = dot_right(low_query, weights[:, :feature])
        grad_kv_in = dot_right(low_kv, weights[:, feature : 3 * feature])
    return (grad_q_in, grad_kv_in, grad_weights, (grad_bias_q, grad_bias_v, grad_bias_o))


def feed(rows_in, w_in, b_in, w_out, b_out):
    hidden = dot_plain(rows_in, w_in) + b_in
    active = gelu_exact(hidden).astype(jnp.bfloat16)
    return (dot_plain(active, w_out) + b_out, (hidden, active))


def feed_back(gradient, rows_in, w_in, w_out, saved):
    hidden, active = saved
    grad_b_out = jnp.sum(gradient, axis=0)
    grad_low = gradient.astype(jnp.bfloat16)
    grad_w_out = dot_left(active, grad_low)
    grad_active = dot_right(grad_low, w_out)
    unused, pullback = jax.vjp(gelu_exact, hidden)
    grad_hidden = pullback(grad_active)[0]
    grad_b_in = jnp.sum(grad_hidden, axis=0)
    hidden_low = grad_hidden.astype(jnp.bfloat16)
    grad_w_in = dot_left(rows_in, hidden_low)
    grad_rows = dot_right(hidden_low, w_in)
    return (grad_rows, grad_w_in, grad_b_in, grad_w_out, grad_b_out)


def per_device_any(
    enc_in,
    dec_in,
    bucket,
    enc_lengths,
    dec_lengths,
    enc_attn,
    enc_vec,
    enc_w1,
    enc_w2,
    dec_attn,
    dec_vec,
    dec_w1,
    dec_w2,
    enc_cot,
    dec_cot,
):
    row_total, feature = enc_in.shape
    enc_mask, self_mask, cross_mask = build_masks(
        bucket[0], enc_lengths[0], dec_lengths[0], row_total, enc_lengths.shape[1]
    )
    enc_weights = fetch(enc_attn, enc_vec, enc_w1, enc_w2)
    e_attn, e_vec, e_in, e_out = enc_weights
    e_rows, e_tail = unpack(e_vec, 8, feature)
    branch, e_saved_a = attend(enc_in, enc_in, e_attn, e_rows[0:3], enc_mask, True)
    e_hid_a = enc_in.astype(jnp.float32) + branch
    e_first = norm_rows(e_hid_a, e_rows[3], e_rows[4]).astype(jnp.bfloat16)
    branch, e_saved_f = feed(e_first, e_in, e_tail, e_out, e_rows[5])
    e_hid_f = e_first.astype(jnp.float32) + branch
    encoded = norm_rows(e_hid_f, e_rows[6], e_rows[7]).astype(jnp.bfloat16)
    dec_weights = fetch(dec_attn, dec_vec, dec_w1, dec_w2)
    d_attn, d_vec, d_in, d_out = dec_weights
    d_rows, d_tail = unpack(d_vec, 13, feature)
    branch, d_saved_s = attend(
        dec_in, dec_in, d_attn[:, : 4 * feature], d_rows[0:3], self_mask, True
    )
    d_hid_s = dec_in.astype(jnp.float32) + branch
    d_first = norm_rows(d_hid_s, d_rows[3], d_rows[4]).astype(jnp.bfloat16)
    branch, d_saved_c = attend(
        d_first, encoded, d_attn[:, 4 * feature :], d_rows[5:8], cross_mask, False
    )
    d_hid_c = d_first.astype(jnp.float32) + branch
    d_second = norm_rows(d_hid_c, d_rows[8], d_rows[9]).astype(jnp.bfloat16)
    branch, d_saved_f = feed(d_second, d_in, d_tail, d_out, d_rows[10])
    d_hid_f = d_second.astype(jnp.float32) + branch
    decoded = norm_rows(d_hid_f, d_rows[11], d_rows[12]).astype(jnp.bfloat16)
    dec_weights = fetch_again(dec_attn, dec_vec, dec_w1, dec_w2)
    d_attn, d_vec, d_in, d_out = dec_weights
    d_rows, d_tail = unpack(d_vec, 13, feature)
    gradient, grad_g11, grad_n12 = norm_back(
        d_hid_f, d_rows[11], d_rows[12], dec_cot.astype(jnp.float32)
    )
    grad_rows, grad_d_in, grad_d_tail, grad_d_out, grad_b10 = feed_back(
        gradient, d_second, d_in, d_out, d_saved_f
    )
    gradient, grad_g8, grad_n9 = norm_back(d_hid_c, d_rows[8], d_rows[9], gradient + grad_rows)
    grad_q_in, grad_encoded, grad_cross, cross_bias = attend_back(
        gradient, d_first, encoded, d_attn[:, 4 * feature :], d_saved_c, False
    )
    gradient, grad_g3, grad_n4 = norm_back(d_hid_s, d_rows[3], d_rows[4], gradient + grad_q_in)
    grad_self_in, unused, grad_self, self_bias = attend_back(
        gradient, dec_in, dec_in, d_attn[:, : 4 * feature], d_saved_s, True
    )
    dec_in_grad = gradient + grad_self_in
    dec_stack = jnp.stack(
        [
            self_bias[0],
            self_bias[1],
            self_bias[2],
            grad_g3,
            grad_n4,
            cross_bias[0],
            cross_bias[1],
            cross_bias[2],
            grad_g8,
            grad_n9,
            grad_b10,
            grad_g11,
            grad_n12,
        ]
    )
    dec_vec_full = jnp.concatenate([dec_stack.reshape(-1), grad_d_tail])
    dec_shards = reduce_grads(
        jnp.concatenate([grad_self, grad_cross], axis=1), dec_vec_full, grad_d_in, grad_d_out
    )
    enc_weights = fetch_again(enc_attn, enc_vec, enc_w1, enc_w2)
    e_attn, e_vec, e_in, e_out = enc_weights
    e_rows, e_tail = unpack(e_vec, 8, feature)
    gradient, grad_g6, grad_n7 = norm_back(
        e_hid_f, e_rows[6], e_rows[7], enc_cot.astype(jnp.float32) + grad_encoded
    )
    grad_rows, grad_e_in, grad_e_tail, grad_e_out, grad_b5 = feed_back(
        gradient, e_first, e_in, e_out, e_saved_f
    )
    gradient, grad_g3e, grad_n4e = norm_back(e_hid_a, e_rows[3], e_rows[4], gradient + grad_rows)
    grad_self_in, unused, grad_e_attn, enc_bias = attend_back(
        gradient, enc_in, enc_in, e_attn, e_saved_a, True
    )
    enc_in_grad = gradient + grad_self_in
    enc_stack = jnp.stack(
        [enc_bias[0], enc_bias[1], enc_bias[2], grad_g3e, grad_n4e, grad_b5, grad_g6, grad_n7]
    )
    enc_vec_full = jnp.concatenate([enc_stack.reshape(-1), grad_e_tail])
    enc_shards = reduce_grads(grad_e_attn, enc_vec_full, grad_e_in, grad_e_out)
    return (
        encoded,
        decoded,
        enc_in_grad,
        dec_in_grad,
        enc_shards[0],
        enc_shards[1],
        enc_shards[2],
        enc_shards[3],
        dec_shards[0],
        dec_shards[1],
        dec_shards[2],
        dec_shards[3],
    )


def swap(value, bit):
    return lax.ppermute(value, "fsdp", [(i, i ^ bit) for i in range(8)])


def add_low(*terms):
    total = terms[0].astype(jnp.float32)
    for term in terms[1:]:
        total = total + term.astype(jnp.float32)
    return total.astype(jnp.bfloat16)


def tile_up(rows):
    return -(-rows // ROW_TILE) * ROW_TILE


def pack_units(shards, feature):
    unit_rows = feature // 8
    parts = []
    for shard in shards:
        rows, columns = shard.shape
        if rows == unit_rows:
            for block in range(columns // feature):
                parts.append(shard[:, block * feature : (block + 1) * feature])
        else:
            parts.append(shard)
    return jnp.concatenate(parts, axis=0)


def vec_rows(vec_part, feature):
    rows = tile_up(-(-vec_part.shape[0] // feature))
    padded = jnp.pad(vec_part, (0, rows * feature - vec_part.shape[0]))
    return padded.reshape(rows, feature)


def gather_piece(packed, cut):
    from_x = swap(packed, 2)
    from_y = swap(packed, 4)
    corner_top = swap(from_x[:cut], 4)
    corner_low = swap(from_y[cut:], 2)
    mine = [packed, from_x, from_y, corner_top, corner_low]
    return mine + [swap(value, 1) for value in mine]


def gathered_vec(buffers, cut, offset, table, length, feature):
    rows = tile_up(-(-length // feature))
    parts = []
    for chip in range(4):
        for core in range(2):
            group = buffers[5 * core : 5 * core + 5]
            source = group[chip] if chip < 3 else group[4]
            first = offset if chip < 3 else offset - cut
            parts.append(source[first : first + rows].reshape(1, rows * feature)[:, :length])
    stacked = jnp.concatenate(parts, axis=0)
    chosen = (table[:, None] == jnp.arange(8, dtype=jnp.int32)[None, :]).astype(jnp.bfloat16)
    return dot_left(chosen, stacked).reshape(-1)


class Loader:
    def __init__(self, buffers, table, cut, sems):
        self.buffers = buffers
        self.table = table
        self.cut = cut
        self.sems = sems
        self.used = 0

    def unit(self, number, target, stride, first):
        rows = target.shape[1] // 8
        copies = []
        for chip in range(4):
            for core in range(2):
                group = self.buffers[5 * core : 5 * core + 5]
                offset = number * rows
                if chip < 3:
                    source = group[chip]
                elif offset < self.cut:
                    source = group[3]
                else:
                    source = group[4]
                    offset -= self.cut
                place = pl.multiple_of(self.table[2 * chip + core] * stride + first, ROW_TILE)
                copy = pltpu.make_async_copy(
                    source.at[pl.ds(offset, rows), :],
                    target.at[pl.ds(place, rows), :],
                    self.sems.at[self.used],
                )
                copy.start()
                self.used += 1
                copies.append(copy)
        return copies

    def wide(self, number, target):
        return self.unit(number, target, target.shape[1] // 8, 0)

    def tall(self, number, target):
        rows = target.shape[1] // 8
        copies = []
        for block in range(4):
            copies += self.unit(number + block, target, 4 * rows, block * rows)
        return copies


def wait_all(copies):
    for copy in copies:
        copy.wait()


class Storer:
    def __init__(self, keep, send, table, sems):
        self.keep = keep
        self.send = send
        self.table = table
        self.sems = sems
        self.copies = []

    def rows(self, source, stride, count, offset, chips_of=None):
        for core, out in ((1, self.send), (0, self.keep)):
            for chip in range(4):
                place = pl.multiple_of(self.table[2 * chip + core] * stride, ROW_TILE)
                copy = pltpu.make_async_copy(
                    source.at[pl.ds(place, count), :],
                    out.at[chip, pl.ds(offset, count), :],
                    self.sems.at[len(self.copies)],
                )
                copy.start()
                self.copies.append(copy)

    def finish(self):
        wait_all(self.copies)


def low(value):
    return value.astype(jnp.bfloat16)


def layer_norm(hidden, gain, shift):
    mean = jnp.mean(hidden, axis=-1, keepdims=True)
    centred = hidden - mean
    variance = jnp.mean(centred * centred, axis=-1, keepdims=True)
    return centred * lax.rsqrt(variance + EPSILON) * gain + shift


def layer_norm_back(hidden, gain, gradient):
    mean = jnp.mean(hidden, axis=-1, keepdims=True)
    centred = hidden - mean
    variance = jnp.mean(centred * centred, axis=-1, keepdims=True)
    scale = lax.rsqrt(variance + EPSILON)
    unit = centred * scale
    grad_gain = jnp.sum(gradient * unit, axis=0, keepdims=True)
    grad_shift = jnp.sum(gradient, axis=0, keepdims=True)
    inner = gradient * gain
    mean_inner = jnp.mean(inner, axis=-1, keepdims=True)
    mean_unit = jnp.mean(inner * unit, axis=-1, keepdims=True)
    return (scale * (inner - mean_inner - unit * mean_unit), grad_gain, grad_shift)


def key_mask(bucket, lengths, rows, segs, causal):
    span = rows // segs
    one_long = bucket[0] == 1
    query = lax.broadcasted_iota(jnp.int32, (rows, rows), 0)
    key = lax.broadcasted_iota(jnp.int32, (rows, rows), 1)
    key_row = lax.broadcasted_iota(jnp.int32, (1, rows), 1)
    limit = jnp.zeros((1, rows), jnp.int32)
    start = jnp.zeros((1, rows), jnp.int32)
    first = jnp.zeros((rows, 1), jnp.int32)
    query_col = lax.broadcasted_iota(jnp.int32, (rows, 1), 0)
    for seg in range(segs):
        inside = (key_row >= seg * span) & (key_row < (seg + 1) * span)
        limit = jnp.where(inside, seg * span + lengths[0, seg], limit)
        start = jnp.where(inside, seg * span, start)
        first = jnp.where((query_col >= seg * span) & (query_col < (seg + 1) * span), seg * span, first)
    limit = jnp.where(one_long, lengths[0, 0], limit)
    start = jnp.where(one_long, 0, start)
    first = jnp.where(one_long, 0, first)
    mask = (first == start) & (key < limit)
    if causal:
        mask = mask & (key <= query)
    return mask


def head_lanes(rows):
    return lax.broadcasted_iota(jnp.int32, (rows, PAIR), 1) < HEAD


def attn_body(
    cross, causal, first_unit, cut, segs, table, bucket, lengths, *refs
):
    refs = list(refs)
    q_in = refs.pop(0)
    kv_in = refs.pop(0) if cross else q_in
    vec = refs.pop(0)
    buffers = [refs.pop(0) for _ in range(10)]
    hidden_out, norm_out, q_out, k_out, v_out, o_out, p_out = refs[:7]
    w_q, w_k, w_v, w_o, sems = refs[7:]
    rows, feature = q_in.shape
    load = Loader(buffers, table, cut, sems)
    waits = [load.wide(first_unit + i, w) for i, w in enumerate((w_q, w_k, w_v, w_o))]
    mask = key_mask(bucket, lengths, rows, segs, causal)
    lanes = head_lanes(rows)
    wait_all(waits[0])
    q_out[...] = low(dot_plain(q_in[...], w_q[...]) + vec[0:1, :])
    wait_all(waits[1])
    k_out[...] = low(dot_plain(kv_in[...], w_k[...]))
    wait_all(waits[2])
    v_out[...] = low(dot_plain(kv_in[...], w_v[...]) + vec[1:2, :])
    for pair in range(feature // PAIR):
        columns = slice(pair * PAIR, (pair + 1) * PAIR)
        q_pair, k_pair, v_pair = q_out[:, columns], k_out[:, columns], v_out[:, columns]
        mixed = []
        for half in range(2):
            mine = lanes if half == 0 else ~lanes
            score = dot_right(jnp.where(mine, q_pair, jnp.zeros_like(q_pair)), k_pair)
            score = jnp.where(mask, score * SCORE_SCALE, NEG_FILL)
            power = jnp.exp(score - jnp.max(score, axis=-1, keepdims=True))
            probs = low(power / jnp.sum(power, axis=-1, keepdims=True))
            p_out[2 * pair + half] = probs
            mixed.append(dot_plain(probs, v_pair))
        o_out[:, columns] = low(jnp.where(lanes, mixed[0], mixed[1]))
    wait_all(waits[3])
    hidden = q_in[...].astype(jnp.float32) + (dot_plain(o_out[...], w_o[...]) + vec[2:3, :])
    hidden_out[...] = hidden
    norm_out[...] = low(layer_norm(hidden, vec[3:4, :], vec[4:5, :]))


def params(flops, moved):
    return dict(
        compiler_params=pltpu.CompilerParams(vmem_limit_bytes=VMEM_BYTES),
        cost_estimate=pl.CostEstimate(flops=flops, bytes_accessed=moved, transcendentals=0),
    )


def attn_forward(q_in, kv_in, vec, buffers, ids, lengths, first_unit, cut, causal, name):
    table, bucket = ids
    rows, feature = q_in.shape
    heads = feature // HEAD
    cross = kv_in is not None
    wide = jax.ShapeDtypeStruct((rows, feature), jnp.bfloat16)
    sources = [q_in] + ([kv_in] if cross else []) + [vec]
    square = pltpu.VMEM((feature, feature), jnp.bfloat16)
    return pl.pallas_call(
        functools.partial(attn_body, cross, causal, first_unit, cut, lengths.shape[1]),
        out_shape=[
            jax.ShapeDtypeStruct((rows, feature), jnp.float32),
            wide,
            wide,
            wide,
            wide,
            wide,
            jax.ShapeDtypeStruct((heads, rows, rows), jnp.bfloat16),
        ],
        in_specs=[SMEM] * 3 + [VMEM] * len(sources) + [ANY] * 10,
        out_specs=[VMEM] * 7,
        scratch_shapes=[square] * 4 + [pltpu.SemaphoreType.DMA((32,))],
        name=name,
        **params(8 * rows * feature * feature, 10 * feature * feature),
    )(table, bucket, lengths, *sources, *buffers)


def gelu_parts(hidden):
    phi = 0.5 * (1.0 + lax.erf(hidden * 0.7071067811865476))
    slope = phi + hidden * (0.3989422804014327 * jnp.exp(-0.5 * hidden * hidden))
    return (hidden * phi, slope)


def feed_body(cut, table, rows_in, vec, b_in, *refs):
    buffers = refs[:10]
    hidden_out, norm_out, r_out, slope_out, w_in, w_out, sems = refs[10:]
    feature = rows_in.shape[1]
    load = Loader(buffers, table, cut, sems)
    waits = [load.wide(j, w_in.at[j]) for j in range(4)]
    tail = load.tall(4, w_out)
    total = None
    for j in range(4):
        columns = slice(j * feature, (j + 1) * feature)
        wait_all(waits[j])
        hidden = dot_plain(rows_in[...], w_in[j]) + b_in[:, columns]
        active, slope = gelu_parts(hidden)
        r_out[:, columns] = low(active)
        slope_out[:, columns] = low(slope)
    wait_all(tail)
    total = dot_plain(r_out[...], w_out[...]) + vec[0:1, :]
    hidden = rows_in[...].astype(jnp.float32) + total
    hidden_out[...] = hidden
    norm_out[...] = low(layer_norm(hidden, vec[1:2, :], vec[2:3, :]))


def feed_forward(rows_in, vec, b_in, buffers, table, cut, name):
    rows, feature = rows_in.shape
    width = b_in.shape[1]
    return pl.pallas_call(
        functools.partial(feed_body, cut),
        out_shape=[
            jax.ShapeDtypeStruct((rows, feature), jnp.float32),
            jax.ShapeDtypeStruct((rows, feature), jnp.bfloat16),
            jax.ShapeDtypeStruct((rows, width), jnp.bfloat16),
            jax.ShapeDtypeStruct((rows, width), jnp.bfloat16),
        ],
        in_specs=[SMEM] + [VMEM] * 3 + [ANY] * 10,
        out_specs=[VMEM] * 4,
        scratch_shapes=[
            pltpu.VMEM((4, feature, feature), jnp.bfloat16),
            pltpu.VMEM((width, feature), jnp.bfloat16),
            pltpu.SemaphoreType.DMA((64,)),
        ],
        name=name,
        **params(4 * rows * feature * width, 8 * feature * width),
    )(table, rows_in, vec, b_in, *buffers)


def feed_back_out_body(cut, extra, table, *refs):
    refs = list(refs)
    gradient = refs.pop(0)[...].astype(jnp.float32)
    if extra:
        gradient = gradient + refs.pop(0)[...].astype(jnp.float32)
    hidden, gain, active, slope = refs[:4]
    buffers = refs[4:14]
    g_out, gu_out, sums, bias_in, keep, send, w_out, stage, sems, out_sems = refs[14:]
    feature = hidden.shape[1]
    load = Loader(buffers, table, cut, sems)
    tail = load.tall(4, w_out)
    store = Storer(keep, send, table, out_sems)
    gradient, grad_gain, grad_shift = layer_norm_back(hidden[...], gain[...], gradient)
    sums[0:1, :] = jnp.sum(gradient, axis=0, keepdims=True)
    sums[1:2, :] = grad_gain
    sums[2:3, :] = grad_shift
    g_out[...] = gradient
    grad_low = low(gradient)
    for j in range(4):
        columns = slice(j * feature, (j + 1) * feature)
        stage[columns, :] = low(dot_left(active[:, columns], grad_low))
    store.rows(stage, feature // 2, feature // 2, 0)
    wait_all(tail)
    for j in range(4):
        columns = slice(j * feature, (j + 1) * feature)
        grad_hidden = dot_right(grad_low, w_out[columns, :]) * slope[:, columns].astype(jnp.float32)
        bias_in[0:1, columns] = jnp.sum(grad_hidden, axis=0, keepdims=True)
        gu_out[:, columns] = low(grad_hidden)
    store.finish()


def feed_back_out(gradients, hidden, gain, active, slope, buffers, table, cut, name):
    rows, feature = hidden.shape
    width = active.shape[1]
    block = jax.ShapeDtypeStruct((4, feature // 2, feature), jnp.bfloat16)
    return pl.pallas_call(
        functools.partial(feed_back_out_body, cut, len(gradients) == 2),
        out_shape=[
            jax.ShapeDtypeStruct((rows, feature), jnp.float32),
            jax.ShapeDtypeStruct((rows, width), jnp.bfloat16),
            jax.ShapeDtypeStruct((3, feature), jnp.float32),
            jax.ShapeDtypeStruct((1, width), jnp.float32),
            block,
            block,
        ],
        in_specs=[SMEM] + [VMEM] * (len(gradients) + 4) + [ANY] * 10,
        out_specs=[VMEM] * 4 + [ANY] * 2,
        scratch_shapes=[
            pltpu.VMEM((width, feature), jnp.bfloat16),
            pltpu.VMEM((width, feature), jnp.bfloat16),
            pltpu.SemaphoreType.DMA((32,)),
            pltpu.SemaphoreType.DMA((8,)),
        ],
        name=name,
        **params(4 * rows * feature * width, 6 * feature * width),
    )(table, *gradients, hidden, gain, active, slope, *buffers)


def feed_back_in_body(cut, table, gradient, grad_hidden, rows_in, *refs):
    buffers = refs[:10]
    total_out, keep, send, w_in, stage, sems, out_sems = refs[10:]
    feature = rows_in.shape[1]
    load = Loader(buffers, table, cut, sems)
    waits = [load.wide(j, w_in.at[j]) for j in range(4)]
    store = Storer(keep, send, table, out_sems)
    total = gradient[...]
    for j in range(4):
        columns = slice(j * feature, (j + 1) * feature)
        stage[j] = low(dot_left(rows_in[...], grad_hidden[:, columns]))
        store.rows(stage.at[j], feature // 8, feature // 8, j * (feature // 8))
    for j in range(4):
        columns = slice(j * feature, (j + 1) * feature)
        wait_all(waits[j])
        total = total + dot_right(grad_hidden[:, columns], w_in[j])
    total_out[...] = total
    store.finish()


def feed_back_in(gradient, grad_hidden, rows_in, buffers, table, cut, name):
    rows, feature = rows_in.shape
    width = grad_hidden.shape[1]
    block = jax.ShapeDtypeStruct((4, feature // 2, feature), jnp.bfloat16)
    return pl.pallas_call(
        functools.partial(feed_back_in_body, cut),
        out_shape=[jax.ShapeDtypeStruct((rows, feature), jnp.float32), block, block],
        in_specs=[SMEM] + [VMEM] * 3 + [ANY] * 10,
        out_specs=[VMEM] + [ANY] * 2,
        scratch_shapes=[
            pltpu.VMEM((4, feature, feature), jnp.bfloat16),
            pltpu.VMEM((4, feature, feature), jnp.bfloat16),
            pltpu.SemaphoreType.DMA((32,)),
            pltpu.SemaphoreType.DMA((32,)),
        ],
        name=name,
        **params(4 * rows * feature * width, 6 * feature * width),
    )(table, gradient, grad_hidden, rows_in, *buffers)


def attn_back_body(cross, first_unit, cut, table, gradient, *refs):
    refs = list(refs)
    hidden, gain, q_in = refs[:3]
    refs = refs[3:]
    kv_in = refs.pop(0) if cross else q_in
    queries, keys, values, mixed, probs_in = refs[:5]
    buffers = refs[5:15]
    refs = refs[15:]
    q_grad_out = refs.pop(0)
    kv_grad_out = refs.pop(0) if cross else None
    sums, keep, send, w_q, w_k, w_v, w_o, stage, go, gq, gk, gv, sems, out_sems = refs
    rows, feature = hidden.shape
    unit = feature // 8
    load = Loader(buffers, table, cut, sems)
    wait_o = load.wide(first_unit + 3, w_o)
    waits = [load.wide(first_unit + i, w) for i, w in enumerate((w_q, w_k, w_v))]
    store = Storer(keep, send, table, out_sems)
    lanes = head_lanes(rows)
    total, grad_gain, grad_shift = layer_norm_back(hidden[...], gain[...], gradient[...])
    sums[2:3, :] = jnp.sum(total, axis=0, keepdims=True)
    sums[3:4, :] = grad_gain
    sums[4:5, :] = grad_shift
    grad_low = low(total)
    stage[3] = low(dot_left(mixed[...], grad_low))
    store.rows(stage.at[3], unit, unit, 3 * unit)
    wait_all(wait_o)
    go[...] = low(dot_right(grad_low, w_o[...]))
    for pair in range(feature // PAIR):
        columns = slice(pair * PAIR, (pair + 1) * PAIR)
        q_pair, k_pair, v_pair = queries[:, columns], keys[:, columns], values[:, columns]
        go_pair = go[:, columns]
        parts = []
        for half in range(2):
            mine = lanes if half == 0 else ~lanes
            probs_low = probs_in[2 * pair + half]
            probs = probs_low.astype(jnp.float32)
            grad_probs = dot_right(jnp.where(mine, go_pair, jnp.zeros_like(go_pair)), v_pair)
            weighted = grad_probs * probs
            row_sum = jnp.sum(weighted, axis=-1, keepdims=True)
            grad_raw = low((weighted - probs * row_sum) * SCORE_SCALE)
            parts.append(
                (
                    dot_plain(grad_raw, k_pair),
                    dot_left(grad_raw, q_pair),
                    dot_left(probs_low, go_pair),
                )
            )
        grad_q, grad_k, grad_v = (jnp.where(lanes, a, b) for a, b in zip(*parts))
        sums[0:1, columns] = jnp.sum(grad_q, axis=0, keepdims=True)
        sums[1:2, columns] = jnp.sum(grad_v, axis=0, keepdims=True)
        gq[:, columns] = low(grad_q)
        gk[:, columns] = low(grad_k)
        gv[:, columns] = low(grad_v)
    for index, (source, grad) in enumerate(((q_in, gq), (kv_in, gk), (kv_in, gv))):
        stage[index] = low(dot_left(source[...], grad[...]))
        store.rows(stage.at[index], unit, unit, index * unit)
    for copies in waits:
        wait_all(copies)
    total = total + dot_right(gq[...], w_q[...])
    kv_total = dot_right(gk[...], w_k[...]) + dot_right(gv[...], w_v[...])
    if cross:
        q_grad_out[...] = total
        kv_grad_out[...] = kv_total
    else:
        q_grad_out[...] = total + kv_total
    store.finish()


def attn_back(gradient, hidden, gain, q_in, kv_in, saved, buffers, table, first_unit, cut, name):
    rows, feature = hidden.shape
    cross = kv_in is not None
    wide = jax.ShapeDtypeStruct((rows, feature), jnp.float32)
    block = jax.ShapeDtypeStruct((4, feature // 2, feature), jnp.bfloat16)
    sources = [gradient, hidden, gain, q_in] + ([kv_in] if cross else []) + list(saved)
    square = pltpu.VMEM((feature, feature), jnp.bfloat16)
    low_rows = pltpu.VMEM((rows, feature), jnp.bfloat16)
    return pl.pallas_call(
        functools.partial(attn_back_body, cross, first_unit, cut),
        out_shape=[wide] * (1 + cross)
        + [jax.ShapeDtypeStruct((5, feature), jnp.float32), block, block],
        in_specs=[SMEM] + [VMEM] * len(sources) + [ANY] * 10,
        out_specs=[VMEM] * (2 + cross) + [ANY] * 2,
        scratch_shapes=[square] * 4
        + [pltpu.VMEM((4, feature, feature), jnp.bfloat16)]
        + [low_rows] * 4
        + [pltpu.SemaphoreType.DMA((32,)), pltpu.SemaphoreType.DMA((32,))],
        name=name,
        **params(16 * rows * feature * feature, 20 * feature * feature),
    )(table, *sources, *buffers)


def line_sum(value):
    place = lax.axis_index("rep")
    inner = (place == 1) | (place == 2)
    half = add_low(value, lax.ppermute(value, "rep", [(0, 1), (3, 2)]))
    total = add_low(half, lax.ppermute(half, "rep", [(1, 2), (2, 1)]))
    return jnp.where(inner, total, lax.ppermute(total, "rep", [(1, 0), (2, 3)]))


def reduce_blocks(keep, send, vec_blocks=None):
    full = add_low(keep, swap(send, 1))
    if vec_blocks is not None:
        full = jnp.concatenate([full, add_low(vec_blocks[0], swap(vec_blocks[1], 1))], axis=1)
    cut = tile_up(full.shape[1] // 2)
    low_x = swap(full[3, :cut], 2)
    low_y = swap(full[3, cut:], 4)
    to_x = jnp.concatenate([full[1, :cut], add_low(full[1, cut:], low_y)], axis=0)
    to_y = jnp.concatenate([add_low(full[2, :cut], low_x), full[2, cut:]], axis=0)
    return line_sum(add_low(full[0], swap(to_x, 2), swap(to_y, 4)))


def vec_blocks(rows_list, tail, table, feature):
    flat = jnp.concatenate([rows.reshape(-1) for rows in rows_list] + [tail.reshape(-1)])
    parts = flat.astype(jnp.bfloat16).reshape(8, -1)
    chosen = (table[:, None] == jnp.arange(8, dtype=jnp.int32)[None, :]).astype(jnp.bfloat16)
    placed = dot_plain(chosen, parts).astype(jnp.bfloat16)
    count = tile_up(-(-parts.shape[1] // feature))
    placed = jnp.pad(placed, ((0, 0), (0, count * feature - parts.shape[1])))
    placed = placed.reshape(4, 2, count, feature)
    return (placed[:, 0], placed[:, 1])


def wide_out(block, feature):
    unit = feature // 8
    parts = [block[j * unit : (j + 1) * unit] for j in range(4)]
    return jnp.concatenate(parts, axis=1).astype(jnp.float32)


def per_device(
    enc_in,
    dec_in,
    bucket,
    enc_lengths,
    dec_lengths,
    enc_attn,
    enc_vec,
    enc_w1,
    enc_w2,
    dec_attn,
    dec_vec,
    dec_w1,
    dec_w2,
    enc_cot,
    dec_cot,
):
    feature = enc_in.shape[1]
    unit = feature // 8
    table = lax.axis_index("fsdp").astype(jnp.int32) ^ jnp.arange(8, dtype=jnp.int32)
    ids = (table, bucket)
    e_attn = gather_piece(pack_units([enc_attn, vec_rows(enc_vec, feature)], feature), 2 * unit)
    e_feed = gather_piece(pack_units([enc_w1, enc_w2], feature), 4 * unit)
    d_attn = gather_piece(pack_units([dec_attn, vec_rows(dec_vec, feature)], feature), 4 * unit)
    d_feed = gather_piece(pack_units([dec_w1, dec_w2], feature), 4 * unit)
    e_vec = gathered_vec(e_attn, 2 * unit, 4 * unit, table, enc_vec.shape[0], feature)
    e_rows, e_tail = unpack(e_vec, 8, feature)
    e_tail = e_tail.reshape(1, -1)
    e_hid_a, e_first, *e_saved = attn_forward(
        enc_in, None, e_rows[0:5], e_attn, ids, enc_lengths, 0, 2 * unit, False, "enc_attn"
    )
    e_hid_f, encoded, e_act, e_slope = feed_forward(
        e_first, e_rows[5:8], e_tail, e_feed, table, 4 * unit, "enc_feed"
    )
    d_vec = gathered_vec(d_attn, 4 * unit, 8 * unit, table, dec_vec.shape[0], feature)
    d_rows, d_tail = unpack(d_vec, 13, feature)
    d_tail = d_tail.reshape(1, -1)
    d_hid_s, d_first, *s_saved = attn_forward(
        dec_in, None, d_rows[0:5], d_attn, ids, dec_lengths, 0, 4 * unit, True, "dec_self"
    )
    d_hid_c, d_second, *c_saved = attn_forward(
        d_first, encoded, d_rows[5:10], d_attn, ids, enc_lengths, 4, 4 * unit, False, "dec_cross"
    )
    d_hid_f, decoded, d_act, d_slope = feed_forward(
        d_second, d_rows[10:13], d_tail, d_feed, table, 4 * unit, "dec_feed"
    )
    gradient, d_gu, d_sums_f, d_bias, keep, send = feed_back_out(
        [dec_cot], d_hid_f, d_rows[11:12], d_act, d_slope, d_feed, table, 4 * unit, "dec_feed_back_out"
    )
    grad_d_w2 = reduce_blocks(keep, send)
    gradient, keep, send = feed_back_in(
        gradient, d_gu, d_second, d_feed, table, 4 * unit, "dec_feed_back_in"
    )
    grad_d_w1 = reduce_blocks(keep, send)
    gradient, grad_encoded, d_sums_c, keep, send = attn_back(
        gradient, d_hid_c, d_rows[8:9], d_first, encoded, c_saved, d_attn, table, 4, 4 * unit, "cross_back"
    )
    grad_d_cross = reduce_blocks(keep, send)
    e_gradient, e_gu, e_sums_f, e_bias, keep, send = feed_back_out(
        [enc_cot, grad_encoded], e_hid_f, e_rows[6:7], e_act, e_slope, e_feed, table, 4 * unit, "enc_feed_back_out"
    )
    grad_e_w2 = reduce_blocks(keep, send)
    e_gradient, keep, send = feed_back_in(
        e_gradient, e_gu, e_first, e_feed, table, 4 * unit, "enc_feed_back_in"
    )
    grad_e_w1 = reduce_blocks(keep, send)
    dec_in_grad, d_sums_s, keep, send = attn_back(
        gradient, d_hid_s, d_rows[3:4], dec_in, None, s_saved, d_attn, table, 0, 4 * unit, "self_back"
    )
    grad_d_self = reduce_blocks(
        keep, send, vec_blocks([d_sums_s, d_sums_c, d_sums_f], d_bias, table, feature)
    )
    enc_in_grad, e_sums_a, keep, send = attn_back(
        e_gradient, e_hid_a, e_rows[3:4], enc_in, None, e_saved, e_attn, table, 0, 2 * unit, "enc_attn_back"
    )
    grad_e_attn = reduce_blocks(
        keep, send, vec_blocks([e_sums_a, e_sums_f], e_bias, table, feature)
    )
    d_wide = jnp.concatenate([wide_out(grad_d_self, feature), wide_out(grad_d_cross, feature)], axis=1)
    return (
        encoded,
        decoded,
        enc_in_grad,
        dec_in_grad,
        wide_out(grad_e_attn, feature),
        grad_e_attn[4 * unit :].reshape(-1)[: enc_vec.shape[0]].astype(jnp.float32),
        wide_out(grad_e_w1, feature),
        grad_e_w2.astype(jnp.float32),
        d_wide,
        grad_d_self[4 * unit :].reshape(-1)[: dec_vec.shape[0]].astype(jnp.float32),
        wide_out(grad_d_w1, feature),
        grad_d_w2.astype(jnp.float32),
    )


def solution(mesh):
    in_specs = (
        P(("rep", "fsdp"), None),
        P(("rep", "fsdp"), None),
        P(("rep", "fsdp")),
        P(("rep", "fsdp"), None),
        P(("rep", "fsdp"), None),
        P("fsdp", None),
        P("fsdp"),
        P("fsdp", None),
        P("fsdp", None),
        P("fsdp", None),
        P("fsdp"),
        P("fsdp", None),
        P("fsdp", None),
        P(("rep", "fsdp"), None),
        P(("rep", "fsdp"), None),
    )
    out_specs = (
        P(("rep", "fsdp"), None),
        P(("rep", "fsdp"), None),
        P(("rep", "fsdp"), None),
        P(("rep", "fsdp"), None),
        P("fsdp", None),
        P("fsdp"),
        P("fsdp", None),
        P("fsdp", None),
        P("fsdp", None),
        P("fsdp"),
        P("fsdp", None),
        P("fsdp", None),
    )
    small = mesh.shape["fsdp"] == 8 and mesh.shape["rep"] == 4
    return jax.shard_map(
        per_device if small else per_device_any, mesh=mesh, in_specs=in_specs, out_specs=out_specs, check_vma=False
    )
```

```python
import functools

import jax
import jax.numpy as jnp
from jax import lax
from jax.experimental import pallas as pl
from jax.experimental.pallas import tpu as pltpu
from jax.sharding import PartitionSpec as P

HEAD = 64
PAIR = 2 * HEAD
ROW_TILE = 16
VMEM_BYTES = 56 * 1024 * 1024
ANY = pl.BlockSpec(memory_space=pl.ANY)
SMEM = pl.BlockSpec(memory_space=pltpu.SMEM)
VMEM = pl.BlockSpec(memory_space=pltpu.VMEM)


EPSILON = 1e-05
NEG_FILL = -1e30
SCORE_SCALE = 0.125


def norm_rows(hidden, gain_row, shift_row):
    row_mean = jnp.mean(hidden, axis=-1, keepdims=True)
    centred = hidden - row_mean
    variance = jnp.mean(centred * centred, axis=-1, keepdims=True)
    return centred * lax.rsqrt(variance + EPSILON) * gain_row + shift_row


def norm_back(hidden, gain_row, shift_row, gradient):
    unused, pullback = jax.vjp(norm_rows, hidden, gain_row, shift_row)
    return pullback(gradient)


def gelu_exact(hidden):
    return jax.nn.gelu(hidden, approximate=False)


def dot_plain(first_op, second_op):
    return jnp.dot(first_op, second_op, preferred_element_type=jnp.float32)


def dot_left(first_op, second_op):
    return lax.dot_general(
        first_op, second_op, (((0,), (0,)), ((), ())), preferred_element_type=jnp.float32
    )


def dot_right(first_op, second_op):
    return lax.dot_general(
        first_op, second_op, (((1,), (1,)), ((), ())), preferred_element_type=jnp.float32
    )


def build_masks(one_long, enc_len, dec_len, row_total, seg_count):
    span_rows = jnp.where(one_long == 1, row_total, row_total // seg_count).astype(jnp.int32)
    row_index = jnp.arange(row_total, dtype=jnp.int32)
    group_id = row_index // span_rows
    row_place = row_index - group_id * span_rows
    in_group = group_id[:, None] == jnp.arange(seg_count, dtype=jnp.int32)[None, :]
    enc_live = row_place < jnp.sum(jnp.where(in_group, enc_len[None, :], 0), axis=1)
    dec_live = row_place < jnp.sum(jnp.where(in_group, dec_len[None, :], 0), axis=1)
    same_group = group_id[:, None] == group_id[None, :]
    enc_mask = same_group & enc_live[None, :]
    self_mask = same_group & dec_live[None, :] & (row_index[None, :] <= row_index[:, None])
    return (enc_mask, self_mask, enc_mask)


def unpack(vector, row_count, feature):
    rows_part = vector[: row_count * feature].astype(jnp.float32).reshape(row_count, feature)
    return (rows_part, vector[row_count * feature :].astype(jnp.float32))


def fetch(attn_rows, vec_part, w_in, w_out):
    return (
        lax.all_gather(attn_rows, "fsdp", axis=0, tiled=True),
        lax.all_gather(vec_part, "fsdp", axis=0, tiled=True),
        lax.all_gather(w_in, "fsdp", axis=0, tiled=True),
        lax.all_gather(w_out, "fsdp", axis=0, tiled=True),
    )


def fetch_again(attn_rows, vec_part, w_in, w_out):
    return (
        lax.all_gather(attn_rows, "fsdp", axis=0, tiled=True),
        lax.all_gather(vec_part, "fsdp", axis=0, tiled=True),
        lax.all_gather(w_in, "fsdp", axis=0, tiled=True),
        lax.all_gather(w_out, "fsdp", axis=0, tiled=True),
    )


def reduce_grads(grad_attn, grad_vec, grad_in, grad_out):
    shard = (
        lax.psum_scatter(
            grad_attn.astype(jnp.bfloat16), "fsdp", scatter_dimension=0, tiled=True
        ).astype(jnp.float32),
        lax.psum_scatter(
            grad_vec.astype(jnp.bfloat16), "fsdp", scatter_dimension=0, tiled=True
        ).astype(jnp.float32),
        lax.psum_scatter(
            grad_in.astype(jnp.bfloat16), "fsdp", scatter_dimension=0, tiled=True
        ).astype(jnp.float32),
        lax.psum_scatter(
            grad_out.astype(jnp.bfloat16), "fsdp", scatter_dimension=0, tiled=True
        ).astype(jnp.float32),
    )
    return (
        lax.psum(shard[0].astype(jnp.bfloat16), "rep").astype(jnp.float32),
        lax.psum(shard[1].astype(jnp.bfloat16), "rep").astype(jnp.float32),
        lax.psum(shard[2].astype(jnp.bfloat16), "rep").astype(jnp.float32),
        lax.psum(shard[3].astype(jnp.bfloat16), "rep").astype(jnp.float32),
    )


def attend(q_in, kv_in, weights, biases, key_mask, one_source):
    row_total, feature = q_in.shape
    head_count = feature // HEAD
    if one_source:
        packed = dot_plain(q_in, weights[:, : 3 * feature])
        q_pre = packed[:, :feature]
        k_pre = packed[:, feature : 2 * feature]
        v_pre = packed[:, 2 * feature :]
    else:
        q_pre = dot_plain(q_in, weights[:, :feature])
        packed = dot_plain(kv_in, weights[:, feature : 3 * feature])
        k_pre = packed[:, :feature]
        v_pre = packed[:, feature:]
    queries = (q_pre + biases[0]).astype(jnp.bfloat16).reshape(row_total, head_count, HEAD)
    keys_low = k_pre.astype(jnp.bfloat16).reshape(row_total, head_count, HEAD)
    values = (v_pre + biases[1]).astype(jnp.bfloat16).reshape(row_total, head_count, HEAD)
    raw_score = jnp.einsum("qhd,khd->hqk", queries, keys_low, preferred_element_type=jnp.float32)
    probs = jax.nn.softmax(jnp.where(key_mask[None], raw_score * SCORE_SCALE, NEG_FILL), axis=-1)
    probs_low = probs.astype(jnp.bfloat16)
    mixed = jnp.einsum("hqk,khd->qhd", probs_low, values, preferred_element_type=jnp.float32)
    mixed = mixed.reshape(row_total, feature).astype(jnp.bfloat16)
    branch = dot_plain(mixed, weights[:, 3 * feature :]) + biases[2]
    return (branch, (queries, keys_low, values, probs, probs_low, mixed))


def attend_back(gradient, q_in, kv_in, weights, saved, one_source):
    queries, keys_low, values, probs, probs_low, mixed = saved
    row_total, feature = q_in.shape
    head_count = feature // HEAD
    grad_bias_o = jnp.sum(gradient, axis=0)
    grad_low = gradient.astype(jnp.bfloat16)
    grad_w_o = dot_left(mixed, grad_low)
    grad_mixed = dot_right(grad_low, weights[:, 3 * feature :]).astype(jnp.bfloat16)
    grad_mixed = grad_mixed.reshape(row_total, head_count, HEAD)
    grad_probs = jnp.einsum("qhd,khd->hqk", grad_mixed, values, preferred_element_type=jnp.float32)
    grad_values = jnp.einsum(
        "hqk,qhd->khd", probs_low, grad_mixed, preferred_element_type=jnp.float32
    )
    grad_score = probs * (grad_probs - jnp.sum(grad_probs * probs, axis=-1, keepdims=True))
    grad_raw = (grad_score * SCORE_SCALE).astype(jnp.bfloat16)
    grad_query = jnp.einsum(
        "hqk,khd->qhd", grad_raw, keys_low, preferred_element_type=jnp.float32
    ).reshape(row_total, feature)
    grad_keys = jnp.einsum(
        "hqk,qhd->khd", grad_raw, queries, preferred_element_type=jnp.float32
    ).reshape(row_total, feature)
    grad_values = grad_values.reshape(row_total, feature)
    grad_bias_q = jnp.sum(grad_query, axis=0)
    grad_bias_v = jnp.sum(grad_values, axis=0)
    low_query = grad_query.astype(jnp.bfloat16)
    low_kv = jnp.concatenate(
        [grad_keys.astype(jnp.bfloat16), grad_values.astype(jnp.bfloat16)], axis=1
    )
    if one_source:
        packed = jnp.concatenate([low_query, low_kv], axis=1)
        grad_weights = jnp.concatenate([dot_left(q_in, packed), grad_w_o], axis=1)
        grad_q_in = dot_right(packed, weights[:, : 3 * feature])
        grad_kv_in = grad_q_in
    else:
        grad_weights = jnp.concatenate(
            [dot_left(q_in, low_query), dot_left(kv_in, low_kv), grad_w_o], axis=1
        )
        grad_q_in = dot_right(low_query, weights[:, :feature])
        grad_kv_in = dot_right(low_kv, weights[:, feature : 3 * feature])
    return (grad_q_in, grad_kv_in, grad_weights, (grad_bias_q, grad_bias_v, grad_bias_o))


def feed(rows_in, w_in, b_in, w_out, b_out):
    hidden = dot_plain(rows_in, w_in) + b_in
    active = gelu_exact(hidden).astype(jnp.bfloat16)
    return (dot_plain(active, w_out) + b_out, (hidden, active))


def feed_back(gradient, rows_in, w_in, w_out, saved):
    hidden, active = saved
    grad_b_out = jnp.sum(gradient, axis=0)
    grad_low = gradient.astype(jnp.bfloat16)
    grad_w_out = dot_left(active, grad_low)
    grad_active = dot_right(grad_low, w_out)
    unused, pullback = jax.vjp(gelu_exact, hidden)
    grad_hidden = pullback(grad_active)[0]
    grad_b_in = jnp.sum(grad_hidden, axis=0)
    hidden_low = grad_hidden.astype(jnp.bfloat16)
    grad_w_in = dot_left(rows_in, hidden_low)
    grad_rows = dot_right(hidden_low, w_in)
    return (grad_rows, grad_w_in, grad_b_in, grad_w_out, grad_b_out)


def per_device_any(
    enc_in,
    dec_in,
    bucket,
    enc_lengths,
    dec_lengths,
    enc_attn,
    enc_vec,
    enc_w1,
    enc_w2,
    dec_attn,
    dec_vec,
    dec_w1,
    dec_w2,
    enc_cot,
    dec_cot,
):
    row_total, feature = enc_in.shape
    enc_mask, self_mask, cross_mask = build_masks(
        bucket[0], enc_lengths[0], dec_lengths[0], row_total, enc_lengths.shape[1]
    )
    enc_weights = fetch(enc_attn, enc_vec, enc_w1, enc_w2)
    e_attn, e_vec, e_in, e_out = enc_weights
    e_rows, e_tail = unpack(e_vec, 8, feature)
    branch, e_saved_a = attend(enc_in, enc_in, e_attn, e_rows[0:3], enc_mask, True)
    e_hid_a = enc_in.astype(jnp.float32) + branch
    e_first = norm_rows(e_hid_a, e_rows[3], e_rows[4]).astype(jnp.bfloat16)
    branch, e_saved_f = feed(e_first, e_in, e_tail, e_out, e_rows[5])
    e_hid_f = e_first.astype(jnp.float32) + branch
    encoded = norm_rows(e_hid_f, e_rows[6], e_rows[7]).astype(jnp.bfloat16)
    dec_weights = fetch(dec_attn, dec_vec, dec_w1, dec_w2)
    d_attn, d_vec, d_in, d_out = dec_weights
    d_rows, d_tail = unpack(d_vec, 13, feature)
    branch, d_saved_s = attend(
        dec_in, dec_in, d_attn[:, : 4 * feature], d_rows[0:3], self_mask, True
    )
    d_hid_s = dec_in.astype(jnp.float32) + branch
    d_first = norm_rows(d_hid_s, d_rows[3], d_rows[4]).astype(jnp.bfloat16)
    branch, d_saved_c = attend(
        d_first, encoded, d_attn[:, 4 * feature :], d_rows[5:8], cross_mask, False
    )
    d_hid_c = d_first.astype(jnp.float32) + branch
    d_second = norm_rows(d_hid_c, d_rows[8], d_rows[9]).astype(jnp.bfloat16)
    branch, d_saved_f = feed(d_second, d_in, d_tail, d_out, d_rows[10])
    d_hid_f = d_second.astype(jnp.float32) + branch
    decoded = norm_rows(d_hid_f, d_rows[11], d_rows[12]).astype(jnp.bfloat16)
    dec_weights = fetch_again(dec_attn, dec_vec, dec_w1, dec_w2)
    d_attn, d_vec, d_in, d_out = dec_weights
    d_rows, d_tail = unpack(d_vec, 13, feature)
    gradient, grad_g11, grad_n12 = norm_back(
        d_hid_f, d_rows[11], d_rows[12], dec_cot.astype(jnp.float32)
    )
    grad_rows, grad_d_in, grad_d_tail, grad_d_out, grad_b10 = feed_back(
        gradient, d_second, d_in, d_out, d_saved_f
    )
    gradient, grad_g8, grad_n9 = norm_back(d_hid_c, d_rows[8], d_rows[9], gradient + grad_rows)
    grad_q_in, grad_encoded, grad_cross, cross_bias = attend_back(
        gradient, d_first, encoded, d_attn[:, 4 * feature :], d_saved_c, False
    )
    gradient, grad_g3, grad_n4 = norm_back(d_hid_s, d_rows[3], d_rows[4], gradient + grad_q_in)
    grad_self_in, unused, grad_self, self_bias = attend_back(
        gradient, dec_in, dec_in, d_attn[:, : 4 * feature], d_saved_s, True
    )
    dec_in_grad = gradient + grad_self_in
    dec_stack = jnp.stack(
        [
            self_bias[0],
            self_bias[1],
            self_bias[2],
            grad_g3,
            grad_n4,
            cross_bias[0],
            cross_bias[1],
            cross_bias[2],
            grad_g8,
            grad_n9,
            grad_b10,
            grad_g11,
            grad_n12,
        ]
    )
    dec_vec_full = jnp.concatenate([dec_stack.reshape(-1), grad_d_tail])
    dec_shards = reduce_grads(
        jnp.concatenate([grad_self, grad_cross], axis=1), dec_vec_full, grad_d_in, grad_d_out
    )
    enc_weights = fetch_again(enc_attn, enc_vec, enc_w1, enc_w2)
    e_attn, e_vec, e_in, e_out = enc_weights
    e_rows, e_tail = unpack(e_vec, 8, feature)
    gradient, grad_g6, grad_n7 = norm_back(
        e_hid_f, e_rows[6], e_rows[7], enc_cot.astype(jnp.float32) + grad_encoded
    )
    grad_rows, grad_e_in, grad_e_tail, grad_e_out, grad_b5 = feed_back(
        gradient, e_first, e_in, e_out, e_saved_f
    )
    gradient, grad_g3e, grad_n4e = norm_back(e_hid_a, e_rows[3], e_rows[4], gradient + grad_rows)
    grad_self_in, unused, grad_e_attn, enc_bias = attend_back(
        gradient, enc_in, enc_in, e_attn, e_saved_a, True
    )
    enc_in_grad = gradient + grad_self_in
    enc_stack = jnp.stack(
        [enc_bias[0], enc_bias[1], enc_bias[2], grad_g3e, grad_n4e, grad_b5, grad_g6, grad_n7]
    )
    enc_vec_full = jnp.concatenate([enc_stack.reshape(-1), grad_e_tail])
    enc_shards = reduce_grads(grad_e_attn, enc_vec_full, grad_e_in, grad_e_out)
    return (
        encoded,
        decoded,
        enc_in_grad,
        dec_in_grad,
        enc_shards[0],
        enc_shards[1],
        enc_shards[2],
        enc_shards[3],
        dec_shards[0],
        dec_shards[1],
        dec_shards[2],
        dec_shards[3],
    )


def swap(value, bit):
    return lax.ppermute(value, "fsdp", [(i, i ^ bit) for i in range(8)])


def add_low(*terms):
    total = terms[0].astype(jnp.float32)
    for term in terms[1:]:
        total = total + term.astype(jnp.float32)
    return total.astype(jnp.bfloat16)


def tile_up(rows):
    return -(-rows // ROW_TILE) * ROW_TILE


def size_of(shape):
    total = 1
    for extent in shape:
        total *= extent
    return total


class Order:
    def __init__(self):
        self.token = None
        self.waits = []

    def mark(self, *values):
        self.waits += values

    def tie(self, value):
        if self.token is None:
            return value
        value, self.token = lax.optimization_barrier((value, self.token))
        return value

    def kernel(self, body, operands, specs, outs, scratch, name, flops=0, moved=0):
        extra = self.waits + ([] if self.token is None else [self.token])
        self.waits = []
        count, skip = len(operands), len(extra)
        results = pl.pallas_call(
            lambda *refs: body(*refs[:count], *refs[count + skip :]),
            out_shape=[jax.ShapeDtypeStruct(shape, dtype) for shape, dtype, spec in outs],
            in_specs=list(specs) + [ANY] * skip,
            out_specs=[spec for shape, dtype, spec in outs],
            scratch_shapes=scratch,
            compiler_params=pltpu.CompilerParams(vmem_limit_bytes=VMEM_BYTES),
            cost_estimate=pl.CostEstimate(flops=flops, bytes_accessed=moved, transcendentals=0),
            name=name,
        )(*operands, *extra)
        self.token = min(results, key=lambda result: result.size)
        return results


def pack_body(count, *refs):
    shards, out = refs[:count], refs[-1]
    feature = out.shape[1]
    offset = 0
    for shard in shards:
        rows, columns = shard.shape
        for block in range(columns // feature):
            out[offset : offset + rows, :] = shard[:, block * feature : (block + 1) * feature]
            offset += rows


def split_body(cut, from_x, from_y, top, lower):
    top[...] = from_x[:cut, :]
    lower[...] = from_y[cut:, :]


def vec_rows(vec_part, feature):
    rows = tile_up(-(-vec_part.shape[0] // feature))
    padded = jnp.pad(vec_part, (0, rows * feature - vec_part.shape[0]))
    return padded.reshape(rows, feature)


class Gather:
    def __init__(self, order, feature, name):
        self.order = order
        self.feature = feature
        self.name = name
        self.mine = []

    def sides(self, *shards):
        feature = self.feature
        rows = sum(shard.size for shard in shards) // feature
        (packed,) = self.order.kernel(
            functools.partial(pack_body, len(shards)),
            shards,
            [VMEM] * len(shards),
            [((rows, feature), jnp.bfloat16, VMEM)],
            [],
            self.name + "_pack",
            moved=4 * rows * feature,
        )
        self.mine = [packed, swap(packed, 2), swap(packed, 4)]

    def corners(self):
        rows, feature = self.mine[0].shape
        cut = rows // (2 * ROW_TILE) * ROW_TILE
        top, lower = self.order.kernel(
            functools.partial(split_body, cut),
            self.mine[1:3],
            [VMEM] * 2,
            [
                ((cut, feature), jnp.bfloat16, VMEM),
                ((rows - cut, feature), jnp.bfloat16, VMEM),
            ],
            [],
            self.name + "_split",
            moved=4 * rows * feature,
        )
        self.mine += [swap(top, 4), swap(lower, 2)]

    def join(self, *parts):
        rows, feature = self.mine[0].shape
        joined = self.order.kernel(
            functools.partial(join_body, parts),
            self.mine,
            [ANY] * 5,
            [((4 * count, feature), jnp.bfloat16, ANY) for first, count in parts],
            [pltpu.VMEM((4 * rows, feature), jnp.bfloat16), pltpu.SemaphoreType.DMA((5 + 4 * len(parts),))],
            self.name + "_join",
        )
        return [(part, swap(part, 1)) for part in joined]


def join_body(parts, own, from_x, from_y, top, lower, *refs):
    outs, stage, sems = refs[:-2], refs[-2], refs[-1]
    copies = []
    place = 0
    for index, source in enumerate((own, from_x, from_y, top, lower)):
        rows = source.shape[0]
        copy = pltpu.make_async_copy(source, stage.at[pl.ds(place, rows), :], sems.at[index])
        copy.start()
        copies.append(copy)
        place += rows
    block = own.shape[0]
    stores = []
    for chip in range(4):
        wait_all(copies[chip : chip + 1] if chip < 3 else copies[3:])
        for (first, count), out in zip(parts, outs):
            copy = pltpu.make_async_copy(
                stage.at[pl.ds(chip * block + first, count), :],
                out.at[pl.ds(chip * count, count), :],
                sems.at[5 + len(stores)],
            )
            copy.start()
            stores.append(copy)
    wait_all(stores)


def vec_body(table, mine, theirs, out, sems):
    rows = out.shape[0] // 8
    block = mine.shape[0] // 4
    copies = []
    for chip in range(4):
        for core, source in enumerate((mine, theirs)):
            copies.append(
                pltpu.make_async_copy(
                    source.at[pl.ds((chip + 1) * block - rows, rows), :],
                    out.at[pl.ds(pl.multiple_of(table[2 * chip + core] * rows, ROW_TILE), rows), :],
                    sems.at[len(copies)],
                )
            )
    for copy in copies:
        copy.start()
    wait_all(copies)


def gathered_vec(order, buffers, table, rows, feature):
    (out,) = order.kernel(
        vec_body,
        [table, *buffers],
        [SMEM] + [ANY] * 2,
        [((8 * rows, feature), jnp.bfloat16, VMEM)],
        [pltpu.SemaphoreType.DMA((8,))],
        "vectors",
    )
    return out.reshape(8, rows * feature)


class Loader:
    def __init__(self, buffers, table, sems, used=0):
        self.buffers = buffers
        self.block = buffers[0].shape[0] // 4
        self.table = table
        self.sems = sems
        self.used = used

    def unit(self, number, target, stride, first):
        rows = target.shape[1] // 8
        copies = []
        for chip in range(4):
            for core in range(2):
                offset = chip * self.block + number * rows
                place = pl.multiple_of(self.table[2 * chip + core] * stride + first, ROW_TILE)
                copy = pltpu.make_async_copy(
                    self.buffers[core].at[pl.ds(offset, rows), :],
                    target.at[pl.ds(place, rows), :],
                    self.sems.at[self.used],
                )
                copy.start()
                self.used += 1
                copies.append(copy)
        return copies

    def wide(self, number, target):
        return self.unit(number, target, target.shape[1] // 8, 0)

    def tall(self, number, target):
        rows = target.shape[1] // 8
        copies = []
        for block in range(4):
            copies += self.unit(number + block, target, 4 * rows, block * rows)
        return copies


def wait_all(copies):
    for copy in copies:
        copy.wait()


class Storer:
    def __init__(self, outs, table, slots, sems):
        self.keep, self.upper, self.lower = outs if len(outs) == 3 else (outs[0], None, outs[1])
        self.table = table
        self.slots = slots
        self.block = self.keep.shape[1] // 2
        self.sems = sems
        self.copies = []

    def add(self, source, out, row):
        copy = pltpu.make_async_copy(
            source, out.at[pl.ds(row, source.shape[0]), :], self.sems.at[len(self.copies)]
        )
        copy.start()
        self.copies.append(copy)

    def rows(self, source, stride, count, offset):
        for core in (1, 0):
            for slot in (2, 3, 0, 1):
                place = self.table[2 * self.slots[slot] + core] * stride
                block = source.at[pl.ds(pl.multiple_of(place, ROW_TILE), count), :]
                if core == 0:
                    self.add(block, self.keep, slot * self.block + offset)
                elif slot < 2 or self.upper is None:
                    self.add(block, self.lower, slot * self.block + offset)
                else:
                    self.add(block, self.upper, (slot - 2) * self.block + offset)

    def tail(self, source):
        self.add(source, self.lower, (4 if self.upper is None else 2) * self.block)
        self.add(source, self.keep, 4 * self.block)

    def finish(self):
        wait_all(self.copies)


def gradient_outs(feature, extra=0, single=False):
    rows = feature // 2
    if single:
        return [((4 * rows + extra, feature), jnp.bfloat16, ANY)] * 2
    return [((count, feature), jnp.bfloat16, ANY) for count in (4 * rows + extra, 2 * rows, 2 * rows + extra)]


def low(value):
    return value.astype(jnp.bfloat16)


def layer_norm(hidden, gain, shift):
    mean = jnp.mean(hidden, axis=-1, keepdims=True)
    centred = hidden - mean
    variance = jnp.mean(centred * centred, axis=-1, keepdims=True)
    return centred * lax.rsqrt(variance + EPSILON) * gain + shift


def layer_norm_back(hidden, gain, gradient):
    mean = jnp.mean(hidden, axis=-1, keepdims=True)
    centred = hidden - mean
    variance = jnp.mean(centred * centred, axis=-1, keepdims=True)
    scale = lax.rsqrt(variance + EPSILON)
    unit = centred * scale
    grad_gain = jnp.sum(gradient * unit, axis=0, keepdims=True)
    grad_shift = jnp.sum(gradient, axis=0, keepdims=True)
    inner = gradient * gain
    mean_inner = jnp.mean(inner, axis=-1, keepdims=True)
    mean_unit = jnp.mean(inner * unit, axis=-1, keepdims=True)
    return (scale * (inner - mean_inner - unit * mean_unit), grad_gain, grad_shift)


def key_mask(bucket, lengths, rows, segs, causal):
    span = rows // segs
    one_long = bucket[0] == 1
    query = lax.broadcasted_iota(jnp.int32, (rows, rows), 0)
    key = lax.broadcasted_iota(jnp.int32, (rows, rows), 1)
    key_row = lax.broadcasted_iota(jnp.int32, (1, rows), 1)
    limit = jnp.zeros((1, rows), jnp.int32)
    start = jnp.zeros((1, rows), jnp.int32)
    first = jnp.zeros((rows, 1), jnp.int32)
    query_col = lax.broadcasted_iota(jnp.int32, (rows, 1), 0)
    for seg in range(segs):
        inside = (key_row >= seg * span) & (key_row < (seg + 1) * span)
        limit = jnp.where(inside, seg * span + lengths[0, seg], limit)
        start = jnp.where(inside, seg * span, start)
        first = jnp.where((query_col >= seg * span) & (query_col < (seg + 1) * span), seg * span, first)
    limit = jnp.where(one_long, lengths[0, 0], limit)
    start = jnp.where(one_long, 0, start)
    first = jnp.where(one_long, 0, first)
    mask = (first == start) & (key < limit)
    if causal:
        mask = mask & (key <= query)
    return mask


def head_lanes(rows):
    return lax.broadcasted_iota(jnp.int32, (rows, PAIR), 1) < HEAD


def attn_body(
    cross, causal, first_unit, segs, table, bucket, lengths, *refs
):
    refs = list(refs)
    q_in = refs.pop(0)
    kv_in = refs.pop(0) if cross else q_in
    vec = refs.pop(0)
    buffers = [refs.pop(0) for _ in range(2)]
    hidden_out, norm_out, q_out, k_out, v_out, o_out, p_out = refs[:7]
    w_q, w_k, w_v, w_o, sems = refs[7:]
    rows, feature = q_in.shape
    load = Loader(buffers, table, sems)
    waits = [load.wide(first_unit + i, w) for i, w in enumerate((w_q, w_k, w_v, w_o))]
    mask = key_mask(bucket, lengths, rows, segs, causal)
    lanes = head_lanes(rows)
    wait_all(waits[0])
    q_out[...] = low(dot_plain(q_in[...], w_q[...]) + vec[0:1, :])
    wait_all(waits[1])
    k_out[...] = low(dot_plain(kv_in[...], w_k[...]))
    wait_all(waits[2])
    v_out[...] = low(dot_plain(kv_in[...], w_v[...]) + vec[1:2, :])
    for pair in range(feature // PAIR):
        columns = slice(pair * PAIR, (pair + 1) * PAIR)
        q_pair, k_pair, v_pair = q_out[:, columns], k_out[:, columns], v_out[:, columns]
        mixed = []
        for half in range(2):
            mine = lanes if half == 0 else ~lanes
            score = dot_right(jnp.where(mine, q_pair, jnp.zeros_like(q_pair)), k_pair)
            score = jnp.where(mask, score * SCORE_SCALE, NEG_FILL)
            power = jnp.exp(score - jnp.max(score, axis=-1, keepdims=True))
            probs = low(power / jnp.sum(power, axis=-1, keepdims=True))
            p_out[2 * pair + half] = probs
            mixed.append(dot_plain(probs, v_pair))
        o_out[:, columns] = low(jnp.where(lanes, mixed[0], mixed[1]))
    wait_all(waits[3])
    hidden = q_in[...].astype(jnp.float32) + (dot_plain(o_out[...], w_o[...]) + vec[2:3, :])
    hidden_out[...] = hidden
    norm_out[...] = low(layer_norm(hidden, vec[3:4, :], vec[4:5, :]))


def attn_forward(order, q_in, kv_in, vec, weights, ids, lengths, causal, name):
    rows, feature = q_in.shape
    sources = [q_in] + ([] if kv_in is None else [kv_in]) + [vec]
    wide = ((rows, feature), jnp.bfloat16, VMEM)
    return order.kernel(
        functools.partial(attn_body, kv_in is not None, causal, weights[1], lengths.shape[1]),
        [*ids, lengths, *sources, *weights[0]],
        [SMEM] * 3 + [VMEM] * len(sources) + [ANY] * 2,
        [((rows, feature), jnp.float32, VMEM)]
        + [wide] * 5
        + [((feature // HEAD, rows, rows), jnp.bfloat16, VMEM)],
        [pltpu.VMEM((feature, feature), jnp.bfloat16)] * 4 + [pltpu.SemaphoreType.DMA((32,))],
        name,
        8 * rows * feature * feature,
        10 * feature * feature,
    )


def gelu_parts(hidden):
    phi = 0.5 * (1.0 + lax.erf(hidden * 0.7071067811865476))
    slope = phi + hidden * (0.3989422804014327 * jnp.exp(-0.5 * hidden * hidden))
    return (hidden * phi, slope)


def feed_body(units, table, rows_in, vec, b_in, *refs):
    hidden_out, norm_out, r_out, slope_out, w_in, w_out, sems = refs[4:]
    feature = rows_in.shape[1]
    load = Loader(refs[:2], table, sems)
    waits = [load.wide(units[0] + j, w_in.at[j]) for j in range(4)]
    tail = Loader(refs[2:4], table, sems, load.used).tall(units[1], w_out)
    total = None
    for j in range(4):
        columns = slice(j * feature, (j + 1) * feature)
        wait_all(waits[j])
        hidden = dot_plain(rows_in[...], w_in[j]) + b_in[:, columns]
        active, slope = gelu_parts(hidden)
        r_out[:, columns] = low(active)
        slope_out[:, columns] = low(slope)
    wait_all(tail)
    total = dot_plain(r_out[...], w_out[...]) + vec[0:1, :]
    hidden = rows_in[...].astype(jnp.float32) + total
    hidden_out[...] = hidden
    norm_out[...] = low(layer_norm(hidden, vec[1:2, :], vec[2:3, :]))


def feed_forward(order, rows_in, vec, b_in, w_in, w_out, table, name):
    rows, feature = rows_in.shape
    width = b_in.shape[1]
    return order.kernel(
        functools.partial(feed_body, (w_in[1], w_out[1])),
        [table, rows_in, vec, b_in, *w_in[0], *w_out[0]],
        [SMEM] + [VMEM] * 3 + [ANY] * 4,
        [
            ((rows, feature), jnp.float32, VMEM),
            ((rows, feature), jnp.bfloat16, VMEM),
            ((rows, width), jnp.bfloat16, VMEM),
            ((rows, width), jnp.bfloat16, VMEM),
        ],
        [
            pltpu.VMEM((4, feature, feature), jnp.bfloat16),
            pltpu.VMEM((width, feature), jnp.bfloat16),
            pltpu.SemaphoreType.DMA((64,)),
        ],
        name,
        4 * rows * feature * width,
        8 * feature * width,
    )


def feed_back_out_body(extra, slots, table, *refs):
    refs = list(refs)
    gradient = refs.pop(0)[...].astype(jnp.float32)
    if extra:
        gradient = gradient + refs.pop(0)[...].astype(jnp.float32)
    hidden, gain, active, g_out, sums, keep, upper, lower, stage, out_sems = refs
    feature = hidden.shape[1]
    store = Storer((keep, upper, lower), table, slots, out_sems)
    gradient, grad_gain, grad_shift = layer_norm_back(hidden[...], gain[...], gradient)
    sums[0:1, :] = jnp.sum(gradient, axis=0, keepdims=True)
    sums[1:2, :] = grad_gain
    sums[2:3, :] = grad_shift
    g_out[...] = gradient
    grad_low = low(gradient)
    for j in range(4):
        columns = slice(j * feature, (j + 1) * feature)
        stage[columns, :] = low(dot_left(active[:, columns], grad_low))
    store.rows(stage, feature // 2, feature // 2, 0)
    store.finish()


def feed_back_out(order, gradients, hidden, gain, active, table, slots, name):
    rows, feature = hidden.shape
    width = active.shape[1]
    return order.kernel(
        functools.partial(feed_back_out_body, len(gradients) == 2, slots),
        [table, *gradients, hidden, gain, active],
        [SMEM] + [VMEM] * (len(gradients) + 3),
        [((rows, feature), jnp.float32, VMEM), ((3, feature), jnp.float32, VMEM), *gradient_outs(feature)],
        [pltpu.VMEM((width, feature), jnp.bfloat16), pltpu.SemaphoreType.DMA((8,))],
        name,
        2 * rows * feature * width,
        4 * feature * width,
    )


def feed_back_in_body(slots, units, table, gradient, slope, rows_in, *refs):
    total_out, bias_in, keep, upper, lower, w_in, w_out, grad_hidden, stage, sems, out_sems = refs[4:]
    feature = rows_in.shape[1]
    tail = Loader(refs[2:4], table, sems).tall(units[1], w_out)
    load = Loader(refs[:2], table, sems, len(tail))
    waits = [load.wide(units[0] + j, w_in.at[j]) for j in range(4)]
    store = Storer((keep, upper, lower), table, slots, out_sems)
    total = gradient[...]
    grad_low = low(total)
    wait_all(tail)
    for j in range(4):
        columns = slice(j * feature, (j + 1) * feature)
        hidden = dot_right(grad_low, w_out[columns, :]) * slope[:, columns].astype(jnp.float32)
        bias_in[j : j + 1, :] = jnp.sum(hidden, axis=0, keepdims=True)
        grad_hidden[:, columns] = low(hidden)
        stage[j] = low(dot_left(rows_in[...], grad_hidden[:, columns]))
        store.rows(stage.at[j], feature // 8, feature // 8, j * (feature // 8))
    for j in range(4):
        columns = slice(j * feature, (j + 1) * feature)
        wait_all(waits[j])
        total = total + dot_right(grad_hidden[:, columns], w_in[j])
    total_out[...] = total
    store.finish()


def feed_back_in(order, gradient, slope, rows_in, w_in, w_out, table, slots, name):
    rows, feature = rows_in.shape
    width = slope.shape[1]
    square = pltpu.VMEM((4, feature, feature), jnp.bfloat16)
    return order.kernel(
        functools.partial(feed_back_in_body, slots, (w_in[1], w_out[1])),
        [table, gradient, slope, rows_in, *w_in[0], *w_out[0]],
        [SMEM] + [VMEM] * 3 + [ANY] * 4,
        [((rows, feature), jnp.float32, VMEM), ((4, feature), jnp.float32, VMEM), *gradient_outs(feature)],
        [
            square,
            pltpu.VMEM((width, feature), jnp.bfloat16),
            pltpu.VMEM((rows, width), jnp.bfloat16),
            square,
            pltpu.SemaphoreType.DMA((64,)),
            pltpu.SemaphoreType.DMA((32,)),
        ],
        name,
        6 * rows * feature * width,
        6 * feature * width,
    )


def attn_back_body(cross, first_unit, others, slots, out_count, table, gradient, *refs):
    refs = list(refs)
    other_sums = [refs.pop(0) for _ in range(others)]
    hidden, gain, q_in = refs[:3]
    refs = refs[3:]
    kv_in = refs.pop(0) if cross else q_in
    queries, keys, values, mixed, probs_in = refs[:5]
    buffers = refs[5:7]
    refs = refs[7:]
    q_grad_out = refs.pop(0)
    kv_grad_out = refs.pop(0) if cross else None
    sums = refs.pop(0)
    grads = [refs.pop(0) for _ in range(out_count)]
    w_q, w_k, w_v, w_o, stage, go, gq, gk, gv, vec_low, sems, out_sems = refs
    rows, feature = hidden.shape
    unit = feature // 8
    load = Loader(buffers, table, sems)
    wait_o = load.wide(first_unit + 3, w_o)
    waits = [load.wide(first_unit + i, w) for i, w in enumerate((w_q, w_k, w_v))]
    store = Storer(grads, table, slots, out_sems)
    lanes = head_lanes(rows)
    total, grad_gain, grad_shift = layer_norm_back(hidden[...], gain[...], gradient[...])
    sums[2:3, :] = jnp.sum(total, axis=0, keepdims=True)
    sums[3:4, :] = grad_gain
    sums[4:5, :] = grad_shift
    grad_low = low(total)
    stage[3] = low(dot_left(mixed[...], grad_low))
    store.rows(stage.at[3], unit, unit, 3 * unit)
    wait_all(wait_o)
    go[...] = low(dot_right(grad_low, w_o[...]))
    for pair in range(feature // PAIR):
        columns = slice(pair * PAIR, (pair + 1) * PAIR)
        q_pair, k_pair, v_pair = queries[:, columns], keys[:, columns], values[:, columns]
        go_pair = go[:, columns]
        parts = []
        for half in range(2):
            mine = lanes if half == 0 else ~lanes
            probs_low = probs_in[2 * pair + half]
            probs = probs_low.astype(jnp.float32)
            grad_probs = dot_right(jnp.where(mine, go_pair, jnp.zeros_like(go_pair)), v_pair)
            weighted = grad_probs * probs
            row_sum = jnp.sum(weighted, axis=-1, keepdims=True)
            grad_raw = low((weighted - probs * row_sum) * SCORE_SCALE)
            parts.append(
                (
                    dot_plain(grad_raw, k_pair),
                    dot_left(grad_raw, q_pair),
                    dot_left(probs_low, go_pair),
                )
            )
        grad_q, grad_k, grad_v = (jnp.where(lanes, a, b) for a, b in zip(*parts))
        sums[0:1, columns] = jnp.sum(grad_q, axis=0, keepdims=True)
        sums[1:2, columns] = jnp.sum(grad_v, axis=0, keepdims=True)
        gq[:, columns] = low(grad_q)
        gk[:, columns] = low(grad_k)
        gv[:, columns] = low(grad_v)
    if others:
        parts = [sums[...]] + [other[...] for other in other_sums]
        count = sum(part.shape[0] for part in parts)
        parts.append(jnp.zeros((vec_low.shape[0] - count, feature), jnp.float32))
        vec_low[...] = low(jnp.concatenate(parts, axis=0))
        store.tail(vec_low)
    for index, (source, grad) in enumerate(((q_in, gq), (kv_in, gk), (kv_in, gv))):
        stage[index] = low(dot_left(source[...], grad[...]))
        store.rows(stage.at[index], unit, unit, index * unit)
    for copies in waits:
        wait_all(copies)
    total = total + dot_right(gq[...], w_q[...])
    kv_total = dot_right(gk[...], w_k[...]) + dot_right(gv[...], w_v[...])
    if cross:
        q_grad_out[...] = total
        kv_grad_out[...] = kv_total
    else:
        q_grad_out[...] = total + kv_total
    store.finish()


def attn_back(
    order, gradient, hidden, gain, q_in, kv_in, saved, weights, table, others, slots, name, single=False
):
    rows, feature = hidden.shape
    cross = kv_in is not None
    sources = [gradient, *others, hidden, gain, q_in] + ([kv_in] if cross else []) + list(saved)
    count = tile_up(5 + sum(other.shape[0] for other in others)) if others else 0
    return order.kernel(
        functools.partial(attn_back_body, cross, weights[1], len(others), slots, 2 if single else 3),
        [table, *sources, *weights[0]],
        [SMEM] + [VMEM] * len(sources) + [ANY] * 2,
        [((rows, feature), jnp.float32, VMEM)] * (1 + cross)
        + [((5, feature), jnp.float32, VMEM), *gradient_outs(feature, count, single)],
        [pltpu.VMEM((feature, feature), jnp.bfloat16)] * 4
        + [pltpu.VMEM((4, feature, feature), jnp.bfloat16)]
        + [pltpu.VMEM((rows, feature), jnp.bfloat16)] * 4
        + [pltpu.VMEM((max(count, ROW_TILE), feature), jnp.bfloat16)]
        + [pltpu.SemaphoreType.DMA((32,)), pltpu.SemaphoreType.DMA((34,))],
        name,
        16 * rows * feature * feature,
        20 * feature * feature,
    )


def combine_body(plan, count, *refs):
    inputs = refs[:count]
    outs = refs[count:-4]
    landed, summed, in_sems, out_sems = refs[-4:]
    loads = []
    place = 0
    for out, first, rows, terms in plan:
        parts = []
        for source, row in terms:
            copy = pltpu.make_async_copy(
                inputs[source].at[pl.ds(row, rows), :],
                landed.at[pl.ds(place, rows), :],
                in_sems.at[sum(len(other) for other in loads) + len(parts)],
            )
            copy.start()
            parts.append((copy, place))
            place += rows
        loads.append(parts)
    stores = []
    place = 0
    for (out, first, rows, terms), parts in zip(plan, loads):
        total = None
        for copy, start in parts:
            copy.wait()
            term = landed[start : start + rows, :].astype(jnp.float32)
            total = term if total is None else total + term
        summed[place : place + rows, :] = low(total)
        copy = pltpu.make_async_copy(
            summed.at[pl.ds(place, rows), :],
            outs[out].at[pl.ds(first, rows), :],
            out_sems.at[len(stores)],
        )
        copy.start()
        stores.append(copy)
        place += rows
    wait_all(stores)


def combine(order, name, *jobs):
    inputs, plan, outs = [], [], []
    for sizes, sums, use in jobs:
        for out, first, rows, terms in sums:
            places = []
            for array, row in terms:
                known = [index for index, other in enumerate(inputs) if other is array]
                if not known:
                    inputs.append(array)
                places.append((known[0] if known else len(inputs) - 1, row))
            plan.append((len(outs) + out, first, rows, tuple(places)))
        outs += sizes
    feature = inputs[0].shape[1]
    reads = sum(rows * len(terms) for out, first, rows, terms in plan)
    writes = sum(rows for out, first, rows, terms in plan)
    results = order.kernel(
        functools.partial(combine_body, plan, len(inputs)),
        inputs,
        [ANY] * len(inputs),
        [((rows, feature), jnp.bfloat16, ANY) for rows in outs],
        [
            pltpu.VMEM((reads, feature), jnp.bfloat16),
            pltpu.VMEM((writes, feature), jnp.bfloat16),
            pltpu.SemaphoreType.DMA((sum(len(terms) for out, first, rows, terms in plan),)),
            pltpu.SemaphoreType.DMA((len(plan),)),
        ],
        name,
    )
    for sizes, sums, use in jobs:
        use(*results[: len(sizes)])
        results = results[len(sizes) :]


OWN, X, Y, DIAGONAL = range(4)
X_FIRST = (OWN, Y, X, DIAGONAL)
Y_FIRST = (OWN, X, Y, DIAGONAL)


class Reduce:
    def __init__(self, order, outs, slots, both=False, pad=0):
        self.order = order
        self.pad = pad
        self.keep, self.upper, self.lower = outs if len(outs) == 3 else (outs[0], None, outs[1])
        self.both = both
        self.bits = (2, 4) if slots == X_FIRST else (4, 2)
        self.rows = self.keep.shape[1] // 2
        self.extra = self.keep.shape[0] - 4 * self.rows

    def cores(self):
        self.from_upper = None if self.upper is None else swap(self.order.tie(self.upper), 1)
        self.from_lower = swap(self.order.tie(self.lower), 1)

    def cores_done(self):
        self.order.mark(*(value for value in (self.from_upper, self.from_lower) if value is not None))

    def block(self, slot, first=0):
        row = slot * self.rows + first
        other = (self.from_lower, row) if slot < 2 or self.upper is None else (self.from_upper, row - 2 * self.rows)
        return ((self.keep, row), other)

    def extra_rows(self):
        return ((self.keep, 4 * self.rows), (self.from_lower, (4 if self.upper is None else 2) * self.rows))

    def first(self):
        rows, extra = self.rows, self.extra
        if not self.both:
            plan = [(0, 0, rows, self.block(2)), (0, rows, rows, self.block(3))]
            if extra:
                plan.append((0, 2 * rows, extra, self.extra_rows()))
            if self.pad:
                plan.append((0, 2 * rows + extra, self.pad, self.block(2)[:1]))
            return ([2 * rows + extra + self.pad], plan, self.first_sent)
        cut = rows // 2
        plan = [(0, 0, cut, self.block(3)), (1, 0, cut, self.block(3, cut))]
        if extra:
            plan.append((0, cut, extra, self.extra_rows()))
        return ([cut + extra, cut], plan, self.first_sent)

    def first_sent(self, *sent):
        self.sent = sent[0]
        self.landed = [swap(value, bit) for value, bit in zip(sent, (2, 4) if self.both else self.bits)]

    def second(self):
        rows, extra = self.rows, self.extra
        if not self.both:
            landed = self.landed[0]
            plan = [(0, 0, rows, self.block(1) + ((landed, rows),))]
            if extra:
                plan.append((0, rows, extra, ((self.sent, 2 * rows), (landed, 2 * rows))))
            return ([rows + extra], plan, self.second_sent)
        cut = rows // 2
        from_x, from_y = self.landed
        plan = [
            (0, 0, cut, self.block(1)),
            (0, cut, cut, self.block(1, cut) + ((from_y, 0),)),
            (1, 0, cut, self.block(2) + ((from_x, 0),)),
            (1, cut, cut, self.block(2, cut)),
        ]
        if extra:
            plan.append((1, rows, extra, ((self.sent, cut), (from_x, cut))))
        return ([rows, rows + extra], plan, self.second_sent)

    def second_sent(self, *sent):
        self.sent_last = sent[-1]
        self.last = [swap(value, bit) for value, bit in zip(sent, (2, 4) if self.both else self.bits[1:])]

    def own(self, use):
        rows, extra = self.rows, self.extra
        terms = self.block(0) + tuple((value, 0) for value in self.last)
        if not self.both:
            terms += ((self.landed[0], 0),)
        plan = [(0, 0, rows, terms)]
        if extra:
            plan.append((0, rows, extra, ((self.sent_last, rows), (self.last[-1], rows))))
        return ([rows + extra], plan, use)


def own_stack(pieces, use):
    rows = pieces[0].rows
    plan = [(0, index * rows) + piece.own(None)[1][0][2:] for index, piece in enumerate(pieces)]
    return ([len(pieces) * rows], plan, use)


class Line:
    def __init__(self, value):
        self.value = value
        self.landed = lax.ppermute(value, "rep", [(0, 1), (3, 2)])

    def part(self, first):
        return (self, first)

    def step(self, use):
        rows = self.value.shape[0]
        return ([rows], [(0, 0, rows, ((self.value, 0), (self.landed, 0)))], use)

    def middle(self):
        return self.step(self.middle_sent)

    def middle_sent(self, value):
        self.value = value
        self.landed = lax.ppermute(value, "rep", [(1, 2), (2, 1)])

    def outward(self):
        return self.step(self.outward_sent)

    def outward_sent(self, value):
        self.value = value
        self.landed = lax.ppermute(value, "rep", [(1, 0), (2, 3)])


def finish_body(parts, inner, *refs):
    wide, rest = refs[2 * len(parts)], list(refs[2 * len(parts) + 1 :])
    feature = refs[0].shape[1]
    unit = feature // 8
    for index, first in enumerate(parts):
        value, landed = refs[2 * index], refs[2 * index + 1]

        def rows(begin, count):
            mine = value[first + begin : first + begin + count, :].astype(jnp.float32)
            other = landed[first + begin : first + begin + count, :].astype(jnp.float32)
            return jnp.where(inner[0] == 1, mine, other)

        for j in range(4):
            column = (4 * index + j) * feature
            if wide.shape[0] == unit:
                wide[:, column : column + feature] = rows(j * unit, unit)
            else:
                wide[j * unit : (j + 1) * unit, :] = rows(j * unit, unit)
        if first == 0 and value.shape[0] % (4 * unit):
            rest.pop(0)[...] = rows(4 * unit, value.shape[0] - 4 * unit)


def finish(order, inner, parts, wide, name):
    operands = [inner]
    for line, first in parts:
        operands += [line.value, line.landed]
    feature = operands[1].shape[1]
    unit = feature // 8
    shape = (unit, 4 * feature * len(parts)) if wide else (4 * unit, feature)
    outs = [(shape, jnp.float32, VMEM)]
    for line, first in parts:
        rows = line.value.shape[0] % (4 * unit)
        if rows:
            outs.append(((rows, feature), jnp.float32, VMEM))
    return order.kernel(
        functools.partial(finish_body, [first for line, first in parts]),
        operands,
        [SMEM] + [VMEM] * (len(operands) - 1),
        outs,
        [],
        name,
    )


def per_device(
    enc_in,
    dec_in,
    bucket,
    enc_lengths,
    dec_lengths,
    enc_attn,
    enc_vec,
    enc_w1,
    enc_w2,
    dec_attn,
    dec_vec,
    dec_w1,
    dec_w2,
    enc_cot,
    dec_cot,
):
    feature = enc_in.shape[1]
    unit = feature // 8
    chip_index = lax.axis_index("fsdp").astype(jnp.int32)
    table = chip_index ^ jnp.arange(8, dtype=jnp.int32)
    place = lax.axis_index("rep")
    inner = ((place == 1) | (place == 2)).astype(jnp.int32).reshape(1)
    ids = (table, bucket)
    order = Order()
    mark = order.mark
    g_1, g_2, g_3, g_4 = (Gather(order, feature, "piece_" + name) for name in "1234")
    half = 4 * unit
    e_len, d_len = enc_vec.shape[0], dec_vec.shape[0]
    vec_part = vec_rows(jnp.concatenate([enc_vec, dec_vec]), feature)
    g_1.sides(enc_attn, dec_attn[:, : 4 * feature], vec_part)
    g_2.sides(enc_w1, enc_w2)
    g_1.corners()
    g_2.corners()
    mark(*g_2.mine[3:])
    (attn_pair,) = g_1.join((0, 2 * half + vec_part.shape[0]))
    (e_feed,) = g_2.join((0, 2 * half))
    g_3.sides(dec_attn[:, 4 * feature :], dec_w1)
    vecs = gathered_vec(order, attn_pair, table, vec_part.shape[0], feature)
    e_rows, e_tail = unpack(vecs[:, :e_len].reshape(-1), 8, feature)
    d_rows, d_tail = unpack(vecs[:, e_len : e_len + d_len].reshape(-1), 13, feature)
    e_tail, d_tail = e_tail.reshape(1, -1), d_tail.reshape(1, -1)
    e_hid_a, e_first, *e_saved = attn_forward(
        order, enc_in, None, e_rows[0:5], (attn_pair, 0), ids, enc_lengths, False, "enc_attn"
    )
    mark(e_feed[1], d_rows, d_tail, e_tail)
    g_4.sides(dec_w2)
    d_hid_s, d_first, *s_saved = attn_forward(
        order, dec_in, None, d_rows[0:5], (attn_pair, 4), ids, dec_lengths, True, "dec_self"
    )
    g_3.corners()
    e_hid_f, encoded, e_act, e_slope = feed_forward(
        order, e_first, e_rows[5:8], e_tail, (e_feed, 0), (e_feed, 4), table, "enc_feed"
    )
    g_4.corners()
    cross_pair, w1_pair = g_3.join((0, half), (half, half))
    (w2_pair,) = g_4.join((0, half))
    d_hid_c, d_second, *c_saved = attn_forward(
        order, d_first, encoded, d_rows[5:10], (cross_pair, 0), ids, enc_lengths, False, "dec_cross"
    )
    d_hid_f, decoded, d_act, d_slope = feed_forward(
        order, d_second, d_rows[10:13], d_tail, (w1_pair, 0), (w2_pair, 0), table, "dec_feed"
    )
    gradient, d_sums_f, *outs = feed_back_out(
        order, [dec_cot], d_hid_f, d_rows[11:12], d_act, table, X_FIRST, "dec_back_out"
    )
    red_0 = Reduce(order, outs, X_FIRST)
    red_0.cores()
    gradient, d_bias, *outs = feed_back_in(
        order, gradient, d_slope, d_second, (w1_pair, 0), (w2_pair, 0), table, Y_FIRST, "dec_back_in"
    )
    red_1 = Reduce(order, outs, Y_FIRST)
    red_0.cores_done()
    combine(order, "add_1", red_0.first())
    red_1.cores()
    gradient, grad_encoded, d_sums_c, *outs = attn_back(
        order, gradient, d_hid_c, d_rows[8:9], d_first, encoded, c_saved, (cross_pair, 0), table, [],
        X_FIRST, "cross_back",
    )
    red_2 = Reduce(order, outs, X_FIRST)
    red_1.cores_done()
    combine(order, "add_2", red_1.first())
    red_2.cores()
    e_gradient, e_sums_f, *outs = feed_back_out(
        order, [enc_cot, grad_encoded], e_hid_f, e_rows[6:7], e_act, table, Y_FIRST, "enc_back_out"
    )
    red_3 = Reduce(order, outs, Y_FIRST, pad=2 * ROW_TILE)
    combine(order, "add_3a", red_0.second())
    red_2.cores_done()
    combine(order, "add_3b", red_2.first())
    red_3.cores()
    e_gradient, e_bias, *outs = feed_back_in(
        order, e_gradient, e_slope, e_first, (e_feed, 0), (e_feed, 4), table, X_FIRST, "enc_back_in"
    )
    red_4 = Reduce(order, outs, X_FIRST)
    totals = {}

    def keep_as(key):
        return lambda value: totals.update({key: value})

    mark(*red_0.last)
    combine(order, "add_4a", red_1.second())
    red_3.cores_done()
    combine(order, "add_4b", red_3.first())
    red_4.cores()
    dec_in_grad, d_sums_s, *outs = attn_back(
        order, gradient, d_hid_s, d_rows[3:4], dec_in, None, s_saved, (attn_pair, 4), table,
        [d_sums_c, d_sums_f, d_bias], Y_FIRST, "self_back",
    )
    red_5 = Reduce(order, outs, Y_FIRST, True)
    combine(order, "add_5a", red_2.second())
    mark(*red_1.last)
    red_4.cores_done()
    combine(order, "add_5b", red_4.first())
    red_5.cores()
    enc_in_grad, e_sums_a, *outs = attn_back(
        order, e_gradient, e_hid_a, e_rows[3:4], enc_in, None, e_saved, (attn_pair, 0), table,
        [e_sums_f, e_bias], Y_FIRST, "enc_attn_back", True,
    )
    red_6 = Reduce(order, outs, Y_FIRST, True)
    red_5.cores_done()
    mark(*red_2.last)
    combine(
        order, "add_6a", red_3.second(), red_5.first(), own_stack([red_0, red_1], keep_as("a"))
    )
    line_a = Line(totals["a"])
    mark(red_5.landed[1])
    combine(order, "add_6b", red_4.second())
    red_6.cores()
    mark(*red_3.last)
    red_6.cores_done()
    combine(order, "add_6c", red_6.first())
    mark(*red_6.landed, *red_4.last)
    combine(order, "add_8", line_a.middle(), red_5.second(), own_stack([red_2, red_3], keep_as("b")))
    line_b = Line(totals["b"])
    mark(*red_5.last)
    combine(order, "add_9", red_6.second(), red_4.own(keep_as(4)), red_5.own(keep_as(5)))
    combine(order, "add_10", line_a.outward(), line_b.middle(), red_6.own(keep_as(6)))
    line_4 = Line(totals[4])
    line_5 = Line(order.tie(totals[5]))
    combine(order, "add_11", line_b.outward(), line_4.middle())
    combine(order, "add_12", line_5.middle())
    line_6 = Line(order.tie(totals[6]))
    (grad_d_w2,) = finish(order, inner, [line_a.part(0)], False, "out_0")
    (grad_d_w1,) = finish(order, inner, [line_a.part(half)], True, "out_1")
    combine(order, "add_13", line_4.outward(), line_6.middle())
    combine(order, "add_14", line_5.outward())
    (grad_e_w2,) = finish(order, inner, [line_b.part(half)], False, "out_3")
    (grad_e_w1,) = finish(order, inner, [line_4.part(0)], True, "out_4")
    combine(order, "add_15", line_6.outward())
    grad_d_attn, d_vec = finish(order, inner, [line_5.part(0), line_b.part(0)], True, "out_5")
    grad_e_attn, e_vec = finish(order, inner, [line_6.part(0)], True, "out_6")

    def own_part(rows, length):
        return lax.dynamic_slice(rows.reshape(-1), (chip_index * length,), (length,))

    return (
        encoded,
        decoded,
        enc_in_grad,
        dec_in_grad,
        grad_e_attn,
        own_part(e_vec, e_len),
        grad_e_w1,
        grad_e_w2,
        grad_d_attn,
        own_part(d_vec, d_len),
        grad_d_w1,
        grad_d_w2,
    )


def solution(mesh):
    in_specs = (
        P(("rep", "fsdp"), None),
        P(("rep", "fsdp"), None),
        P(("rep", "fsdp")),
        P(("rep", "fsdp"), None),
        P(("rep", "fsdp"), None),
        P("fsdp", None),
        P("fsdp"),
        P("fsdp", None),
        P("fsdp", None),
        P("fsdp", None),
        P("fsdp"),
        P("fsdp", None),
        P("fsdp", None),
        P(("rep", "fsdp"), None),
        P(("rep", "fsdp"), None),
    )
    out_specs = (
        P(("rep", "fsdp"), None),
        P(("rep", "fsdp"), None),
        P(("rep", "fsdp"), None),
        P(("rep", "fsdp"), None),
        P("fsdp", None),
        P("fsdp"),
        P("fsdp", None),
        P("fsdp", None),
        P("fsdp", None),
        P("fsdp"),
        P("fsdp", None),
        P("fsdp", None),
    )
    small = mesh.shape["fsdp"] == 8 and mesh.shape["rep"] == 4
    return jax.shard_map(
        per_device if small else per_device_any, mesh=mesh, in_specs=in_specs, out_specs=out_specs, check_vma=False
    )
```

```python
import functools

import jax
import jax.numpy as jnp
from jax import lax
from jax.experimental import pallas as pl
from jax.experimental.pallas import tpu as pltpu
from jax.sharding import PartitionSpec as P

HEAD = 64
PAIR = 2 * HEAD
ROW_TILE = 16
VMEM_BYTES = 56 * 1024 * 1024
SMALL_VMEM_BYTES = 20 * 1024 * 1024
MIDDLE_VMEM_BYTES = 44 * 1024 * 1024
MIDDLE = ('enc_attn', 'dec_self', 'cross_back', 'enc_back_out', 'self_back')
ANY = pl.BlockSpec(memory_space=pl.ANY)
SMEM = pl.BlockSpec(memory_space=pltpu.SMEM)
VMEM = pl.BlockSpec(memory_space=pltpu.VMEM)


EPSILON = 1e-05
NEG_FILL = -1e30
SCORE_SCALE = 0.125


def norm_rows(hidden, gain_row, shift_row):
    row_mean = jnp.mean(hidden, axis=-1, keepdims=True)
    centred = hidden - row_mean
    variance = jnp.mean(centred * centred, axis=-1, keepdims=True)
    return centred * lax.rsqrt(variance + EPSILON) * gain_row + shift_row


def norm_back(hidden, gain_row, shift_row, gradient):
    unused, pullback = jax.vjp(norm_rows, hidden, gain_row, shift_row)
    return pullback(gradient)


def gelu_exact(hidden):
    return jax.nn.gelu(hidden, approximate=False)


def dot_plain(first_op, second_op):
    return jnp.dot(first_op, second_op, preferred_element_type=jnp.float32)


def dot_left(first_op, second_op):
    return lax.dot_general(
        first_op, second_op, (((0,), (0,)), ((), ())), preferred_element_type=jnp.float32
    )


def dot_right(first_op, second_op):
    return lax.dot_general(
        first_op, second_op, (((1,), (1,)), ((), ())), preferred_element_type=jnp.float32
    )


def build_masks(one_long, enc_len, dec_len, row_total, seg_count):
    span_rows = jnp.where(one_long == 1, row_total, row_total // seg_count).astype(jnp.int32)
    row_index = jnp.arange(row_total, dtype=jnp.int32)
    group_id = row_index // span_rows
    row_place = row_index - group_id * span_rows
    in_group = group_id[:, None] == jnp.arange(seg_count, dtype=jnp.int32)[None, :]
    enc_live = row_place < jnp.sum(jnp.where(in_group, enc_len[None, :], 0), axis=1)
    dec_live = row_place < jnp.sum(jnp.where(in_group, dec_len[None, :], 0), axis=1)
    same_group = group_id[:, None] == group_id[None, :]
    enc_mask = same_group & enc_live[None, :]
    self_mask = same_group & dec_live[None, :] & (row_index[None, :] <= row_index[:, None])
    return (enc_mask, self_mask, enc_mask)


def unpack(vector, row_count, feature):
    rows_part = vector[: row_count * feature].astype(jnp.float32).reshape(row_count, feature)
    return (rows_part, vector[row_count * feature :].astype(jnp.float32))


def fetch(attn_rows, vec_part, w_in, w_out):
    return (
        lax.all_gather(attn_rows, "fsdp", axis=0, tiled=True),
        lax.all_gather(vec_part, "fsdp", axis=0, tiled=True),
        lax.all_gather(w_in, "fsdp", axis=0, tiled=True),
        lax.all_gather(w_out, "fsdp", axis=0, tiled=True),
    )


def fetch_again(attn_rows, vec_part, w_in, w_out):
    return (
        lax.all_gather(attn_rows, "fsdp", axis=0, tiled=True),
        lax.all_gather(vec_part, "fsdp", axis=0, tiled=True),
        lax.all_gather(w_in, "fsdp", axis=0, tiled=True),
        lax.all_gather(w_out, "fsdp", axis=0, tiled=True),
    )


def reduce_grads(grad_attn, grad_vec, grad_in, grad_out):
    shard = (
        lax.psum_scatter(
            grad_attn.astype(jnp.bfloat16), "fsdp", scatter_dimension=0, tiled=True
        ).astype(jnp.float32),
        lax.psum_scatter(
            grad_vec.astype(jnp.bfloat16), "fsdp", scatter_dimension=0, tiled=True
        ).astype(jnp.float32),
        lax.psum_scatter(
            grad_in.astype(jnp.bfloat16), "fsdp", scatter_dimension=0, tiled=True
        ).astype(jnp.float32),
        lax.psum_scatter(
            grad_out.astype(jnp.bfloat16), "fsdp", scatter_dimension=0, tiled=True
        ).astype(jnp.float32),
    )
    return (
        lax.psum(shard[0].astype(jnp.bfloat16), "rep").astype(jnp.float32),
        lax.psum(shard[1].astype(jnp.bfloat16), "rep").astype(jnp.float32),
        lax.psum(shard[2].astype(jnp.bfloat16), "rep").astype(jnp.float32),
        lax.psum(shard[3].astype(jnp.bfloat16), "rep").astype(jnp.float32),
    )


def attend(q_in, kv_in, weights, biases, key_mask, one_source):
    row_total, feature = q_in.shape
    head_count = feature // HEAD
    if one_source:
        packed = dot_plain(q_in, weights[:, : 3 * feature])
        q_pre = packed[:, :feature]
        k_pre = packed[:, feature : 2 * feature]
        v_pre = packed[:, 2 * feature :]
    else:
        q_pre = dot_plain(q_in, weights[:, :feature])
        packed = dot_plain(kv_in, weights[:, feature : 3 * feature])
        k_pre = packed[:, :feature]
        v_pre = packed[:, feature:]
    queries = (q_pre + biases[0]).astype(jnp.bfloat16).reshape(row_total, head_count, HEAD)
    keys_low = k_pre.astype(jnp.bfloat16).reshape(row_total, head_count, HEAD)
    values = (v_pre + biases[1]).astype(jnp.bfloat16).reshape(row_total, head_count, HEAD)
    raw_score = jnp.einsum("qhd,khd->hqk", queries, keys_low, preferred_element_type=jnp.float32)
    probs = jax.nn.softmax(jnp.where(key_mask[None], raw_score * SCORE_SCALE, NEG_FILL), axis=-1)
    probs_low = probs.astype(jnp.bfloat16)
    mixed = jnp.einsum("hqk,khd->qhd", probs_low, values, preferred_element_type=jnp.float32)
    mixed = mixed.reshape(row_total, feature).astype(jnp.bfloat16)
    branch = dot_plain(mixed, weights[:, 3 * feature :]) + biases[2]
    return (branch, (queries, keys_low, values, probs, probs_low, mixed))


def attend_back(gradient, q_in, kv_in, weights, saved, one_source):
    queries, keys_low, values, probs, probs_low, mixed = saved
    row_total, feature = q_in.shape
    head_count = feature // HEAD
    grad_bias_o = jnp.sum(gradient, axis=0)
    grad_low = gradient.astype(jnp.bfloat16)
    grad_w_o = dot_left(mixed, grad_low)
    grad_mixed = dot_right(grad_low, weights[:, 3 * feature :]).astype(jnp.bfloat16)
    grad_mixed = grad_mixed.reshape(row_total, head_count, HEAD)
    grad_probs = jnp.einsum("qhd,khd->hqk", grad_mixed, values, preferred_element_type=jnp.float32)
    grad_values = jnp.einsum(
        "hqk,qhd->khd", probs_low, grad_mixed, preferred_element_type=jnp.float32
    )
    grad_score = probs * (grad_probs - jnp.sum(grad_probs * probs, axis=-1, keepdims=True))
    grad_raw = (grad_score * SCORE_SCALE).astype(jnp.bfloat16)
    grad_query = jnp.einsum(
        "hqk,khd->qhd", grad_raw, keys_low, preferred_element_type=jnp.float32
    ).reshape(row_total, feature)
    grad_keys = jnp.einsum(
        "hqk,qhd->khd", grad_raw, queries, preferred_element_type=jnp.float32
    ).reshape(row_total, feature)
    grad_values = grad_values.reshape(row_total, feature)
    grad_bias_q = jnp.sum(grad_query, axis=0)
    grad_bias_v = jnp.sum(grad_values, axis=0)
    low_query = grad_query.astype(jnp.bfloat16)
    low_kv = jnp.concatenate(
        [grad_keys.astype(jnp.bfloat16), grad_values.astype(jnp.bfloat16)], axis=1
    )
    if one_source:
        packed = jnp.concatenate([low_query, low_kv], axis=1)
        grad_weights = jnp.concatenate([dot_left(q_in, packed), grad_w_o], axis=1)
        grad_q_in = dot_right(packed, weights[:, : 3 * feature])
        grad_kv_in = grad_q_in
    else:
        grad_weights = jnp.concatenate(
            [dot_left(q_in, low_query), dot_left(kv_in, low_kv), grad_w_o], axis=1
        )
        grad_q_in = dot_right(low_query, weights[:, :feature])
        grad_kv_in = dot_right(low_kv, weights[:, feature : 3 * feature])
    return (grad_q_in, grad_kv_in, grad_weights, (grad_bias_q, grad_bias_v, grad_bias_o))


def feed(rows_in, w_in, b_in, w_out, b_out):
    hidden = dot_plain(rows_in, w_in) + b_in
    active = gelu_exact(hidden).astype(jnp.bfloat16)
    return (dot_plain(active, w_out) + b_out, (hidden, active))


def feed_back(gradient, rows_in, w_in, w_out, saved):
    hidden, active = saved
    grad_b_out = jnp.sum(gradient, axis=0)
    grad_low = gradient.astype(jnp.bfloat16)
    grad_w_out = dot_left(active, grad_low)
    grad_active = dot_right(grad_low, w_out)
    unused, pullback = jax.vjp(gelu_exact, hidden)
    grad_hidden = pullback(grad_active)[0]
    grad_b_in = jnp.sum(grad_hidden, axis=0)
    hidden_low = grad_hidden.astype(jnp.bfloat16)
    grad_w_in = dot_left(rows_in, hidden_low)
    grad_rows = dot_right(hidden_low, w_in)
    return (grad_rows, grad_w_in, grad_b_in, grad_w_out, grad_b_out)


def per_device_any(
    enc_in,
    dec_in,
    bucket,
    enc_lengths,
    dec_lengths,
    enc_attn,
    enc_vec,
    enc_w1,
    enc_w2,
    dec_attn,
    dec_vec,
    dec_w1,
    dec_w2,
    enc_cot,
    dec_cot,
):
    row_total, feature = enc_in.shape
    enc_mask, self_mask, cross_mask = build_masks(
        bucket[0], enc_lengths[0], dec_lengths[0], row_total, enc_lengths.shape[1]
    )
    enc_weights = fetch(enc_attn, enc_vec, enc_w1, enc_w2)
    e_attn, e_vec, e_in, e_out = enc_weights
    e_rows, e_tail = unpack(e_vec, 8, feature)
    branch, e_saved_a = attend(enc_in, enc_in, e_attn, e_rows[0:3], enc_mask, True)
    e_hid_a = enc_in.astype(jnp.float32) + branch
    e_first = norm_rows(e_hid_a, e_rows[3], e_rows[4]).astype(jnp.bfloat16)
    branch, e_saved_f = feed(e_first, e_in, e_tail, e_out, e_rows[5])
    e_hid_f = e_first.astype(jnp.float32) + branch
    encoded = norm_rows(e_hid_f, e_rows[6], e_rows[7]).astype(jnp.bfloat16)
    dec_weights = fetch(dec_attn, dec_vec, dec_w1, dec_w2)
    d_attn, d_vec, d_in, d_out = dec_weights
    d_rows, d_tail = unpack(d_vec, 13, feature)
    branch, d_saved_s = attend(
        dec_in, dec_in, d_attn[:, : 4 * feature], d_rows[0:3], self_mask, True
    )
    d_hid_s = dec_in.astype(jnp.float32) + branch
    d_first = norm_rows(d_hid_s, d_rows[3], d_rows[4]).astype(jnp.bfloat16)
    branch, d_saved_c = attend(
        d_first, encoded, d_attn[:, 4 * feature :], d_rows[5:8], cross_mask, False
    )
    d_hid_c = d_first.astype(jnp.float32) + branch
    d_second = norm_rows(d_hid_c, d_rows[8], d_rows[9]).astype(jnp.bfloat16)
    branch, d_saved_f = feed(d_second, d_in, d_tail, d_out, d_rows[10])
    d_hid_f = d_second.astype(jnp.float32) + branch
    decoded = norm_rows(d_hid_f, d_rows[11], d_rows[12]).astype(jnp.bfloat16)
    dec_weights = fetch_again(dec_attn, dec_vec, dec_w1, dec_w2)
    d_attn, d_vec, d_in, d_out = dec_weights
    d_rows, d_tail = unpack(d_vec, 13, feature)
    gradient, grad_g11, grad_n12 = norm_back(
        d_hid_f, d_rows[11], d_rows[12], dec_cot.astype(jnp.float32)
    )
    grad_rows, grad_d_in, grad_d_tail, grad_d_out, grad_b10 = feed_back(
        gradient, d_second, d_in, d_out, d_saved_f
    )
    gradient, grad_g8, grad_n9 = norm_back(d_hid_c, d_rows[8], d_rows[9], gradient + grad_rows)
    grad_q_in, grad_encoded, grad_cross, cross_bias = attend_back(
        gradient, d_first, encoded, d_attn[:, 4 * feature :], d_saved_c, False
    )
    gradient, grad_g3, grad_n4 = norm_back(d_hid_s, d_rows[3], d_rows[4], gradient + grad_q_in)
    grad_self_in, unused, grad_self, self_bias = attend_back(
        gradient, dec_in, dec_in, d_attn[:, : 4 * feature], d_saved_s, True
    )
    dec_in_grad = gradient + grad_self_in
    dec_stack = jnp.stack(
        [
            self_bias[0],
            self_bias[1],
            self_bias[2],
            grad_g3,
            grad_n4,
            cross_bias[0],
            cross_bias[1],
            cross_bias[2],
            grad_g8,
            grad_n9,
            grad_b10,
            grad_g11,
            grad_n12,
        ]
    )
    dec_vec_full = jnp.concatenate([dec_stack.reshape(-1), grad_d_tail])
    dec_shards = reduce_grads(
        jnp.concatenate([grad_self, grad_cross], axis=1), dec_vec_full, grad_d_in, grad_d_out
    )
    enc_weights = fetch_again(enc_attn, enc_vec, enc_w1, enc_w2)
    e_attn, e_vec, e_in, e_out = enc_weights
    e_rows, e_tail = unpack(e_vec, 8, feature)
    gradient, grad_g6, grad_n7 = norm_back(
        e_hid_f, e_rows[6], e_rows[7], enc_cot.astype(jnp.float32) + grad_encoded
    )
    grad_rows, grad_e_in, grad_e_tail, grad_e_out, grad_b5 = feed_back(
        gradient, e_first, e_in, e_out, e_saved_f
    )
    gradient, grad_g3e, grad_n4e = norm_back(e_hid_a, e_rows[3], e_rows[4], gradient + grad_rows)
    grad_self_in, unused, grad_e_attn, enc_bias = attend_back(
        gradient, enc_in, enc_in, e_attn, e_saved_a, True
    )
    enc_in_grad = gradient + grad_self_in
    enc_stack = jnp.stack(
        [enc_bias[0], enc_bias[1], enc_bias[2], grad_g3e, grad_n4e, grad_b5, grad_g6, grad_n7]
    )
    enc_vec_full = jnp.concatenate([enc_stack.reshape(-1), grad_e_tail])
    enc_shards = reduce_grads(grad_e_attn, enc_vec_full, grad_e_in, grad_e_out)
    return (
        encoded,
        decoded,
        enc_in_grad,
        dec_in_grad,
        enc_shards[0],
        enc_shards[1],
        enc_shards[2],
        enc_shards[3],
        dec_shards[0],
        dec_shards[1],
        dec_shards[2],
        dec_shards[3],
    )


def swap(value, bit):
    return lax.ppermute(value, "fsdp", [(i, i ^ bit) for i in range(8)])


def add_low(*terms):
    total = terms[0].astype(jnp.float32)
    for term in terms[1:]:
        total = total + term.astype(jnp.float32)
    return total.astype(jnp.bfloat16)


def tile_up(rows):
    return -(-rows // ROW_TILE) * ROW_TILE


def size_of(shape):
    total = 1
    for extent in shape:
        total *= extent
    return total


class Order:
    def __init__(self):
        self.token = None
        self.waits = []

    def mark(self, *values):
        self.waits += values

    def tie(self, value):
        if self.token is None:
            return value
        value, self.token = lax.optimization_barrier((value, self.token))
        return value

    def kernel(self, body, operands, specs, outs, scratch, name, flops=0, moved=0):
        extra = self.waits + ([] if self.token is None else [self.token])
        self.waits = []
        count, skip = len(operands), len(extra)
        grant = SMALL_VMEM_BYTES if not flops else MIDDLE_VMEM_BYTES if name in MIDDLE else VMEM_BYTES
        results = pl.pallas_call(
            lambda *refs: body(*refs[:count], *refs[count + skip :]),
            out_shape=[jax.ShapeDtypeStruct(shape, dtype) for shape, dtype, spec in outs],
            in_specs=list(specs) + [ANY] * skip,
            out_specs=[spec for shape, dtype, spec in outs],
            scratch_shapes=scratch,
            compiler_params=pltpu.CompilerParams(
                vmem_limit_bytes=grant
            ),
            cost_estimate=pl.CostEstimate(flops=flops, bytes_accessed=moved, transcendentals=0),
            name=name,
        )(*operands, *extra)
        self.token = min(results, key=lambda result: result.size)
        return results


def pack_body(count, *refs):
    shards, out = refs[:count], refs[-1]
    feature = out.shape[1]
    offset = 0
    for shard in shards:
        rows, columns = shard.shape
        for block in range(columns // feature):
            out[offset : offset + rows, :] = shard[:, block * feature : (block + 1) * feature]
            offset += rows


def split_body(cut, from_x, from_y, top, lower):
    top[...] = from_x[:cut, :]
    lower[...] = from_y[cut:, :]


def vec_rows(vec_part, feature):
    rows = tile_up(-(-vec_part.shape[0] // feature))
    padded = jnp.pad(vec_part, (0, rows * feature - vec_part.shape[0]))
    return padded.reshape(rows, feature)


class Gather:
    def __init__(self, order, feature, name):
        self.order = order
        self.feature = feature
        self.name = name
        self.mine = []

    def sides(self, *shards):
        feature = self.feature
        rows = sum(shard.size for shard in shards) // feature
        (packed,) = self.order.kernel(
            functools.partial(pack_body, len(shards)),
            shards,
            [VMEM] * len(shards),
            [((rows, feature), jnp.bfloat16, VMEM)],
            [],
            self.name + "_pack",
            moved=4 * rows * feature,
        )
        self.mine = [packed, swap(packed, 2), swap(packed, 4)]

    def corners(self):
        rows, feature = self.mine[0].shape
        cut = rows // (2 * ROW_TILE) * ROW_TILE
        top, lower = self.order.kernel(
            functools.partial(split_body, cut),
            self.mine[1:3],
            [VMEM] * 2,
            [
                ((cut, feature), jnp.bfloat16, VMEM),
                ((rows - cut, feature), jnp.bfloat16, VMEM),
            ],
            [],
            self.name + "_split",
            moved=4 * rows * feature,
        )
        self.mine += [swap(top, 4), swap(lower, 2)]

    def join(self, *parts):
        rows, feature = self.mine[0].shape
        joined = self.order.kernel(
            functools.partial(join_body, parts),
            self.mine,
            [ANY] * 5,
            [((4 * count, feature), jnp.bfloat16, ANY) for first, count in parts],
            [pltpu.VMEM((4 * rows, feature), jnp.bfloat16), pltpu.SemaphoreType.DMA((5 + 4 * len(parts),))],
            self.name + "_join",
        )
        return [(part, swap(part, 1)) for part in joined]


def join_body(parts, own, from_x, from_y, top, lower, *refs):
    outs, stage, sems = refs[:-2], refs[-2], refs[-1]
    copies = []
    place = 0
    for index, source in enumerate((own, from_x, from_y, top, lower)):
        rows = source.shape[0]
        copy = pltpu.make_async_copy(source, stage.at[pl.ds(place, rows), :], sems.at[index])
        copy.start()
        copies.append(copy)
        place += rows
    block = own.shape[0]
    stores = []
    for chip in range(4):
        wait_all(copies[chip : chip + 1] if chip < 3 else copies[3:])
        for (first, count), out in zip(parts, outs):
            copy = pltpu.make_async_copy(
                stage.at[pl.ds(chip * block + first, count), :],
                out.at[pl.ds(chip * count, count), :],
                sems.at[5 + len(stores)],
            )
            copy.start()
            stores.append(copy)
    wait_all(stores)


LANES = 128


def chunk_count(length):
    return max(-(-((place * length) % LANES + length) // LANES) for place in range(8))


def vec_shards(vectors, chip_index, feature):
    parts = []
    for vector in vectors:
        length = vector.shape[0]
        blank = jnp.zeros((chunk_count(length) * LANES,), vector.dtype)
        parts.append(lax.dynamic_update_slice(blank, vector, ((chip_index * length) % LANES,)))
    return vec_rows(jnp.concatenate(parts), feature)


def vec_body(lengths, sections, table, mine, theirs, *refs):
    outs, landed, wide, sems = refs[:-3], refs[-3], refs[-2], refs[-1]
    rows = landed.shape[0] // 8
    feature = landed.shape[1]
    block = mine.shape[0] // 4
    copies = []
    for chip in range(4):
        for core, source in enumerate((mine, theirs)):
            copies.append(
                pltpu.make_async_copy(
                    source.at[pl.ds((chip + 1) * block - rows, rows), :],
                    landed.at[pl.ds(pl.multiple_of(table[2 * chip + core] * rows, ROW_TILE), rows), :],
                    sems.at[len(copies)],
                )
            )
    for copy in copies:
        copy.start()
    wait_all(copies)
    wide[...] = landed[...].astype(jnp.float32)
    per_row = feature // LANES
    outs = list(outs)
    skip = 0
    for length, section in zip(lengths, sections):
        targets = []
        for count in section:
            out = outs.pop(0)
            targets += [(out, row, lane * LANES) for row in range(count) for lane in range(per_row)]
        out = outs.pop(0)
        targets += [(out, 0, lane * LANES) for lane in range(out.shape[1] // LANES)]
        filled = set()
        for place in range(8):
            base = place * length // LANES
            used = -(-((place * length) % LANES + length) // LANES)
            for chunk in range(used):
                flat = (skip + chunk) * LANES
                row, lane = place * rows + flat // feature, flat % feature
                value = wide[row : row + 1, lane : lane + LANES]
                out, row, lane = targets[base + chunk]
                if base + chunk in filled:
                    value = value + out[row : row + 1, lane : lane + LANES]
                out[row : row + 1, lane : lane + LANES] = value
                filled.add(base + chunk)
        skip += chunk_count(length)


def gathered_vecs(order, buffers, table, rows, feature, lengths, sections):
    outs = []
    for length, section in zip(lengths, sections):
        outs += [((count, feature), jnp.float32, VMEM) for count in section]
        outs.append(((1, 8 * length - sum(section) * feature), jnp.float32, VMEM))
    return order.kernel(
        functools.partial(vec_body, lengths, sections),
        [table, *buffers],
        [SMEM] + [ANY] * 2,
        outs,
        [
            pltpu.VMEM((8 * rows, feature), jnp.bfloat16),
            pltpu.VMEM((8 * rows, feature), jnp.float32),
            pltpu.SemaphoreType.DMA((8,)),
        ],
        "vectors",
    )


class Loader:
    def __init__(self, buffers, table, sems, used=0):
        self.buffers = buffers
        self.block = buffers[0].shape[0] // 4
        self.table = table
        self.sems = sems
        self.used = used

    def unit(self, number, target, stride, first):
        rows = target.shape[1] // 8
        copies = []
        for chip in range(4):
            for core in range(2):
                offset = chip * self.block + number * rows
                place = pl.multiple_of(self.table[2 * chip + core] * stride + first, ROW_TILE)
                copy = pltpu.make_async_copy(
                    self.buffers[core].at[pl.ds(offset, rows), :],
                    target.at[pl.ds(place, rows), :],
                    self.sems.at[self.used],
                )
                copy.start()
                self.used += 1
                copies.append(copy)
        return copies

    def wide(self, number, target):
        return self.unit(number, target, target.shape[1] // 8, 0)

    def tall(self, number, target):
        rows = target.shape[1] // 8
        copies = []
        for block in range(4):
            copies += self.unit(number + block, target, 4 * rows, block * rows)
        return copies


def wait_all(copies):
    for copy in copies:
        copy.wait()


class Storer:
    def __init__(self, outs, table, slots, sems):
        self.keep, self.upper, self.lower = outs if len(outs) == 3 else (outs[0], None, outs[1])
        self.table = table
        self.slots = slots
        self.block = self.keep.shape[1] // 2
        self.sems = sems
        self.copies = []

    def add(self, source, out, row):
        copy = pltpu.make_async_copy(
            source, out.at[pl.ds(row, source.shape[0]), :], self.sems.at[len(self.copies)]
        )
        copy.start()
        self.copies.append(copy)

    def rows(self, source, stride, count, offset):
        for core in (1, 0):
            for slot in (2, 3, 0, 1):
                place = self.table[2 * self.slots[slot] + core] * stride
                block = source.at[pl.ds(pl.multiple_of(place, ROW_TILE), count), :]
                if core == 0:
                    self.add(block, self.keep, slot * self.block + offset)
                elif slot < 2 or self.upper is None:
                    self.add(block, self.lower, slot * self.block + offset)
                else:
                    self.add(block, self.upper, (slot - 2) * self.block + offset)

    def tail(self, source):
        self.add(source, self.lower, (4 if self.upper is None else 2) * self.block)
        self.add(source, self.keep, 4 * self.block)

    def finish(self):
        wait_all(self.copies)


def gradient_outs(feature, extra=0, single=False):
    rows = feature // 2
    if single:
        return [((4 * rows + extra, feature), jnp.bfloat16, ANY)] * 2
    return [((count, feature), jnp.bfloat16, ANY) for count in (4 * rows + extra, 2 * rows, 2 * rows + extra)]


def low(value):
    return value.astype(jnp.bfloat16)


def layer_norm(hidden, gain, shift):
    mean = jnp.mean(hidden, axis=-1, keepdims=True)
    centred = hidden - mean
    variance = jnp.mean(centred * centred, axis=-1, keepdims=True)
    return centred * lax.rsqrt(variance + EPSILON) * gain + shift


def layer_norm_back(hidden, gain, gradient):
    mean = jnp.mean(hidden, axis=-1, keepdims=True)
    centred = hidden - mean
    variance = jnp.mean(centred * centred, axis=-1, keepdims=True)
    scale = lax.rsqrt(variance + EPSILON)
    unit = centred * scale
    grad_gain = jnp.sum(gradient * unit, axis=0, keepdims=True)
    grad_shift = jnp.sum(gradient, axis=0, keepdims=True)
    inner = gradient * gain
    mean_inner = jnp.mean(inner, axis=-1, keepdims=True)
    mean_unit = jnp.mean(inner * unit, axis=-1, keepdims=True)
    return (scale * (inner - mean_inner - unit * mean_unit), grad_gain, grad_shift)


def key_mask(bucket, lengths, rows, segs, causal):
    span = rows // segs
    one_long = bucket[0] == 1
    query = lax.broadcasted_iota(jnp.int32, (rows, rows), 0)
    key = lax.broadcasted_iota(jnp.int32, (rows, rows), 1)
    key_row = lax.broadcasted_iota(jnp.int32, (1, rows), 1)
    limit = jnp.zeros((1, rows), jnp.int32)
    start = jnp.zeros((1, rows), jnp.int32)
    first = jnp.zeros((rows, 1), jnp.int32)
    query_col = lax.broadcasted_iota(jnp.int32, (rows, 1), 0)
    for seg in range(segs):
        inside = (key_row >= seg * span) & (key_row < (seg + 1) * span)
        limit = jnp.where(inside, seg * span + lengths[0, seg], limit)
        start = jnp.where(inside, seg * span, start)
        first = jnp.where((query_col >= seg * span) & (query_col < (seg + 1) * span), seg * span, first)
    limit = jnp.where(one_long, lengths[0, 0], limit)
    start = jnp.where(one_long, 0, start)
    first = jnp.where(one_long, 0, first)
    mask = (first == start) & (key < limit)
    if causal:
        mask = mask & (key <= query)
    return mask


def head_lanes(rows):
    return lax.broadcasted_iota(jnp.int32, (rows, PAIR), 1) < HEAD


def attn_body(
    cross, causal, first_unit, segs, table, bucket, lengths, *refs
):
    refs = list(refs)
    q_in = refs.pop(0)
    kv_in = refs.pop(0) if cross else q_in
    vec = refs.pop(0)
    buffers = [refs.pop(0) for _ in range(2)]
    hidden_out, norm_out, q_out, k_out, v_out, o_out, p_out = refs[:7]
    w_q, w_k, w_v, w_o, sems = refs[7:]
    rows, feature = q_in.shape
    load = Loader(buffers, table, sems)
    waits = [load.wide(first_unit + i, w) for i, w in enumerate((w_q, w_k, w_v, w_o))]
    mask = key_mask(bucket, lengths, rows, segs, causal)
    lanes = head_lanes(rows)
    wait_all(waits[0])
    q_out[...] = low(dot_plain(q_in[...], w_q[...]) + vec[0:1, :])
    wait_all(waits[1])
    k_out[...] = low(dot_plain(kv_in[...], w_k[...]))
    wait_all(waits[2])
    v_out[...] = low(dot_plain(kv_in[...], w_v[...]) + vec[1:2, :])
    for pair in range(feature // PAIR):
        columns = slice(pair * PAIR, (pair + 1) * PAIR)
        q_pair, k_pair, v_pair = q_out[:, columns], k_out[:, columns], v_out[:, columns]
        mixed = []
        for half in range(2):
            mine = lanes if half == 0 else ~lanes
            score = dot_right(jnp.where(mine, q_pair, jnp.zeros_like(q_pair)), k_pair)
            score = jnp.where(mask, score * SCORE_SCALE, NEG_FILL)
            power = jnp.exp(score - jnp.max(score, axis=-1, keepdims=True))
            probs = low(power / jnp.sum(power, axis=-1, keepdims=True))
            p_out[2 * pair + half] = probs
            mixed.append(dot_plain(probs, v_pair))
        o_out[:, columns] = low(jnp.where(lanes, mixed[0], mixed[1]))
    wait_all(waits[3])
    hidden = q_in[...].astype(jnp.float32) + (dot_plain(o_out[...], w_o[...]) + vec[2:3, :])
    hidden_out[...] = hidden
    norm_out[...] = low(layer_norm(hidden, vec[3:4, :], vec[4:5, :]))


def attn_forward(order, q_in, kv_in, vec, weights, ids, lengths, causal, name):
    rows, feature = q_in.shape
    sources = [q_in] + ([] if kv_in is None else [kv_in]) + [vec]
    wide = ((rows, feature), jnp.bfloat16, VMEM)
    return order.kernel(
        functools.partial(attn_body, kv_in is not None, causal, weights[1], lengths.shape[1]),
        [*ids, lengths, *sources, *weights[0]],
        [SMEM] * 3 + [VMEM] * len(sources) + [ANY] * 2,
        [((rows, feature), jnp.float32, VMEM)]
        + [wide] * 5
        + [((feature // HEAD, rows, rows), jnp.bfloat16, VMEM)],
        [pltpu.VMEM((feature, feature), jnp.bfloat16)] * 4 + [pltpu.SemaphoreType.DMA((32,))],
        name,
        8 * rows * feature * feature,
        10 * feature * feature,
    )


def gelu_parts(hidden):
    phi = 0.5 * (1.0 + lax.erf(hidden * 0.7071067811865476))
    slope = phi + hidden * (0.3989422804014327 * jnp.exp(-0.5 * hidden * hidden))
    return (hidden * phi, slope)


def feed_body(units, table, rows_in, vec, b_in, *refs):
    hidden_out, norm_out, r_out, slope_out, w_in, w_out, sems = refs[4:]
    feature = rows_in.shape[1]
    load = Loader(refs[:2], table, sems)
    waits = [load.wide(units[0] + j, w_in.at[j]) for j in range(4)]
    tail = Loader(refs[2:4], table, sems, load.used).tall(units[1], w_out)
    total = None
    for j in range(4):
        columns = slice(j * feature, (j + 1) * feature)
        wait_all(waits[j])
        hidden = dot_plain(rows_in[...], w_in[j]) + b_in[:, columns]
        active, slope = gelu_parts(hidden)
        r_out[:, columns] = low(active)
        slope_out[:, columns] = low(slope)
    wait_all(tail)
    total = dot_plain(r_out[...], w_out[...]) + vec[0:1, :]
    hidden = rows_in[...].astype(jnp.float32) + total
    hidden_out[...] = hidden
    norm_out[...] = low(layer_norm(hidden, vec[1:2, :], vec[2:3, :]))


def feed_forward(order, rows_in, vec, b_in, w_in, w_out, table, name):
    rows, feature = rows_in.shape
    width = b_in.shape[1]
    return order.kernel(
        functools.partial(feed_body, (w_in[1], w_out[1])),
        [table, rows_in, vec, b_in, *w_in[0], *w_out[0]],
        [SMEM] + [VMEM] * 3 + [ANY] * 4,
        [
            ((rows, feature), jnp.float32, VMEM),
            ((rows, feature), jnp.bfloat16, VMEM),
            ((rows, width), jnp.bfloat16, VMEM),
            ((rows, width), jnp.bfloat16, VMEM),
        ],
        [
            pltpu.VMEM((4, feature, feature), jnp.bfloat16),
            pltpu.VMEM((width, feature), jnp.bfloat16),
            pltpu.SemaphoreType.DMA((64,)),
        ],
        name,
        4 * rows * feature * width,
        8 * feature * width,
    )


def feed_back_out_body(extra, slots, table, *refs):
    refs = list(refs)
    gradient = refs.pop(0)[...].astype(jnp.float32)
    if extra:
        gradient = gradient + refs.pop(0)[...].astype(jnp.float32)
    hidden, gain, active, g_out, sums, keep, upper, lower, stage, out_sems = refs
    feature = hidden.shape[1]
    store = Storer((keep, upper, lower), table, slots, out_sems)
    gradient, grad_gain, grad_shift = layer_norm_back(hidden[...], gain[1:2, :], gradient)
    sums[0:1, :] = jnp.sum(gradient, axis=0, keepdims=True)
    sums[1:2, :] = grad_gain
    sums[2:3, :] = grad_shift
    g_out[...] = gradient
    grad_low = low(gradient)
    for j in range(4):
        columns = slice(j * feature, (j + 1) * feature)
        stage[columns, :] = low(dot_left(active[:, columns], grad_low))
    store.rows(stage, feature // 2, feature // 2, 0)
    store.finish()


def feed_back_out(order, gradients, hidden, gain, active, table, slots, name):
    rows, feature = hidden.shape
    width = active.shape[1]
    return order.kernel(
        functools.partial(feed_back_out_body, len(gradients) == 2, slots),
        [table, *gradients, hidden, gain, active],
        [SMEM] + [VMEM] * (len(gradients) + 3),
        [((rows, feature), jnp.float32, VMEM), ((3, feature), jnp.float32, VMEM), *gradient_outs(feature)],
        [pltpu.VMEM((width, feature), jnp.bfloat16), pltpu.SemaphoreType.DMA((8,))],
        name,
        2 * rows * feature * width,
        4 * feature * width,
    )


def feed_back_in_body(slots, units, table, gradient, slope, rows_in, *refs):
    total_out, bias_in, keep, upper, lower, w_in, w_out, grad_hidden, stage, sems, out_sems = refs[4:]
    feature = rows_in.shape[1]
    tail = Loader(refs[2:4], table, sems).tall(units[1], w_out)
    load = Loader(refs[:2], table, sems, len(tail))
    waits = [load.wide(units[0] + j, w_in.at[j]) for j in range(4)]
    store = Storer((keep, upper, lower), table, slots, out_sems)
    total = gradient[...]
    grad_low = low(total)
    wait_all(tail)
    for j in range(4):
        columns = slice(j * feature, (j + 1) * feature)
        hidden = dot_right(grad_low, w_out[columns, :]) * slope[:, columns].astype(jnp.float32)
        bias_in[j : j + 1, :] = jnp.sum(hidden, axis=0, keepdims=True)
        grad_hidden[:, columns] = low(hidden)
        stage[j] = low(dot_left(rows_in[...], grad_hidden[:, columns]))
        store.rows(stage.at[j], feature // 8, feature // 8, j * (feature // 8))
    for j in range(4):
        columns = slice(j * feature, (j + 1) * feature)
        wait_all(waits[j])
        total = total + dot_right(grad_hidden[:, columns], w_in[j])
    total_out[...] = total
    store.finish()


def feed_back_in(order, gradient, slope, rows_in, w_in, w_out, table, slots, name):
    rows, feature = rows_in.shape
    width = slope.shape[1]
    square = pltpu.VMEM((4, feature, feature), jnp.bfloat16)
    return order.kernel(
        functools.partial(feed_back_in_body, slots, (w_in[1], w_out[1])),
        [table, gradient, slope, rows_in, *w_in[0], *w_out[0]],
        [SMEM] + [VMEM] * 3 + [ANY] * 4,
        [((rows, feature), jnp.float32, VMEM), ((4, feature), jnp.float32, VMEM), *gradient_outs(feature)],
        [
            square,
            pltpu.VMEM((width, feature), jnp.bfloat16),
            pltpu.VMEM((rows, width), jnp.bfloat16),
            square,
            pltpu.SemaphoreType.DMA((64,)),
            pltpu.SemaphoreType.DMA((32,)),
        ],
        name,
        6 * rows * feature * width,
        6 * feature * width,
    )


def attn_back_body(cross, first_unit, others, slots, out_count, table, gradient, *refs):
    refs = list(refs)
    other_sums = [refs.pop(0) for _ in range(others)]
    hidden, gain, q_in = refs[:3]
    refs = refs[3:]
    kv_in = refs.pop(0) if cross else q_in
    queries, keys, values, mixed, probs_in = refs[:5]
    buffers = refs[5:7]
    refs = refs[7:]
    q_grad_out = refs.pop(0)
    kv_grad_out = refs.pop(0) if cross else None
    sums = refs.pop(0)
    grads = [refs.pop(0) for _ in range(out_count)]
    w_q, w_k, w_v, w_o, stage, go, gq, gk, gv, vec_low, sems, out_sems = refs
    rows, feature = hidden.shape
    unit = feature // 8
    load = Loader(buffers, table, sems)
    wait_o = load.wide(first_unit + 3, w_o)
    waits = [load.wide(first_unit + i, w) for i, w in enumerate((w_q, w_k, w_v))]
    store = Storer(grads, table, slots, out_sems)
    lanes = head_lanes(rows)
    total, grad_gain, grad_shift = layer_norm_back(hidden[...], gain[3:4, :], gradient[...])
    sums[2:3, :] = jnp.sum(total, axis=0, keepdims=True)
    sums[3:4, :] = grad_gain
    sums[4:5, :] = grad_shift
    grad_low = low(total)
    stage[3] = low(dot_left(mixed[...], grad_low))
    store.rows(stage.at[3], unit, unit, 3 * unit)
    wait_all(wait_o)
    go[...] = low(dot_right(grad_low, w_o[...]))
    for pair in range(feature // PAIR):
        columns = slice(pair * PAIR, (pair + 1) * PAIR)
        q_pair, k_pair, v_pair = queries[:, columns], keys[:, columns], values[:, columns]
        go_pair = go[:, columns]
        parts = []
        for half in range(2):
            mine = lanes if half == 0 else ~lanes
            probs_low = probs_in[2 * pair + half]
            probs = probs_low.astype(jnp.float32)
            grad_probs = dot_right(jnp.where(mine, go_pair, jnp.zeros_like(go_pair)), v_pair)
            weighted = grad_probs * probs
            row_sum = jnp.sum(weighted, axis=-1, keepdims=True)
            grad_raw = low((weighted - probs * row_sum) * SCORE_SCALE)
            parts.append(
                (
                    dot_plain(grad_raw, k_pair),
                    dot_left(grad_raw, q_pair),
                    dot_left(probs_low, go_pair),
                )
            )
        grad_q, grad_k, grad_v = (jnp.where(lanes, a, b) for a, b in zip(*parts))
        sums[0:1, columns] = jnp.sum(grad_q, axis=0, keepdims=True)
        sums[1:2, columns] = jnp.sum(grad_v, axis=0, keepdims=True)
        gq[:, columns] = low(grad_q)
        gk[:, columns] = low(grad_k)
        gv[:, columns] = low(grad_v)
    if others:
        parts = [sums[...]] + [other[...] for other in other_sums]
        count = sum(part.shape[0] for part in parts)
        parts.append(jnp.zeros((vec_low.shape[0] - count, feature), jnp.float32))
        vec_low[...] = low(jnp.concatenate(parts, axis=0))
        store.tail(vec_low)
    for index, (source, grad) in enumerate(((q_in, gq), (kv_in, gk), (kv_in, gv))):
        stage[index] = low(dot_left(source[...], grad[...]))
        store.rows(stage.at[index], unit, unit, index * unit)
    for copies in waits:
        wait_all(copies)
    total = total + dot_right(gq[...], w_q[...])
    kv_total = dot_right(gk[...], w_k[...]) + dot_right(gv[...], w_v[...])
    if cross:
        q_grad_out[...] = total
        kv_grad_out[...] = kv_total
    else:
        q_grad_out[...] = total + kv_total
    store.finish()


def attn_back(
    order, gradient, hidden, gain, q_in, kv_in, saved, weights, table, others, slots, name, single=False
):
    rows, feature = hidden.shape
    cross = kv_in is not None
    sources = [gradient, *others, hidden, gain, q_in] + ([kv_in] if cross else []) + list(saved)
    count = tile_up(5 + sum(other.shape[0] for other in others)) if others else 0
    return order.kernel(
        functools.partial(attn_back_body, cross, weights[1], len(others), slots, 2 if single else 3),
        [table, *sources, *weights[0]],
        [SMEM] + [VMEM] * len(sources) + [ANY] * 2,
        [((rows, feature), jnp.float32, VMEM)] * (1 + cross)
        + [((5, feature), jnp.float32, VMEM), *gradient_outs(feature, count, single)],
        [pltpu.VMEM((feature, feature), jnp.bfloat16)] * 4
        + [pltpu.VMEM((4, feature, feature), jnp.bfloat16)]
        + [pltpu.VMEM((rows, feature), jnp.bfloat16)] * 4
        + [pltpu.VMEM((max(count, ROW_TILE), feature), jnp.bfloat16)]
        + [pltpu.SemaphoreType.DMA((32,)), pltpu.SemaphoreType.DMA((34,))],
        name,
        16 * rows * feature * feature,
        20 * feature * feature,
    )


def combine_body(plan, count, *refs):
    inputs = refs[:count]
    outs = refs[count:-4]
    landed, summed, in_sems, out_sems = refs[-4:]
    loads = []
    place = 0
    for out, first, rows, terms in plan:
        parts = []
        for source, row in terms:
            copy = pltpu.make_async_copy(
                inputs[source].at[pl.ds(row, rows), :],
                landed.at[pl.ds(place, rows), :],
                in_sems.at[sum(len(other) for other in loads) + len(parts)],
            )
            copy.start()
            parts.append((copy, place))
            place += rows
        loads.append(parts)
    stores = []
    place = 0
    for (out, first, rows, terms), parts in zip(plan, loads):
        total = None
        for copy, start in parts:
            copy.wait()
            term = landed[start : start + rows, :].astype(jnp.float32)
            total = term if total is None else total + term
        summed[place : place + rows, :] = low(total)
        copy = pltpu.make_async_copy(
            summed.at[pl.ds(place, rows), :],
            outs[out].at[pl.ds(first, rows), :],
            out_sems.at[len(stores)],
        )
        copy.start()
        stores.append(copy)
        place += rows
    wait_all(stores)


def combine(order, name, *jobs):
    inputs, plan, outs = [], [], []
    for sizes, sums, use in jobs:
        for out, first, rows, terms in sums:
            places = []
            for array, row in terms:
                known = [index for index, other in enumerate(inputs) if other is array]
                if not known:
                    inputs.append(array)
                places.append((known[0] if known else len(inputs) - 1, row))
            plan.append((len(outs) + out, first, rows, tuple(places)))
        outs += sizes
    feature = inputs[0].shape[1]
    reads = sum(rows * len(terms) for out, first, rows, terms in plan)
    writes = sum(rows for out, first, rows, terms in plan)
    results = order.kernel(
        functools.partial(combine_body, plan, len(inputs)),
        inputs,
        [ANY] * len(inputs),
        [((rows, feature), jnp.bfloat16, ANY) for rows in outs],
        [
            pltpu.VMEM((reads, feature), jnp.bfloat16),
            pltpu.VMEM((writes, feature), jnp.bfloat16),
            pltpu.SemaphoreType.DMA((sum(len(terms) for out, first, rows, terms in plan),)),
            pltpu.SemaphoreType.DMA((len(plan),)),
        ],
        name,
    )
    for sizes, sums, use in jobs:
        use(*results[: len(sizes)])
        results = results[len(sizes) :]


OWN, X, Y, DIAGONAL = range(4)
X_FIRST = (OWN, Y, X, DIAGONAL)
Y_FIRST = (OWN, X, Y, DIAGONAL)


class Reduce:
    def __init__(self, order, outs, slots, both=False, pad=0):
        self.order = order
        self.pad = pad
        self.keep, self.upper, self.lower = outs if len(outs) == 3 else (outs[0], None, outs[1])
        self.both = both
        self.bits = (2, 4) if slots == X_FIRST else (4, 2)
        self.rows = self.keep.shape[1] // 2
        self.extra = self.keep.shape[0] - 4 * self.rows

    def cores(self):
        self.from_upper = None if self.upper is None else swap(self.order.tie(self.upper), 1)
        self.from_lower = swap(self.order.tie(self.lower), 1)

    def cores_done(self):
        self.order.mark(*(value for value in (self.from_upper, self.from_lower) if value is not None))

    def block(self, slot, first=0):
        row = slot * self.rows + first
        other = (self.from_lower, row) if slot < 2 or self.upper is None else (self.from_upper, row - 2 * self.rows)
        return ((self.keep, row), other)

    def extra_rows(self):
        return ((self.keep, 4 * self.rows), (self.from_lower, (4 if self.upper is None else 2) * self.rows))

    def first(self):
        rows, extra = self.rows, self.extra
        if not self.both:
            plan = [(0, 0, rows, self.block(2)), (0, rows, rows, self.block(3))]
            if extra:
                plan.append((0, 2 * rows, extra, self.extra_rows()))
            if self.pad:
                plan.append((0, 2 * rows + extra, self.pad, self.block(2)[:1]))
            return ([2 * rows + extra + self.pad], plan, self.first_sent)
        cut = rows // 2
        plan = [(0, 0, cut, self.block(3)), (1, 0, cut, self.block(3, cut))]
        if extra:
            plan.append((0, cut, extra, self.extra_rows()))
        return ([cut + extra, cut], plan, self.first_sent)

    def first_sent(self, *sent):
        self.sent = sent[0]
        self.landed = [swap(value, bit) for value, bit in zip(sent, (2, 4) if self.both else self.bits)]

    def second(self):
        rows, extra = self.rows, self.extra
        if not self.both:
            landed = self.landed[0]
            plan = [(0, 0, rows, self.block(1) + ((landed, rows),))]
            if extra:
                plan.append((0, rows, extra, ((self.sent, 2 * rows), (landed, 2 * rows))))
            return ([rows + extra], plan, self.second_sent)
        cut = rows // 2
        from_x, from_y = self.landed
        plan = [
            (0, 0, cut, self.block(1)),
            (0, cut, cut, self.block(1, cut) + ((from_y, 0),)),
            (1, 0, cut, self.block(2) + ((from_x, 0),)),
            (1, cut, cut, self.block(2, cut)),
        ]
        if extra:
            plan.append((1, rows, extra, ((self.sent, cut), (from_x, cut))))
        return ([rows, rows + extra], plan, self.second_sent)

    def second_sent(self, *sent):
        self.sent_last = sent[-1]
        self.last = [swap(value, bit) for value, bit in zip(sent, (2, 4) if self.both else self.bits[1:])]

    def own(self, use):
        rows, extra = self.rows, self.extra
        terms = self.block(0) + tuple((value, 0) for value in self.last)
        if not self.both:
            terms += ((self.landed[0], 0),)
        plan = [(0, 0, rows, terms)]
        if extra:
            plan.append((0, rows, extra, ((self.sent_last, rows), (self.last[-1], rows))))
        return ([rows + extra], plan, use)


def own_stack(pieces, use):
    rows = pieces[0].rows
    plan = [(0, index * rows) + piece.own(None)[1][0][2:] for index, piece in enumerate(pieces)]
    return ([len(pieces) * rows], plan, use)


class Line:
    def __init__(self, value):
        self.value = value
        self.landed = lax.ppermute(value, "rep", [(0, 1), (3, 2)])

    def part(self, first):
        return (self, first)

    def step(self, use):
        rows = self.value.shape[0]
        return ([rows], [(0, 0, rows, ((self.value, 0), (self.landed, 0)))], use)

    def middle(self):
        return self.step(self.middle_sent)

    def middle_sent(self, value):
        self.value = value
        self.landed = lax.ppermute(value, "rep", [(1, 2), (2, 1)])

    def outward(self):
        return self.step(self.outward_sent)

    def outward_sent(self, value):
        self.value = value
        self.landed = lax.ppermute(value, "rep", [(1, 0), (2, 3)])


def finish_body(parts, inner, *refs):
    wide, rest = refs[2 * len(parts)], list(refs[2 * len(parts) + 1 :])
    feature = refs[0].shape[1]
    unit = feature // 8
    for index, first in enumerate(parts):
        value, landed = refs[2 * index], refs[2 * index + 1]

        def rows(begin, count):
            mine = value[first + begin : first + begin + count, :].astype(jnp.float32)
            other = landed[first + begin : first + begin + count, :].astype(jnp.float32)
            return jnp.where(inner[0] == 1, mine, other)

        for j in range(4):
            column = (4 * index + j) * feature
            if wide.shape[0] == unit:
                wide[:, column : column + feature] = rows(j * unit, unit)
            else:
                wide[j * unit : (j + 1) * unit, :] = rows(j * unit, unit)
        if first == 0 and value.shape[0] % (4 * unit):
            rest.pop(0)[...] = rows(4 * unit, value.shape[0] - 4 * unit)


def finish(order, inner, parts, wide, name):
    operands = [inner]
    for line, first in parts:
        operands += [line.value, line.landed]
    feature = operands[1].shape[1]
    unit = feature // 8
    shape = (unit, 4 * feature * len(parts)) if wide else (4 * unit, feature)
    outs = [(shape, jnp.float32, VMEM)]
    for line, first in parts:
        rows = line.value.shape[0] % (4 * unit)
        if rows:
            outs.append(((rows, feature), jnp.float32, VMEM))
    return order.kernel(
        functools.partial(finish_body, [first for line, first in parts]),
        operands,
        [SMEM] + [VMEM] * (len(operands) - 1),
        outs,
        [],
        name,
    )


def per_device(
    enc_in,
    dec_in,
    bucket,
    enc_lengths,
    dec_lengths,
    enc_attn,
    enc_vec,
    enc_w1,
    enc_w2,
    dec_attn,
    dec_vec,
    dec_w1,
    dec_w2,
    enc_cot,
    dec_cot,
):
    feature = enc_in.shape[1]
    unit = feature // 8
    chip_index = lax.axis_index("fsdp").astype(jnp.int32)
    table = chip_index ^ jnp.arange(8, dtype=jnp.int32)
    place = lax.axis_index("rep")
    inner = ((place == 1) | (place == 2)).astype(jnp.int32).reshape(1)
    ids = (table, bucket)
    order = Order()
    mark = order.mark
    g_1, g_2, g_3, g_4 = (Gather(order, feature, "piece_" + name) for name in "1234")
    half = 4 * unit
    e_len, d_len = enc_vec.shape[0], dec_vec.shape[0]
    vec_part = vec_shards([enc_vec, dec_vec], chip_index, feature)
    g_1.sides(enc_attn, dec_attn[:, : 4 * feature], vec_part)
    g_2.sides(enc_w1, enc_w2)
    g_1.corners()
    g_2.corners()
    mark(*g_2.mine[3:])
    (attn_pair,) = g_1.join((0, 2 * half + vec_part.shape[0]))
    (e_feed,) = g_2.join((0, 2 * half))
    g_3.sides(dec_attn[:, 4 * feature :], dec_w1)
    e_attn_vec, e_feed_vec, e_tail, d_self_vec, d_cross_vec, d_feed_vec, d_tail = gathered_vecs(
        order, attn_pair, table, vec_part.shape[0], feature, (e_len, d_len), ((5, 3), (5, 5, 3))
    )
    e_hid_a, e_first, *e_saved = attn_forward(
        order, enc_in, None, e_attn_vec, (attn_pair, 0), ids, enc_lengths, False, "enc_attn"
    )
    mark(e_feed[1])
    g_4.sides(dec_w2)
    d_hid_s, d_first, *s_saved = attn_forward(
        order, dec_in, None, d_self_vec, (attn_pair, 4), ids, dec_lengths, True, "dec_self"
    )
    g_3.corners()
    e_hid_f, encoded, e_act, e_slope = feed_forward(
        order, e_first, e_feed_vec, e_tail, (e_feed, 0), (e_feed, 4), table, "enc_feed"
    )
    g_4.corners()
    cross_pair, w1_pair = g_3.join((0, half), (half, half))
    (w2_pair,) = g_4.join((0, half))
    d_hid_c, d_second, *c_saved = attn_forward(
        order, d_first, encoded, d_cross_vec, (cross_pair, 0), ids, enc_lengths, False, "dec_cross"
    )
    d_hid_f, decoded, d_act, d_slope = feed_forward(
        order, d_second, d_feed_vec, d_tail, (w1_pair, 0), (w2_pair, 0), table, "dec_feed"
    )
    gradient, d_sums_f, *outs = feed_back_out(
        order, [dec_cot], d_hid_f, d_feed_vec, d_act, table, X_FIRST, "dec_back_out"
    )
    red_0 = Reduce(order, outs, X_FIRST)
    red_0.cores()
    gradient, d_bias, *outs = feed_back_in(
        order, gradient, d_slope, d_second, (w1_pair, 0), (w2_pair, 0), table, Y_FIRST, "dec_back_in"
    )
    red_1 = Reduce(order, outs, Y_FIRST)
    red_0.cores_done()
    combine(order, "add_1", red_0.first())
    red_1.cores()
    gradient, grad_encoded, d_sums_c, *outs = attn_back(
        order, gradient, d_hid_c, d_cross_vec, d_first, encoded, c_saved, (cross_pair, 0), table, [],
        X_FIRST, "cross_back",
    )
    red_2 = Reduce(order, outs, X_FIRST)
    red_1.cores_done()
    combine(order, "add_2", red_1.first())
    red_2.cores()
    e_gradient, e_sums_f, *outs = feed_back_out(
        order, [enc_cot, grad_encoded], e_hid_f, e_feed_vec, e_act, table, Y_FIRST, "enc_back_out"
    )
    red_3 = Reduce(order, outs, Y_FIRST, pad=2 * ROW_TILE)
    combine(order, "add_3a", red_0.second())
    red_2.cores_done()
    combine(order, "add_3b", red_2.first())
    red_3.cores()
    e_gradient, e_bias, *outs = feed_back_in(
        order, e_gradient, e_slope, e_first, (e_feed, 0), (e_feed, 4), table, X_FIRST, "enc_back_in"
    )
    red_4 = Reduce(order, outs, X_FIRST)
    totals = {}

    def keep_as(key):
        return lambda value: totals.update({key: value})

    mark(*red_0.last)
    combine(order, "add_4a", red_1.second())
    red_3.cores_done()
    combine(order, "add_4b", red_3.first())
    red_4.cores()
    dec_in_grad, d_sums_s, *outs = attn_back(
        order, gradient, d_hid_s, d_self_vec, dec_in, None, s_saved, (attn_pair, 4), table,
        [d_sums_c, d_sums_f, d_bias], Y_FIRST, "self_back",
    )
    red_5 = Reduce(order, outs, Y_FIRST, True)
    combine(order, "add_5a", red_2.second())
    mark(*red_1.last)
    red_4.cores_done()
    combine(order, "add_5b", red_4.first())
    red_5.cores()
    enc_in_grad, e_sums_a, *outs = attn_back(
        order, e_gradient, e_hid_a, e_attn_vec, enc_in, None, e_saved, (attn_pair, 0), table,
        [e_sums_f, e_bias], Y_FIRST, "enc_attn_back", True,
    )
    red_6 = Reduce(order, outs, Y_FIRST, True)
    red_5.cores_done()
    mark(*red_2.last)
    combine(
        order, "add_6a", red_3.second(), red_5.first(), own_stack([red_0, red_1], keep_as("a"))
    )
    line_a = Line(totals["a"])
    mark(red_5.landed[1])
    combine(order, "add_6b", red_4.second())
    red_6.cores()
    mark(*red_3.last)
    red_6.cores_done()
    combine(order, "add_6c", red_6.first())
    mark(*red_6.landed, *red_4.last)
    combine(order, "add_8", line_a.middle(), red_5.second(), own_stack([red_2, red_3], keep_as("b")))
    line_b = Line(totals["b"])
    mark(*red_5.last)
    combine(order, "add_9", red_6.second(), red_4.own(keep_as(4)), red_5.own(keep_as(5)))
    combine(order, "add_10", line_a.outward(), line_b.middle(), red_6.own(keep_as(6)))
    line_4 = Line(totals[4])
    line_5 = Line(order.tie(totals[5]))
    combine(order, "add_11", line_b.outward(), line_4.middle())
    combine(order, "add_12", line_5.middle())
    line_6 = Line(order.tie(totals[6]))
    (grad_d_w2,) = finish(order, inner, [line_a.part(0)], False, "out_0")
    (grad_d_w1,) = finish(order, inner, [line_a.part(half)], True, "out_1")
    combine(order, "add_13", line_4.outward(), line_6.middle())
    combine(order, "add_14", line_5.outward())
    (grad_e_w2,) = finish(order, inner, [line_b.part(half)], False, "out_3")
    (grad_e_w1,) = finish(order, inner, [line_4.part(0)], True, "out_4")
    combine(order, "add_15", line_6.outward())
    grad_d_attn, d_vec = finish(order, inner, [line_5.part(0), line_b.part(0)], True, "out_5")
    grad_e_attn, e_vec = finish(order, inner, [line_6.part(0)], True, "out_6")

    def own_part(rows, length):
        return lax.dynamic_slice(rows.reshape(-1), (chip_index * length,), (length,))

    return (
        encoded,
        decoded,
        enc_in_grad,
        dec_in_grad,
        grad_e_attn,
        own_part(e_vec, e_len),
        grad_e_w1,
        grad_e_w2,
        grad_d_attn,
        own_part(d_vec, d_len),
        grad_d_w1,
        grad_d_w2,
    )


def solution(mesh):
    in_specs = (
        P(("rep", "fsdp"), None),
        P(("rep", "fsdp"), None),
        P(("rep", "fsdp")),
        P(("rep", "fsdp"), None),
        P(("rep", "fsdp"), None),
        P("fsdp", None),
        P("fsdp"),
        P("fsdp", None),
        P("fsdp", None),
        P("fsdp", None),
        P("fsdp"),
        P("fsdp", None),
        P("fsdp", None),
        P(("rep", "fsdp"), None),
        P(("rep", "fsdp"), None),
    )
    out_specs = (
        P(("rep", "fsdp"), None),
        P(("rep", "fsdp"), None),
        P(("rep", "fsdp"), None),
        P(("rep", "fsdp"), None),
        P("fsdp", None),
        P("fsdp"),
        P("fsdp", None),
        P("fsdp", None),
        P("fsdp", None),
        P("fsdp"),
        P("fsdp", None),
        P("fsdp", None),
    )
    small = mesh.shape["fsdp"] == 8 and mesh.shape["rep"] == 4
    return jax.shard_map(
        per_device if small else per_device_any, mesh=mesh, in_specs=in_specs, out_specs=out_specs, check_vma=False
    )
```

```python
import functools

import jax
import jax.numpy as jnp
from jax import lax
from jax.experimental import pallas as pl
from jax.experimental.pallas import tpu as pltpu
from jax.sharding import PartitionSpec as P

HEAD = 64
PAIR = 2 * HEAD
ROW_TILE = 16
VMEM_BYTES = 56 * 1024 * 1024
SMALL_VMEM_BYTES = 20 * 1024 * 1024
MIDDLE_VMEM_BYTES = 44 * 1024 * 1024
WIDE = ("add_6a", "add_6b", "add_6c", "add_8", "add_9")
MIDDLE = ('enc_attn', 'dec_self', 'cross_back', 'enc_back_out', 'self_back')
ANY = pl.BlockSpec(memory_space=pl.ANY)
SMEM = pl.BlockSpec(memory_space=pltpu.SMEM)
VMEM = pl.BlockSpec(memory_space=pltpu.VMEM)


EPSILON = 1e-05
NEG_FILL = -1e30
SCORE_SCALE = 0.125


def norm_rows(hidden, gain_row, shift_row):
    row_mean = jnp.mean(hidden, axis=-1, keepdims=True)
    centred = hidden - row_mean
    variance = jnp.mean(centred * centred, axis=-1, keepdims=True)
    return centred * lax.rsqrt(variance + EPSILON) * gain_row + shift_row


def norm_back(hidden, gain_row, shift_row, gradient):
    unused, pullback = jax.vjp(norm_rows, hidden, gain_row, shift_row)
    return pullback(gradient)


def gelu_exact(hidden):
    return jax.nn.gelu(hidden, approximate=False)


def dot_plain(first_op, second_op):
    return jnp.dot(first_op, second_op, preferred_element_type=jnp.float32)


def dot_left(first_op, second_op):
    return lax.dot_general(
        first_op, second_op, (((0,), (0,)), ((), ())), preferred_element_type=jnp.float32
    )


def dot_right(first_op, second_op):
    return lax.dot_general(
        first_op, second_op, (((1,), (1,)), ((), ())), preferred_element_type=jnp.float32
    )


def build_masks(one_long, enc_len, dec_len, row_total, seg_count):
    span_rows = jnp.where(one_long == 1, row_total, row_total // seg_count).astype(jnp.int32)
    row_index = jnp.arange(row_total, dtype=jnp.int32)
    group_id = row_index // span_rows
    row_place = row_index - group_id * span_rows
    in_group = group_id[:, None] == jnp.arange(seg_count, dtype=jnp.int32)[None, :]
    enc_live = row_place < jnp.sum(jnp.where(in_group, enc_len[None, :], 0), axis=1)
    dec_live = row_place < jnp.sum(jnp.where(in_group, dec_len[None, :], 0), axis=1)
    same_group = group_id[:, None] == group_id[None, :]
    enc_mask = same_group & enc_live[None, :]
    self_mask = same_group & dec_live[None, :] & (row_index[None, :] <= row_index[:, None])
    return (enc_mask, self_mask, enc_mask)


def unpack(vector, row_count, feature):
    rows_part = vector[: row_count * feature].astype(jnp.float32).reshape(row_count, feature)
    return (rows_part, vector[row_count * feature :].astype(jnp.float32))


def fetch(attn_rows, vec_part, w_in, w_out):
    return (
        lax.all_gather(attn_rows, "fsdp", axis=0, tiled=True),
        lax.all_gather(vec_part, "fsdp", axis=0, tiled=True),
        lax.all_gather(w_in, "fsdp", axis=0, tiled=True),
        lax.all_gather(w_out, "fsdp", axis=0, tiled=True),
    )


def fetch_again(attn_rows, vec_part, w_in, w_out):
    return (
        lax.all_gather(attn_rows, "fsdp", axis=0, tiled=True),
        lax.all_gather(vec_part, "fsdp", axis=0, tiled=True),
        lax.all_gather(w_in, "fsdp", axis=0, tiled=True),
        lax.all_gather(w_out, "fsdp", axis=0, tiled=True),
    )


def reduce_grads(grad_attn, grad_vec, grad_in, grad_out):
    shard = (
        lax.psum_scatter(
            grad_attn.astype(jnp.bfloat16), "fsdp", scatter_dimension=0, tiled=True
        ).astype(jnp.float32),
        lax.psum_scatter(
            grad_vec.astype(jnp.bfloat16), "fsdp", scatter_dimension=0, tiled=True
        ).astype(jnp.float32),
        lax.psum_scatter(
            grad_in.astype(jnp.bfloat16), "fsdp", scatter_dimension=0, tiled=True
        ).astype(jnp.float32),
        lax.psum_scatter(
            grad_out.astype(jnp.bfloat16), "fsdp", scatter_dimension=0, tiled=True
        ).astype(jnp.float32),
    )
    return (
        lax.psum(shard[0].astype(jnp.bfloat16), "rep").astype(jnp.float32),
        lax.psum(shard[1].astype(jnp.bfloat16), "rep").astype(jnp.float32),
        lax.psum(shard[2].astype(jnp.bfloat16), "rep").astype(jnp.float32),
        lax.psum(shard[3].astype(jnp.bfloat16), "rep").astype(jnp.float32),
    )


def attend(q_in, kv_in, weights, biases, key_mask, one_source):
    row_total, feature = q_in.shape
    head_count = feature // HEAD
    if one_source:
        packed = dot_plain(q_in, weights[:, : 3 * feature])
        q_pre = packed[:, :feature]
        k_pre = packed[:, feature : 2 * feature]
        v_pre = packed[:, 2 * feature :]
    else:
        q_pre = dot_plain(q_in, weights[:, :feature])
        packed = dot_plain(kv_in, weights[:, feature : 3 * feature])
        k_pre = packed[:, :feature]
        v_pre = packed[:, feature:]
    queries = (q_pre + biases[0]).astype(jnp.bfloat16).reshape(row_total, head_count, HEAD)
    keys_low = k_pre.astype(jnp.bfloat16).reshape(row_total, head_count, HEAD)
    values = (v_pre + biases[1]).astype(jnp.bfloat16).reshape(row_total, head_count, HEAD)
    raw_score = jnp.einsum("qhd,khd->hqk", queries, keys_low, preferred_element_type=jnp.float32)
    probs = jax.nn.softmax(jnp.where(key_mask[None], raw_score * SCORE_SCALE, NEG_FILL), axis=-1)
    probs_low = probs.astype(jnp.bfloat16)
    mixed = jnp.einsum("hqk,khd->qhd", probs_low, values, preferred_element_type=jnp.float32)
    mixed = mixed.reshape(row_total, feature).astype(jnp.bfloat16)
    branch = dot_plain(mixed, weights[:, 3 * feature :]) + biases[2]
    return (branch, (queries, keys_low, values, probs, probs_low, mixed))


def attend_back(gradient, q_in, kv_in, weights, saved, one_source):
    queries, keys_low, values, probs, probs_low, mixed = saved
    row_total, feature = q_in.shape
    head_count = feature // HEAD
    grad_bias_o = jnp.sum(gradient, axis=0)
    grad_low = gradient.astype(jnp.bfloat16)
    grad_w_o = dot_left(mixed, grad_low)
    grad_mixed = dot_right(grad_low, weights[:, 3 * feature :]).astype(jnp.bfloat16)
    grad_mixed = grad_mixed.reshape(row_total, head_count, HEAD)
    grad_probs = jnp.einsum("qhd,khd->hqk", grad_mixed, values, preferred_element_type=jnp.float32)
    grad_values = jnp.einsum(
        "hqk,qhd->khd", probs_low, grad_mixed, preferred_element_type=jnp.float32
    )
    grad_score = probs * (grad_probs - jnp.sum(grad_probs * probs, axis=-1, keepdims=True))
    grad_raw = (grad_score * SCORE_SCALE).astype(jnp.bfloat16)
    grad_query = jnp.einsum(
        "hqk,khd->qhd", grad_raw, keys_low, preferred_element_type=jnp.float32
    ).reshape(row_total, feature)
    grad_keys = jnp.einsum(
        "hqk,qhd->khd", grad_raw, queries, preferred_element_type=jnp.float32
    ).reshape(row_total, feature)
    grad_values = grad_values.reshape(row_total, feature)
    grad_bias_q = jnp.sum(grad_query, axis=0)
    grad_bias_v = jnp.sum(grad_values, axis=0)
    low_query = grad_query.astype(jnp.bfloat16)
    low_kv = jnp.concatenate(
        [grad_keys.astype(jnp.bfloat16), grad_values.astype(jnp.bfloat16)], axis=1
    )
    if one_source:
        packed = jnp.concatenate([low_query, low_kv], axis=1)
        grad_weights = jnp.concatenate([dot_left(q_in, packed), grad_w_o], axis=1)
        grad_q_in = dot_right(packed, weights[:, : 3 * feature])
        grad_kv_in = grad_q_in
    else:
        grad_weights = jnp.concatenate(
            [dot_left(q_in, low_query), dot_left(kv_in, low_kv), grad_w_o], axis=1
        )
        grad_q_in = dot_right(low_query, weights[:, :feature])
        grad_kv_in = dot_right(low_kv, weights[:, feature : 3 * feature])
    return (grad_q_in, grad_kv_in, grad_weights, (grad_bias_q, grad_bias_v, grad_bias_o))


def feed(rows_in, w_in, b_in, w_out, b_out):
    hidden = dot_plain(rows_in, w_in) + b_in
    active = gelu_exact(hidden).astype(jnp.bfloat16)
    return (dot_plain(active, w_out) + b_out, (hidden, active))


def feed_back(gradient, rows_in, w_in, w_out, saved):
    hidden, active = saved
    grad_b_out = jnp.sum(gradient, axis=0)
    grad_low = gradient.astype(jnp.bfloat16)
    grad_w_out = dot_left(active, grad_low)
    grad_active = dot_right(grad_low, w_out)
    unused, pullback = jax.vjp(gelu_exact, hidden)
    grad_hidden = pullback(grad_active)[0]
    grad_b_in = jnp.sum(grad_hidden, axis=0)
    hidden_low = grad_hidden.astype(jnp.bfloat16)
    grad_w_in = dot_left(rows_in, hidden_low)
    grad_rows = dot_right(hidden_low, w_in)
    return (grad_rows, grad_w_in, grad_b_in, grad_w_out, grad_b_out)


def per_device_any(
    enc_in,
    dec_in,
    bucket,
    enc_lengths,
    dec_lengths,
    enc_attn,
    enc_vec,
    enc_w1,
    enc_w2,
    dec_attn,
    dec_vec,
    dec_w1,
    dec_w2,
    enc_cot,
    dec_cot,
):
    row_total, feature = enc_in.shape
    enc_mask, self_mask, cross_mask = build_masks(
        bucket[0], enc_lengths[0], dec_lengths[0], row_total, enc_lengths.shape[1]
    )
    enc_weights = fetch(enc_attn, enc_vec, enc_w1, enc_w2)
    e_attn, e_vec, e_in, e_out = enc_weights
    e_rows, e_tail = unpack(e_vec, 8, feature)
    branch, e_saved_a = attend(enc_in, enc_in, e_attn, e_rows[0:3], enc_mask, True)
    e_hid_a = enc_in.astype(jnp.float32) + branch
    e_first = norm_rows(e_hid_a, e_rows[3], e_rows[4]).astype(jnp.bfloat16)
    branch, e_saved_f = feed(e_first, e_in, e_tail, e_out, e_rows[5])
    e_hid_f = e_first.astype(jnp.float32) + branch
    encoded = norm_rows(e_hid_f, e_rows[6], e_rows[7]).astype(jnp.bfloat16)
    dec_weights = fetch(dec_attn, dec_vec, dec_w1, dec_w2)
    d_attn, d_vec, d_in, d_out = dec_weights
    d_rows, d_tail = unpack(d_vec, 13, feature)
    branch, d_saved_s = attend(
        dec_in, dec_in, d_attn[:, : 4 * feature], d_rows[0:3], self_mask, True
    )
    d_hid_s = dec_in.astype(jnp.float32) + branch
    d_first = norm_rows(d_hid_s, d_rows[3], d_rows[4]).astype(jnp.bfloat16)
    branch, d_saved_c = attend(
        d_first, encoded, d_attn[:, 4 * feature :], d_rows[5:8], cross_mask, False
    )
    d_hid_c = d_first.astype(jnp.float32) + branch
    d_second = norm_rows(d_hid_c, d_rows[8], d_rows[9]).astype(jnp.bfloat16)
    branch, d_saved_f = feed(d_second, d_in, d_tail, d_out, d_rows[10])
    d_hid_f = d_second.astype(jnp.float32) + branch
    decoded = norm_rows(d_hid_f, d_rows[11], d_rows[12]).astype(jnp.bfloat16)
    dec_weights = fetch_again(dec_attn, dec_vec, dec_w1, dec_w2)
    d_attn, d_vec, d_in, d_out = dec_weights
    d_rows, d_tail = unpack(d_vec, 13, feature)
    gradient, grad_g11, grad_n12 = norm_back(
        d_hid_f, d_rows[11], d_rows[12], dec_cot.astype(jnp.float32)
    )
    grad_rows, grad_d_in, grad_d_tail, grad_d_out, grad_b10 = feed_back(
        gradient, d_second, d_in, d_out, d_saved_f
    )
    gradient, grad_g8, grad_n9 = norm_back(d_hid_c, d_rows[8], d_rows[9], gradient + grad_rows)
    grad_q_in, grad_encoded, grad_cross, cross_bias = attend_back(
        gradient, d_first, encoded, d_attn[:, 4 * feature :], d_saved_c, False
    )
    gradient, grad_g3, grad_n4 = norm_back(d_hid_s, d_rows[3], d_rows[4], gradient + grad_q_in)
    grad_self_in, unused, grad_self, self_bias = attend_back(
        gradient, dec_in, dec_in, d_attn[:, : 4 * feature], d_saved_s, True
    )
    dec_in_grad = gradient + grad_self_in
    dec_stack = jnp.stack(
        [
            self_bias[0],
            self_bias[1],
            self_bias[2],
            grad_g3,
            grad_n4,
            cross_bias[0],
            cross_bias[1],
            cross_bias[2],
            grad_g8,
            grad_n9,
            grad_b10,
            grad_g11,
            grad_n12,
        ]
    )
    dec_vec_full = jnp.concatenate([dec_stack.reshape(-1), grad_d_tail])
    dec_shards = reduce_grads(
        jnp.concatenate([grad_self, grad_cross], axis=1), dec_vec_full, grad_d_in, grad_d_out
    )
    enc_weights = fetch_again(enc_attn, enc_vec, enc_w1, enc_w2)
    e_attn, e_vec, e_in, e_out = enc_weights
    e_rows, e_tail = unpack(e_vec, 8, feature)
    gradient, grad_g6, grad_n7 = norm_back(
        e_hid_f, e_rows[6], e_rows[7], enc_cot.astype(jnp.float32) + grad_encoded
    )
    grad_rows, grad_e_in, grad_e_tail, grad_e_out, grad_b5 = feed_back(
        gradient, e_first, e_in, e_out, e_saved_f
    )
    gradient, grad_g3e, grad_n4e = norm_back(e_hid_a, e_rows[3], e_rows[4], gradient + grad_rows)
    grad_self_in, unused, grad_e_attn, enc_bias = attend_back(
        gradient, enc_in, enc_in, e_attn, e_saved_a, True
    )
    enc_in_grad = gradient + grad_self_in
    enc_stack = jnp.stack(
        [enc_bias[0], enc_bias[1], enc_bias[2], grad_g3e, grad_n4e, grad_b5, grad_g6, grad_n7]
    )
    enc_vec_full = jnp.concatenate([enc_stack.reshape(-1), grad_e_tail])
    enc_shards = reduce_grads(grad_e_attn, enc_vec_full, grad_e_in, grad_e_out)
    return (
        encoded,
        decoded,
        enc_in_grad,
        dec_in_grad,
        enc_shards[0],
        enc_shards[1],
        enc_shards[2],
        enc_shards[3],
        dec_shards[0],
        dec_shards[1],
        dec_shards[2],
        dec_shards[3],
    )


def swap(value, bit):
    return lax.ppermute(value, "fsdp", [(i, i ^ bit) for i in range(8)])


def add_low(*terms):
    total = terms[0].astype(jnp.float32)
    for term in terms[1:]:
        total = total + term.astype(jnp.float32)
    return total.astype(jnp.bfloat16)


def tile_up(rows):
    return -(-rows // ROW_TILE) * ROW_TILE


def size_of(shape):
    total = 1
    for extent in shape:
        total *= extent
    return total


class Order:
    def __init__(self):
        self.token = None
        self.waits = []

    def mark(self, *values):
        self.waits += values

    def tie(self, value):
        if self.token is None:
            return value
        value, self.token = lax.optimization_barrier((value, self.token))
        return value

    def kernel(self, body, operands, specs, outs, scratch, name, flops=0, moved=0):
        extra = self.waits + ([] if self.token is None else [self.token])
        self.waits = []
        count, skip = len(operands), len(extra)
        grant = SMALL_VMEM_BYTES if not flops and name not in WIDE else MIDDLE_VMEM_BYTES if name in MIDDLE else VMEM_BYTES
        results = pl.pallas_call(
            lambda *refs: body(*refs[:count], *refs[count + skip :]),
            out_shape=[jax.ShapeDtypeStruct(shape, dtype) for shape, dtype, spec in outs],
            in_specs=list(specs) + [ANY] * skip,
            out_specs=[spec for shape, dtype, spec in outs],
            scratch_shapes=scratch,
            compiler_params=pltpu.CompilerParams(
                vmem_limit_bytes=grant
            ),
            cost_estimate=pl.CostEstimate(flops=flops, bytes_accessed=moved, transcendentals=0),
            name=name,
        )(*operands, *extra)
        self.token = min(results, key=lambda result: result.size)
        return results


def pack_body(count, *refs):
    shards, out = refs[:count], refs[-1]
    feature = out.shape[1]
    offset = 0
    for shard in shards:
        rows, columns = shard.shape
        for block in range(columns // feature):
            out[offset : offset + rows, :] = shard[:, block * feature : (block + 1) * feature]
            offset += rows


def split_body(cut, from_x, from_y, top, lower):
    top[...] = from_x[:cut, :]
    lower[...] = from_y[cut:, :]


def vec_rows(vec_part, feature):
    rows = tile_up(-(-vec_part.shape[0] // feature))
    padded = jnp.pad(vec_part, (0, rows * feature - vec_part.shape[0]))
    return padded.reshape(rows, feature)


class Gather:
    def __init__(self, order, feature, name):
        self.order = order
        self.feature = feature
        self.name = name
        self.mine = []

    def sides(self, *shards):
        feature = self.feature
        rows = sum(shard.size for shard in shards) // feature
        (packed,) = self.order.kernel(
            functools.partial(pack_body, len(shards)),
            shards,
            [VMEM] * len(shards),
            [((rows, feature), jnp.bfloat16, VMEM)],
            [],
            self.name + "_pack",
            moved=4 * rows * feature,
        )
        self.mine = [packed, swap(packed, 2), swap(packed, 4)]

    def corners(self):
        rows, feature = self.mine[0].shape
        cut = rows // (2 * ROW_TILE) * ROW_TILE
        top, lower = self.order.kernel(
            functools.partial(split_body, cut),
            self.mine[1:3],
            [VMEM] * 2,
            [
                ((cut, feature), jnp.bfloat16, VMEM),
                ((rows - cut, feature), jnp.bfloat16, VMEM),
            ],
            [],
            self.name + "_split",
            moved=4 * rows * feature,
        )
        self.mine += [swap(top, 4), swap(lower, 2)]

    def join(self, *parts):
        rows, feature = self.mine[0].shape
        joined = self.order.kernel(
            functools.partial(join_body, parts),
            self.mine,
            [ANY] * 5,
            [((4 * count, feature), jnp.bfloat16, ANY) for first, count in parts],
            [pltpu.VMEM((4 * rows, feature), jnp.bfloat16), pltpu.SemaphoreType.DMA((5 + 4 * len(parts),))],
            self.name + "_join",
        )
        return [(part, swap(part, 1)) for part in joined]


def join_body(parts, own, from_x, from_y, top, lower, *refs):
    outs, stage, sems = refs[:-2], refs[-2], refs[-1]
    copies = []
    place = 0
    for index, source in enumerate((own, from_x, from_y, top, lower)):
        rows = source.shape[0]
        copy = pltpu.make_async_copy(source, stage.at[pl.ds(place, rows), :], sems.at[index])
        copy.start()
        copies.append(copy)
        place += rows
    block = own.shape[0]
    stores = []
    for chip in range(4):
        wait_all(copies[chip : chip + 1] if chip < 3 else copies[3:])
        for (first, count), out in zip(parts, outs):
            copy = pltpu.make_async_copy(
                stage.at[pl.ds(chip * block + first, count), :],
                out.at[pl.ds(chip * count, count), :],
                sems.at[5 + len(stores)],
            )
            copy.start()
            stores.append(copy)
    wait_all(stores)


LANES = 128


def chunk_count(length):
    return max(-(-((place * length) % LANES + length) // LANES) for place in range(8))


def vec_shards(vectors, chip_index, feature):
    parts = []
    for vector in vectors:
        length = vector.shape[0]
        blank = jnp.zeros((chunk_count(length) * LANES,), vector.dtype)
        parts.append(lax.dynamic_update_slice(blank, vector, ((chip_index * length) % LANES,)))
    return vec_rows(jnp.concatenate(parts), feature)


def vec_body(lengths, sections, table, mine, theirs, *refs):
    outs, landed, wide, sems = refs[:-3], refs[-3], refs[-2], refs[-1]
    rows = landed.shape[0] // 8
    feature = landed.shape[1]
    block = mine.shape[0] // 4
    copies = []
    for chip in range(4):
        for core, source in enumerate((mine, theirs)):
            copies.append(
                pltpu.make_async_copy(
                    source.at[pl.ds((chip + 1) * block - rows, rows), :],
                    landed.at[pl.ds(pl.multiple_of(table[2 * chip + core] * rows, ROW_TILE), rows), :],
                    sems.at[len(copies)],
                )
            )
    for copy in copies:
        copy.start()
    wait_all(copies)
    wide[...] = landed[...].astype(jnp.float32)
    per_row = feature // LANES
    outs = list(outs)
    skip = 0
    for length, section in zip(lengths, sections):
        targets = []
        for count in section:
            out = outs.pop(0)
            targets += [(out, row, lane * LANES) for row in range(count) for lane in range(per_row)]
        out = outs.pop(0)
        targets += [(out, 0, lane * LANES) for lane in range(out.shape[1] // LANES)]
        filled = set()
        for place in range(8):
            base = place * length // LANES
            used = -(-((place * length) % LANES + length) // LANES)
            for chunk in range(used):
                flat = (skip + chunk) * LANES
                row, lane = place * rows + flat // feature, flat % feature
                value = wide[row : row + 1, lane : lane + LANES]
                out, row, lane = targets[base + chunk]
                if base + chunk in filled:
                    value = value + out[row : row + 1, lane : lane + LANES]
                out[row : row + 1, lane : lane + LANES] = value
                filled.add(base + chunk)
        skip += chunk_count(length)


def gathered_vecs(order, buffers, table, rows, feature, lengths, sections):
    outs = []
    for length, section in zip(lengths, sections):
        outs += [((count, feature), jnp.float32, VMEM) for count in section]
        outs.append(((1, 8 * length - sum(section) * feature), jnp.float32, VMEM))
    return order.kernel(
        functools.partial(vec_body, lengths, sections),
        [table, *buffers],
        [SMEM] + [ANY] * 2,
        outs,
        [
            pltpu.VMEM((8 * rows, feature), jnp.bfloat16),
            pltpu.VMEM((8 * rows, feature), jnp.float32),
            pltpu.SemaphoreType.DMA((8,)),
        ],
        "vectors",
    )


class Loader:
    def __init__(self, buffers, table, sems, used=0):
        self.buffers = buffers
        self.block = buffers[0].shape[0] // 4
        self.table = table
        self.sems = sems
        self.used = used

    def unit(self, number, target, stride, first):
        rows = target.shape[1] // 8
        copies = []
        for chip in range(4):
            for core in range(2):
                offset = chip * self.block + number * rows
                place = pl.multiple_of(self.table[2 * chip + core] * stride + first, ROW_TILE)
                copy = pltpu.make_async_copy(
                    self.buffers[core].at[pl.ds(offset, rows), :],
                    target.at[pl.ds(place, rows), :],
                    self.sems.at[self.used],
                )
                copy.start()
                self.used += 1
                copies.append(copy)
        return copies

    def wide(self, number, target):
        return self.unit(number, target, target.shape[1] // 8, 0)

    def tall(self, number, target):
        rows = target.shape[1] // 8
        copies = []
        for block in range(4):
            copies += self.unit(number + block, target, 4 * rows, block * rows)
        return copies


def wait_all(copies):
    for copy in copies:
        copy.wait()


class Storer:
    def __init__(self, outs, table, slots, sems):
        self.keep, self.upper, self.lower = outs if len(outs) == 3 else (outs[0], None, outs[1])
        self.table = table
        self.slots = slots
        self.block = self.keep.shape[1] // 2
        self.sems = sems
        self.copies = []

    def add(self, source, out, row):
        copy = pltpu.make_async_copy(
            source, out.at[pl.ds(row, source.shape[0]), :], self.sems.at[len(self.copies)]
        )
        copy.start()
        self.copies.append(copy)

    def rows(self, source, stride, count, offset):
        for core in (1, 0):
            for slot in (2, 3, 0, 1):
                place = self.table[2 * self.slots[slot] + core] * stride
                block = source.at[pl.ds(pl.multiple_of(place, ROW_TILE), count), :]
                if core == 0:
                    self.add(block, self.keep, slot * self.block + offset)
                elif slot < 2 or self.upper is None:
                    self.add(block, self.lower, slot * self.block + offset)
                else:
                    self.add(block, self.upper, (slot - 2) * self.block + offset)

    def tail(self, source):
        self.add(source, self.lower, (4 if self.upper is None else 2) * self.block)
        self.add(source, self.keep, 4 * self.block)

    def finish(self):
        wait_all(self.copies)


def gradient_outs(feature, extra=0, single=False):
    rows = feature // 2
    if single:
        return [((4 * rows + extra, feature), jnp.bfloat16, ANY)] * 2
    return [((count, feature), jnp.bfloat16, ANY) for count in (4 * rows + extra, 2 * rows, 2 * rows + extra)]


def low(value):
    return value.astype(jnp.bfloat16)


def layer_norm(hidden, gain, shift):
    mean = jnp.mean(hidden, axis=-1, keepdims=True)
    centred = hidden - mean
    variance = jnp.mean(centred * centred, axis=-1, keepdims=True)
    return centred * lax.rsqrt(variance + EPSILON) * gain + shift


def layer_norm_back(hidden, gain, gradient):
    mean = jnp.mean(hidden, axis=-1, keepdims=True)
    centred = hidden - mean
    variance = jnp.mean(centred * centred, axis=-1, keepdims=True)
    scale = lax.rsqrt(variance + EPSILON)
    unit = centred * scale
    grad_gain = jnp.sum(gradient * unit, axis=0, keepdims=True)
    grad_shift = jnp.sum(gradient, axis=0, keepdims=True)
    inner = gradient * gain
    mean_inner = jnp.mean(inner, axis=-1, keepdims=True)
    mean_unit = jnp.mean(inner * unit, axis=-1, keepdims=True)
    return (scale * (inner - mean_inner - unit * mean_unit), grad_gain, grad_shift)


def key_mask(bucket, lengths, rows, segs, causal):
    span = rows // segs
    one_long = bucket[0] == 1
    query = lax.broadcasted_iota(jnp.int32, (rows, rows), 0)
    key = lax.broadcasted_iota(jnp.int32, (rows, rows), 1)
    key_row = lax.broadcasted_iota(jnp.int32, (1, rows), 1)
    limit = jnp.zeros((1, rows), jnp.int32)
    start = jnp.zeros((1, rows), jnp.int32)
    first = jnp.zeros((rows, 1), jnp.int32)
    query_col = lax.broadcasted_iota(jnp.int32, (rows, 1), 0)
    for seg in range(segs):
        inside = (key_row >= seg * span) & (key_row < (seg + 1) * span)
        limit = jnp.where(inside, seg * span + lengths[0, seg], limit)
        start = jnp.where(inside, seg * span, start)
        first = jnp.where((query_col >= seg * span) & (query_col < (seg + 1) * span), seg * span, first)
    limit = jnp.where(one_long, lengths[0, 0], limit)
    start = jnp.where(one_long, 0, start)
    first = jnp.where(one_long, 0, first)
    mask = (first == start) & (key < limit)
    if causal:
        mask = mask & (key <= query)
    return mask


def head_lanes(rows):
    return lax.broadcasted_iota(jnp.int32, (rows, PAIR), 1) < HEAD


def attn_body(
    cross, causal, first_unit, segs, table, bucket, lengths, *refs
):
    refs = list(refs)
    q_in = refs.pop(0)
    kv_in = refs.pop(0) if cross else q_in
    vec = refs.pop(0)
    buffers = [refs.pop(0) for _ in range(2)]
    hidden_out, norm_out, q_out, k_out, v_out, o_out, p_out = refs[:7]
    w_q, w_k, w_v, w_o, sems = refs[7:]
    rows, feature = q_in.shape
    load = Loader(buffers, table, sems)
    waits = [load.wide(first_unit + i, w) for i, w in enumerate((w_q, w_k, w_v, w_o))]
    mask = key_mask(bucket, lengths, rows, segs, causal)
    lanes = head_lanes(rows)
    wait_all(waits[0])
    q_out[...] = low(dot_plain(q_in[...], w_q[...]) + vec[0:1, :])
    wait_all(waits[1])
    k_out[...] = low(dot_plain(kv_in[...], w_k[...]))
    wait_all(waits[2])
    v_out[...] = low(dot_plain(kv_in[...], w_v[...]) + vec[1:2, :])
    for pair in range(feature // PAIR):
        columns = slice(pair * PAIR, (pair + 1) * PAIR)
        q_pair, k_pair, v_pair = q_out[:, columns], k_out[:, columns], v_out[:, columns]
        mixed = []
        for half in range(2):
            mine = lanes if half == 0 else ~lanes
            score = dot_right(jnp.where(mine, q_pair, jnp.zeros_like(q_pair)), k_pair)
            score = jnp.where(mask, score * SCORE_SCALE, NEG_FILL)
            power = jnp.exp(score - jnp.max(score, axis=-1, keepdims=True))
            probs = low(power / jnp.sum(power, axis=-1, keepdims=True))
            p_out[2 * pair + half] = probs
            mixed.append(dot_plain(probs, v_pair))
        o_out[:, columns] = low(jnp.where(lanes, mixed[0], mixed[1]))
    wait_all(waits[3])
    hidden = q_in[...].astype(jnp.float32) + (dot_plain(o_out[...], w_o[...]) + vec[2:3, :])
    hidden_out[...] = hidden
    norm_out[...] = low(layer_norm(hidden, vec[3:4, :], vec[4:5, :]))


def attn_forward(order, q_in, kv_in, vec, weights, ids, lengths, causal, name):
    rows, feature = q_in.shape
    sources = [q_in] + ([] if kv_in is None else [kv_in]) + [vec]
    wide = ((rows, feature), jnp.bfloat16, VMEM)
    return order.kernel(
        functools.partial(attn_body, kv_in is not None, causal, weights[1], lengths.shape[1]),
        [*ids, lengths, *sources, *weights[0]],
        [SMEM] * 3 + [VMEM] * len(sources) + [ANY] * 2,
        [((rows, feature), jnp.float32, VMEM)]
        + [wide] * 5
        + [((feature // HEAD, rows, rows), jnp.bfloat16, VMEM)],
        [pltpu.VMEM((feature, feature), jnp.bfloat16)] * 4 + [pltpu.SemaphoreType.DMA((32,))],
        name,
        8 * rows * feature * feature,
        10 * feature * feature,
    )


def gelu_parts(hidden):
    phi = 0.5 * (1.0 + lax.erf(hidden * 0.7071067811865476))
    slope = phi + hidden * (0.3989422804014327 * jnp.exp(-0.5 * hidden * hidden))
    return (hidden * phi, slope)


def feed_body(units, table, rows_in, vec, b_in, *refs):
    hidden_out, norm_out, r_out, slope_out, w_in, w_out, sems = refs[4:]
    feature = rows_in.shape[1]
    load = Loader(refs[:2], table, sems)
    waits = [load.wide(units[0] + j, w_in.at[j]) for j in range(4)]
    tail = Loader(refs[2:4], table, sems, load.used).tall(units[1], w_out)
    total = None
    for j in range(4):
        columns = slice(j * feature, (j + 1) * feature)
        wait_all(waits[j])
        hidden = dot_plain(rows_in[...], w_in[j]) + b_in[:, columns]
        active, slope = gelu_parts(hidden)
        r_out[:, columns] = low(active)
        slope_out[:, columns] = low(slope)
    wait_all(tail)
    total = dot_plain(r_out[...], w_out[...]) + vec[0:1, :]
    hidden = rows_in[...].astype(jnp.float32) + total
    hidden_out[...] = hidden
    norm_out[...] = low(layer_norm(hidden, vec[1:2, :], vec[2:3, :]))


def feed_forward(order, rows_in, vec, b_in, w_in, w_out, table, name):
    rows, feature = rows_in.shape
    width = b_in.shape[1]
    return order.kernel(
        functools.partial(feed_body, (w_in[1], w_out[1])),
        [table, rows_in, vec, b_in, *w_in[0], *w_out[0]],
        [SMEM] + [VMEM] * 3 + [ANY] * 4,
        [
            ((rows, feature), jnp.float32, VMEM),
            ((rows, feature), jnp.bfloat16, VMEM),
            ((rows, width), jnp.bfloat16, VMEM),
            ((rows, width), jnp.bfloat16, VMEM),
        ],
        [
            pltpu.VMEM((4, feature, feature), jnp.bfloat16),
            pltpu.VMEM((width, feature), jnp.bfloat16),
            pltpu.SemaphoreType.DMA((64,)),
        ],
        name,
        4 * rows * feature * width,
        8 * feature * width,
    )


def feed_back_out_body(extra, slots, table, *refs):
    refs = list(refs)
    gradient = refs.pop(0)[...].astype(jnp.float32)
    if extra:
        gradient = gradient + refs.pop(0)[...].astype(jnp.float32)
    hidden, gain, active, g_out, sums, keep, upper, lower, stage, out_sems = refs
    feature = hidden.shape[1]
    store = Storer((keep, upper, lower), table, slots, out_sems)
    gradient, grad_gain, grad_shift = layer_norm_back(hidden[...], gain[1:2, :], gradient)
    sums[0:1, :] = jnp.sum(gradient, axis=0, keepdims=True)
    sums[1:2, :] = grad_gain
    sums[2:3, :] = grad_shift
    g_out[...] = gradient
    grad_low = low(gradient)
    for j in range(4):
        columns = slice(j * feature, (j + 1) * feature)
        stage[columns, :] = low(dot_left(active[:, columns], grad_low))
    store.rows(stage, feature // 2, feature // 2, 0)
    store.finish()


def feed_back_out(order, gradients, hidden, gain, active, table, slots, name):
    rows, feature = hidden.shape
    width = active.shape[1]
    return order.kernel(
        functools.partial(feed_back_out_body, len(gradients) == 2, slots),
        [table, *gradients, hidden, gain, active],
        [SMEM] + [VMEM] * (len(gradients) + 3),
        [((rows, feature), jnp.float32, VMEM), ((3, feature), jnp.float32, VMEM), *gradient_outs(feature)],
        [pltpu.VMEM((width, feature), jnp.bfloat16), pltpu.SemaphoreType.DMA((8,))],
        name,
        2 * rows * feature * width,
        4 * feature * width,
    )


def feed_back_in_body(slots, units, table, gradient, slope, rows_in, *refs):
    total_out, bias_in, keep, upper, lower, w_in, w_out, grad_hidden, stage, sems, out_sems = refs[4:]
    feature = rows_in.shape[1]
    tail = Loader(refs[2:4], table, sems).tall(units[1], w_out)
    load = Loader(refs[:2], table, sems, len(tail))
    waits = [load.wide(units[0] + j, w_in.at[j]) for j in range(4)]
    store = Storer((keep, upper, lower), table, slots, out_sems)
    total = gradient[...]
    grad_low = low(total)
    wait_all(tail)
    for j in range(4):
        columns = slice(j * feature, (j + 1) * feature)
        hidden = dot_right(grad_low, w_out[columns, :]) * slope[:, columns].astype(jnp.float32)
        bias_in[j : j + 1, :] = jnp.sum(hidden, axis=0, keepdims=True)
        grad_hidden[:, columns] = low(hidden)
        stage[j] = low(dot_left(rows_in[...], grad_hidden[:, columns]))
        store.rows(stage.at[j], feature // 8, feature // 8, j * (feature // 8))
    for j in range(4):
        columns = slice(j * feature, (j + 1) * feature)
        wait_all(waits[j])
        total = total + dot_right(grad_hidden[:, columns], w_in[j])
    total_out[...] = total
    store.finish()


def feed_back_in(order, gradient, slope, rows_in, w_in, w_out, table, slots, name):
    rows, feature = rows_in.shape
    width = slope.shape[1]
    square = pltpu.VMEM((4, feature, feature), jnp.bfloat16)
    return order.kernel(
        functools.partial(feed_back_in_body, slots, (w_in[1], w_out[1])),
        [table, gradient, slope, rows_in, *w_in[0], *w_out[0]],
        [SMEM] + [VMEM] * 3 + [ANY] * 4,
        [((rows, feature), jnp.float32, VMEM), ((4, feature), jnp.float32, VMEM), *gradient_outs(feature)],
        [
            square,
            pltpu.VMEM((width, feature), jnp.bfloat16),
            pltpu.VMEM((rows, width), jnp.bfloat16),
            square,
            pltpu.SemaphoreType.DMA((64,)),
            pltpu.SemaphoreType.DMA((32,)),
        ],
        name,
        6 * rows * feature * width,
        6 * feature * width,
    )


def attn_back_body(cross, first_unit, others, slots, out_count, table, gradient, *refs):
    refs = list(refs)
    other_sums = [refs.pop(0) for _ in range(others)]
    hidden, gain, q_in = refs[:3]
    refs = refs[3:]
    kv_in = refs.pop(0) if cross else q_in
    queries, keys, values, mixed, probs_in = refs[:5]
    buffers = refs[5:7]
    refs = refs[7:]
    q_grad_out = refs.pop(0)
    kv_grad_out = refs.pop(0) if cross else None
    sums = refs.pop(0)
    grads = [refs.pop(0) for _ in range(out_count)]
    w_q, w_k, w_v, w_o, stage, go, gq, gk, gv, vec_low, sems, out_sems = refs
    rows, feature = hidden.shape
    unit = feature // 8
    load = Loader(buffers, table, sems)
    wait_o = load.wide(first_unit + 3, w_o)
    waits = [load.wide(first_unit + i, w) for i, w in enumerate((w_q, w_k, w_v))]
    store = Storer(grads, table, slots, out_sems)
    lanes = head_lanes(rows)
    total, grad_gain, grad_shift = layer_norm_back(hidden[...], gain[3:4, :], gradient[...])
    sums[2:3, :] = jnp.sum(total, axis=0, keepdims=True)
    sums[3:4, :] = grad_gain
    sums[4:5, :] = grad_shift
    grad_low = low(total)
    stage[3] = low(dot_left(mixed[...], grad_low))
    store.rows(stage.at[3], unit, unit, 3 * unit)
    wait_all(wait_o)
    go[...] = low(dot_right(grad_low, w_o[...]))
    for pair in range(feature // PAIR):
        columns = slice(pair * PAIR, (pair + 1) * PAIR)
        q_pair, k_pair, v_pair = queries[:, columns], keys[:, columns], values[:, columns]
        go_pair = go[:, columns]
        parts = []
        for half in range(2):
            mine = lanes if half == 0 else ~lanes
            probs_low = probs_in[2 * pair + half]
            probs = probs_low.astype(jnp.float32)
            grad_probs = dot_right(jnp.where(mine, go_pair, jnp.zeros_like(go_pair)), v_pair)
            weighted = grad_probs * probs
            row_sum = jnp.sum(weighted, axis=-1, keepdims=True)
            grad_raw = low((weighted - probs * row_sum) * SCORE_SCALE)
            parts.append(
                (
                    dot_plain(grad_raw, k_pair),
                    dot_left(grad_raw, q_pair),
                    dot_left(probs_low, go_pair),
                )
            )
        grad_q, grad_k, grad_v = (jnp.where(lanes, a, b) for a, b in zip(*parts))
        sums[0:1, columns] = jnp.sum(grad_q, axis=0, keepdims=True)
        sums[1:2, columns] = jnp.sum(grad_v, axis=0, keepdims=True)
        gq[:, columns] = low(grad_q)
        gk[:, columns] = low(grad_k)
        gv[:, columns] = low(grad_v)
    if others:
        parts = [sums[...]] + [other[...] for other in other_sums]
        count = sum(part.shape[0] for part in parts)
        parts.append(jnp.zeros((vec_low.shape[0] - count, feature), jnp.float32))
        vec_low[...] = low(jnp.concatenate(parts, axis=0))
        store.tail(vec_low)
    for index, (source, grad) in enumerate(((q_in, gq), (kv_in, gk), (kv_in, gv))):
        stage[index] = low(dot_left(source[...], grad[...]))
        store.rows(stage.at[index], unit, unit, index * unit)
    for copies in waits:
        wait_all(copies)
    total = total + dot_right(gq[...], w_q[...])
    kv_total = dot_right(gk[...], w_k[...]) + dot_right(gv[...], w_v[...])
    if cross:
        q_grad_out[...] = total
        kv_grad_out[...] = kv_total
    else:
        q_grad_out[...] = total + kv_total
    store.finish()


def attn_back(
    order, gradient, hidden, gain, q_in, kv_in, saved, weights, table, others, slots, name, single=False
):
    rows, feature = hidden.shape
    cross = kv_in is not None
    sources = [gradient, *others, hidden, gain, q_in] + ([kv_in] if cross else []) + list(saved)
    count = tile_up(5 + sum(other.shape[0] for other in others)) if others else 0
    return order.kernel(
        functools.partial(attn_back_body, cross, weights[1], len(others), slots, 2 if single else 3),
        [table, *sources, *weights[0]],
        [SMEM] + [VMEM] * len(sources) + [ANY] * 2,
        [((rows, feature), jnp.float32, VMEM)] * (1 + cross)
        + [((5, feature), jnp.float32, VMEM), *gradient_outs(feature, count, single)],
        [pltpu.VMEM((feature, feature), jnp.bfloat16)] * 4
        + [pltpu.VMEM((4, feature, feature), jnp.bfloat16)]
        + [pltpu.VMEM((rows, feature), jnp.bfloat16)] * 4
        + [pltpu.VMEM((max(count, ROW_TILE), feature), jnp.bfloat16)]
        + [pltpu.SemaphoreType.DMA((32,)), pltpu.SemaphoreType.DMA((34,))],
        name,
        16 * rows * feature * feature,
        20 * feature * feature,
    )


def combine_body(plan, count, *refs):
    inputs = refs[:count]
    outs = refs[count:-4]
    landed, summed, in_sems, out_sems = refs[-4:]
    loads = []
    place = 0
    for out, first, rows, terms in plan:
        parts = []
        for source, row in terms:
            copy = pltpu.make_async_copy(
                inputs[source].at[pl.ds(row, rows), :],
                landed.at[pl.ds(place, rows), :],
                in_sems.at[sum(len(other) for other in loads) + len(parts)],
            )
            copy.start()
            parts.append((copy, place))
            place += rows
        loads.append(parts)
    stores = []
    place = 0
    for (out, first, rows, terms), parts in zip(plan, loads):
        total = None
        for copy, start in parts:
            copy.wait()
            term = landed[start : start + rows, :].astype(jnp.float32)
            total = term if total is None else total + term
        summed[place : place + rows, :] = low(total)
        copy = pltpu.make_async_copy(
            summed.at[pl.ds(place, rows), :],
            outs[out].at[pl.ds(first, rows), :],
            out_sems.at[len(stores)],
        )
        copy.start()
        stores.append(copy)
        place += rows
    wait_all(stores)


def combine(order, name, *jobs):
    inputs, plan, outs = [], [], []
    for sizes, sums, use in jobs:
        for out, first, rows, terms in sums:
            places = []
            for array, row in terms:
                known = [index for index, other in enumerate(inputs) if other is array]
                if not known:
                    inputs.append(array)
                places.append((known[0] if known else len(inputs) - 1, row))
            plan.append((len(outs) + out, first, rows, tuple(places)))
        outs += sizes
    feature = inputs[0].shape[1]
    reads = sum(rows * len(terms) for out, first, rows, terms in plan)
    writes = sum(rows for out, first, rows, terms in plan)
    results = order.kernel(
        functools.partial(combine_body, plan, len(inputs)),
        inputs,
        [ANY] * len(inputs),
        [((rows, feature), jnp.bfloat16, ANY) for rows in outs],
        [
            pltpu.VMEM((reads, feature), jnp.bfloat16),
            pltpu.VMEM((writes, feature), jnp.bfloat16),
            pltpu.SemaphoreType.DMA((sum(len(terms) for out, first, rows, terms in plan),)),
            pltpu.SemaphoreType.DMA((len(plan),)),
        ],
        name,
    )
    for sizes, sums, use in jobs:
        use(*results[: len(sizes)])
        results = results[len(sizes) :]


OWN, X, Y, DIAGONAL = range(4)
X_FIRST = (OWN, Y, X, DIAGONAL)
Y_FIRST = (OWN, X, Y, DIAGONAL)


class Reduce:
    def __init__(self, order, outs, slots, both=False, pad=0):
        self.order = order
        self.pad = pad
        self.keep, self.upper, self.lower = outs if len(outs) == 3 else (outs[0], None, outs[1])
        self.both = both
        self.bits = (2, 4) if slots == X_FIRST else (4, 2)
        self.rows = self.keep.shape[1] // 2
        self.extra = self.keep.shape[0] - 4 * self.rows

    def cores(self):
        self.from_upper = None if self.upper is None else swap(self.order.tie(self.upper), 1)
        self.from_lower = swap(self.order.tie(self.lower), 1)

    def cores_done(self):
        self.order.mark(*(value for value in (self.from_upper, self.from_lower) if value is not None))

    def block(self, slot, first=0):
        row = slot * self.rows + first
        other = (self.from_lower, row) if slot < 2 or self.upper is None else (self.from_upper, row - 2 * self.rows)
        return ((self.keep, row), other)

    def extra_rows(self):
        return ((self.keep, 4 * self.rows), (self.from_lower, (4 if self.upper is None else 2) * self.rows))

    def first(self):
        rows, extra = self.rows, self.extra
        if not self.both:
            plan = [(0, 0, rows, self.block(2)), (0, rows, rows, self.block(3))]
            if extra:
                plan.append((0, 2 * rows, extra, self.extra_rows()))
            if self.pad:
                plan.append((0, 2 * rows + extra, self.pad, self.block(2)[:1]))
            return ([2 * rows + extra + self.pad], plan, self.first_sent)
        cut = rows // 2
        plan = [(0, 0, cut, self.block(3)), (1, 0, cut, self.block(3, cut))]
        if extra:
            plan.append((0, cut, extra, self.extra_rows()))
        return ([cut + extra, cut], plan, self.first_sent)

    def first_sent(self, *sent):
        self.sent = sent[0]
        self.landed = [swap(value, bit) for value, bit in zip(sent, (2, 4) if self.both else self.bits)]

    def second(self):
        rows, extra = self.rows, self.extra
        if not self.both:
            landed = self.landed[0]
            plan = [(0, 0, rows, self.block(1) + ((landed, rows),))]
            if extra:
                plan.append((0, rows, extra, ((self.sent, 2 * rows), (landed, 2 * rows))))
            return ([rows + extra], plan, self.second_sent)
        cut = rows // 2
        from_x, from_y = self.landed
        plan = [
            (0, 0, cut, self.block(1)),
            (0, cut, cut, self.block(1, cut) + ((from_y, 0),)),
            (1, 0, cut, self.block(2) + ((from_x, 0),)),
            (1, cut, cut, self.block(2, cut)),
        ]
        if extra:
            plan.append((1, rows, extra, ((self.sent, cut), (from_x, cut))))
        return ([rows, rows + extra], plan, self.second_sent)

    def second_sent(self, *sent):
        self.sent_last = sent[-1]
        self.last = [swap(value, bit) for value, bit in zip(sent, (2, 4) if self.both else self.bits[1:])]

    def own(self, use):
        rows, extra = self.rows, self.extra
        terms = self.block(0) + tuple((value, 0) for value in self.last)
        if not self.both:
            terms += ((self.landed[0], 0),)
        plan = [(0, 0, rows, terms)]
        if extra:
            plan.append((0, rows, extra, ((self.sent_last, rows), (self.last[-1], rows))))
        return ([rows + extra], plan, use)


def own_stack(pieces, use):
    rows = pieces[0].rows
    plan = [(0, index * rows) + piece.own(None)[1][0][2:] for index, piece in enumerate(pieces)]
    return ([len(pieces) * rows], plan, use)


class Line:
    def __init__(self, value):
        self.value = value
        self.landed = lax.ppermute(value, "rep", [(0, 1), (3, 2)])

    def part(self, first):
        return (self, first)

    def step(self, use):
        rows = self.value.shape[0]
        return ([rows], [(0, 0, rows, ((self.value, 0), (self.landed, 0)))], use)

    def middle(self):
        return self.step(self.middle_sent)

    def middle_sent(self, value):
        self.value = value
        self.landed = lax.ppermute(value, "rep", [(1, 2), (2, 1)])

    def outward(self):
        return self.step(self.outward_sent)

    def outward_sent(self, value):
        self.value = value
        self.landed = lax.ppermute(value, "rep", [(1, 0), (2, 3)])


def finish_body(parts, inner, *refs):
    wide, rest = refs[2 * len(parts)], list(refs[2 * len(parts) + 1 :])
    feature = refs[0].shape[1]
    unit = feature // 8
    for index, first in enumerate(parts):
        value, landed = refs[2 * index], refs[2 * index + 1]

        def rows(begin, count):
            mine = value[first + begin : first + begin + count, :].astype(jnp.float32)
            other = landed[first + begin : first + begin + count, :].astype(jnp.float32)
            return jnp.where(inner[0] == 1, mine, other)

        for j in range(4):
            column = (4 * index + j) * feature
            if wide.shape[0] == unit:
                wide[:, column : column + feature] = rows(j * unit, unit)
            else:
                wide[j * unit : (j + 1) * unit, :] = rows(j * unit, unit)
        if first == 0 and value.shape[0] % (4 * unit):
            rest.pop(0)[...] = rows(4 * unit, value.shape[0] - 4 * unit)


def finish(order, inner, parts, wide, name):
    operands = [inner]
    for line, first in parts:
        operands += [line.value, line.landed]
    feature = operands[1].shape[1]
    unit = feature // 8
    shape = (unit, 4 * feature * len(parts)) if wide else (4 * unit, feature)
    outs = [(shape, jnp.float32, VMEM)]
    for line, first in parts:
        rows = line.value.shape[0] % (4 * unit)
        if rows:
            outs.append(((rows, feature), jnp.float32, VMEM))
    return order.kernel(
        functools.partial(finish_body, [first for line, first in parts]),
        operands,
        [SMEM] + [VMEM] * (len(operands) - 1),
        outs,
        [],
        name,
    )


def per_device(
    enc_in,
    dec_in,
    bucket,
    enc_lengths,
    dec_lengths,
    enc_attn,
    enc_vec,
    enc_w1,
    enc_w2,
    dec_attn,
    dec_vec,
    dec_w1,
    dec_w2,
    enc_cot,
    dec_cot,
):
    feature = enc_in.shape[1]
    unit = feature // 8
    chip_index = lax.axis_index("fsdp").astype(jnp.int32)
    table = chip_index ^ jnp.arange(8, dtype=jnp.int32)
    place = lax.axis_index("rep")
    inner = ((place == 1) | (place == 2)).astype(jnp.int32).reshape(1)
    ids = (table, bucket)
    order = Order()
    mark = order.mark
    g_1, g_2, g_3, g_4 = (Gather(order, feature, "piece_" + name) for name in "1234")
    half = 4 * unit
    e_len, d_len = enc_vec.shape[0], dec_vec.shape[0]
    vec_part = vec_shards([enc_vec, dec_vec], chip_index, feature)
    g_1.sides(enc_attn, dec_attn[:, : 4 * feature], vec_part)
    g_2.sides(enc_w1, enc_w2)
    g_1.corners()
    g_2.corners()
    mark(*g_2.mine[3:])
    (attn_pair,) = g_1.join((0, 2 * half + vec_part.shape[0]))
    (e_feed,) = g_2.join((0, 2 * half))
    g_3.sides(dec_attn[:, 4 * feature :], dec_w1)
    e_attn_vec, e_feed_vec, e_tail, d_self_vec, d_cross_vec, d_feed_vec, d_tail = gathered_vecs(
        order, attn_pair, table, vec_part.shape[0], feature, (e_len, d_len), ((5, 3), (5, 5, 3))
    )
    e_hid_a, e_first, *e_saved = attn_forward(
        order, enc_in, None, e_attn_vec, (attn_pair, 0), ids, enc_lengths, False, "enc_attn"
    )
    mark(e_feed[1])
    g_4.sides(dec_w2)
    d_hid_s, d_first, *s_saved = attn_forward(
        order, dec_in, None, d_self_vec, (attn_pair, 4), ids, dec_lengths, True, "dec_self"
    )
    g_3.corners()
    e_hid_f, encoded, e_act, e_slope = feed_forward(
        order, e_first, e_feed_vec, e_tail, (e_feed, 0), (e_feed, 4), table, "enc_feed"
    )
    g_4.corners()
    cross_pair, w1_pair = g_3.join((0, half), (half, half))
    (w2_pair,) = g_4.join((0, half))
    d_hid_c, d_second, *c_saved = attn_forward(
        order, d_first, encoded, d_cross_vec, (cross_pair, 0), ids, enc_lengths, False, "dec_cross"
    )
    d_hid_f, decoded, d_act, d_slope = feed_forward(
        order, d_second, d_feed_vec, d_tail, (w1_pair, 0), (w2_pair, 0), table, "dec_feed"
    )
    gradient, d_sums_f, *outs = feed_back_out(
        order, [dec_cot], d_hid_f, d_feed_vec, d_act, table, X_FIRST, "dec_back_out"
    )
    red_0 = Reduce(order, outs, X_FIRST)
    red_0.cores()
    gradient, d_bias, *outs = feed_back_in(
        order, gradient, d_slope, d_second, (w1_pair, 0), (w2_pair, 0), table, Y_FIRST, "dec_back_in"
    )
    red_1 = Reduce(order, outs, Y_FIRST)
    red_0.cores_done()
    combine(order, "add_1", red_0.first())
    red_1.cores()
    gradient, grad_encoded, d_sums_c, *outs = attn_back(
        order, gradient, d_hid_c, d_cross_vec, d_first, encoded, c_saved, (cross_pair, 0), table, [],
        X_FIRST, "cross_back",
    )
    red_2 = Reduce(order, outs, X_FIRST)
    red_1.cores_done()
    combine(order, "add_2", red_1.first())
    red_2.cores()
    e_gradient, e_sums_f, *outs = feed_back_out(
        order, [enc_cot, grad_encoded], e_hid_f, e_feed_vec, e_act, table, Y_FIRST, "enc_back_out"
    )
    red_3 = Reduce(order, outs, Y_FIRST, pad=2 * ROW_TILE)
    combine(order, "add_3a", red_0.second())
    red_2.cores_done()
    combine(order, "add_3b", red_2.first())
    red_3.cores()
    e_gradient, e_bias, *outs = feed_back_in(
        order, e_gradient, e_slope, e_first, (e_feed, 0), (e_feed, 4), table, X_FIRST, "enc_back_in"
    )
    red_4 = Reduce(order, outs, X_FIRST)
    totals = {}

    def keep_as(key):
        return lambda value: totals.update({key: value})

    mark(*red_0.last)
    combine(order, "add_4a", red_1.second())
    red_3.cores_done()
    combine(order, "add_4b", red_3.first())
    red_4.cores()
    dec_in_grad, d_sums_s, *outs = attn_back(
        order, gradient, d_hid_s, d_self_vec, dec_in, None, s_saved, (attn_pair, 4), table,
        [d_sums_c, d_sums_f, d_bias], Y_FIRST, "self_back",
    )
    red_5 = Reduce(order, outs, Y_FIRST, True)
    combine(order, "add_5a", red_2.second())
    mark(*red_1.last)
    red_4.cores_done()
    combine(order, "add_5b", red_4.first())
    red_5.cores()
    enc_in_grad, e_sums_a, *outs = attn_back(
        order, e_gradient, e_hid_a, e_attn_vec, enc_in, None, e_saved, (attn_pair, 0), table,
        [e_sums_f, e_bias], Y_FIRST, "enc_attn_back", True,
    )
    red_6 = Reduce(order, outs, Y_FIRST, True)
    red_5.cores_done()
    mark(*red_2.last)
    combine(
        order, "add_6a", red_3.second(), red_4.second(), own_stack([red_0, red_1], keep_as("a"))
    )
    line_a = Line(totals["a"])
    red_6.cores()
    red_6.cores_done()
    combine(
        order, "add_6b", red_5.first(), red_6.first(), own_stack([red_2, red_3], keep_as("b")),
        red_4.own(keep_as(4)),
    )
    combine(order, "add_7", line_a.middle())
    mark(*red_6.landed)
    combine(order, "add_8", red_5.second())
    line_b = Line(order.tie(totals["b"]))
    line_4 = Line(order.tie(totals[4]))
    combine(order, "add_9", red_6.second(), red_5.own(keep_as(5)), line_a.outward())
    combine(order, "add_10", line_b.middle())
    combine(order, "add_11", red_6.own(keep_as(6)), line_4.middle())
    line_5 = Line(order.tie(totals[5]))
    line_6 = Line(totals[6])
    mark(line_a.landed)
    combine(order, "add_12", line_b.outward())
    (grad_d_w2,) = finish(order, inner, [line_a.part(0)], False, "out_0")
    (grad_d_w1,) = finish(order, inner, [line_a.part(half)], True, "out_1")
    combine(order, "add_13", line_4.outward(), line_5.middle(), line_6.middle())
    mark(line_b.landed)
    combine(order, "add_14", line_5.outward())
    (grad_e_w2,) = finish(order, inner, [line_b.part(half)], False, "out_3")
    (grad_e_w1,) = finish(order, inner, [line_4.part(0)], True, "out_4")
    combine(order, "add_15", line_6.outward())
    grad_d_attn, d_vec = finish(order, inner, [line_5.part(0), line_b.part(0)], True, "out_5")
    grad_e_attn, e_vec = finish(order, inner, [line_6.part(0)], True, "out_6")

    def own_part(rows, length):
        return lax.dynamic_slice(rows.reshape(-1), (chip_index * length,), (length,))

    return (
        encoded,
        decoded,
        enc_in_grad,
        dec_in_grad,
        grad_e_attn,
        own_part(e_vec, e_len),
        grad_e_w1,
        grad_e_w2,
        grad_d_attn,
        own_part(d_vec, d_len),
        grad_d_w1,
        grad_d_w2,
    )


def solution(mesh):
    in_specs = (
        P(("rep", "fsdp"), None),
        P(("rep", "fsdp"), None),
        P(("rep", "fsdp")),
        P(("rep", "fsdp"), None),
        P(("rep", "fsdp"), None),
        P("fsdp", None),
        P("fsdp"),
        P("fsdp", None),
        P("fsdp", None),
        P("fsdp", None),
        P("fsdp"),
        P("fsdp", None),
        P("fsdp", None),
        P(("rep", "fsdp"), None),
        P(("rep", "fsdp"), None),
    )
    out_specs = (
        P(("rep", "fsdp"), None),
        P(("rep", "fsdp"), None),
        P(("rep", "fsdp"), None),
        P(("rep", "fsdp"), None),
        P("fsdp", None),
        P("fsdp"),
        P("fsdp", None),
        P("fsdp", None),
        P("fsdp", None),
        P("fsdp"),
        P("fsdp", None),
        P("fsdp", None),
    )
    small = mesh.shape["fsdp"] == 8 and mesh.shape["rep"] == 4
    return jax.shard_map(
        per_device if small else per_device_any, mesh=mesh, in_specs=in_specs, out_specs=out_specs, check_vma=False
    )
```

```python
import functools

import jax
import jax.numpy as jnp
from jax import lax
from jax.experimental import pallas as pl
from jax.experimental.pallas import tpu as pltpu
from jax.sharding import PartitionSpec as P

HEAD = 64
PAIR = 2 * HEAD
ROW_TILE = 16
VMEM_BYTES = 56 * 1024 * 1024
SMALL_VMEM_BYTES = 20 * 1024 * 1024
MIDDLE_VMEM_BYTES = 44 * 1024 * 1024
WIDE = ("add_6a", "add_6b", "add_6c", "add_8", "add_9")
MIDDLE = ('enc_attn', 'dec_self', 'cross_back', 'enc_back_out', 'self_back')
ANY = pl.BlockSpec(memory_space=pl.ANY)
SMEM = pl.BlockSpec(memory_space=pltpu.SMEM)
VMEM = pl.BlockSpec(memory_space=pltpu.VMEM)


EPSILON = 1e-05
NEG_FILL = -1e30
SCORE_SCALE = 0.125


def norm_rows(hidden, gain_row, shift_row):
    row_mean = jnp.mean(hidden, axis=-1, keepdims=True)
    centred = hidden - row_mean
    variance = jnp.mean(centred * centred, axis=-1, keepdims=True)
    return centred * lax.rsqrt(variance + EPSILON) * gain_row + shift_row


def norm_back(hidden, gain_row, shift_row, gradient):
    unused, pullback = jax.vjp(norm_rows, hidden, gain_row, shift_row)
    return pullback(gradient)


def gelu_exact(hidden):
    return jax.nn.gelu(hidden, approximate=False)


def dot_plain(first_op, second_op):
    return jnp.dot(first_op, second_op, preferred_element_type=jnp.float32)


def dot_left(first_op, second_op):
    return lax.dot_general(
        first_op, second_op, (((0,), (0,)), ((), ())), preferred_element_type=jnp.float32
    )


def dot_right(first_op, second_op):
    return lax.dot_general(
        first_op, second_op, (((1,), (1,)), ((), ())), preferred_element_type=jnp.float32
    )


def build_masks(one_long, enc_len, dec_len, row_total, seg_count):
    span_rows = jnp.where(one_long == 1, row_total, row_total // seg_count).astype(jnp.int32)
    row_index = jnp.arange(row_total, dtype=jnp.int32)
    group_id = row_index // span_rows
    row_place = row_index - group_id * span_rows
    in_group = group_id[:, None] == jnp.arange(seg_count, dtype=jnp.int32)[None, :]
    enc_live = row_place < jnp.sum(jnp.where(in_group, enc_len[None, :], 0), axis=1)
    dec_live = row_place < jnp.sum(jnp.where(in_group, dec_len[None, :], 0), axis=1)
    same_group = group_id[:, None] == group_id[None, :]
    enc_mask = same_group & enc_live[None, :]
    self_mask = same_group & dec_live[None, :] & (row_index[None, :] <= row_index[:, None])
    return (enc_mask, self_mask, enc_mask)


def unpack(vector, row_count, feature):
    rows_part = vector[: row_count * feature].astype(jnp.float32).reshape(row_count, feature)
    return (rows_part, vector[row_count * feature :].astype(jnp.float32))


def fetch(attn_rows, vec_part, w_in, w_out):
    return (
        lax.all_gather(attn_rows, "fsdp", axis=0, tiled=True),
        lax.all_gather(vec_part, "fsdp", axis=0, tiled=True),
        lax.all_gather(w_in, "fsdp", axis=0, tiled=True),
        lax.all_gather(w_out, "fsdp", axis=0, tiled=True),
    )


def fetch_again(attn_rows, vec_part, w_in, w_out):
    return (
        lax.all_gather(attn_rows, "fsdp", axis=0, tiled=True),
        lax.all_gather(vec_part, "fsdp", axis=0, tiled=True),
        lax.all_gather(w_in, "fsdp", axis=0, tiled=True),
        lax.all_gather(w_out, "fsdp", axis=0, tiled=True),
    )


def reduce_grads(grad_attn, grad_vec, grad_in, grad_out):
    shard = (
        lax.psum_scatter(
            grad_attn.astype(jnp.bfloat16), "fsdp", scatter_dimension=0, tiled=True
        ).astype(jnp.float32),
        lax.psum_scatter(
            grad_vec.astype(jnp.bfloat16), "fsdp", scatter_dimension=0, tiled=True
        ).astype(jnp.float32),
        lax.psum_scatter(
            grad_in.astype(jnp.bfloat16), "fsdp", scatter_dimension=0, tiled=True
        ).astype(jnp.float32),
        lax.psum_scatter(
            grad_out.astype(jnp.bfloat16), "fsdp", scatter_dimension=0, tiled=True
        ).astype(jnp.float32),
    )
    return (
        lax.psum(shard[0].astype(jnp.bfloat16), "rep").astype(jnp.float32),
        lax.psum(shard[1].astype(jnp.bfloat16), "rep").astype(jnp.float32),
        lax.psum(shard[2].astype(jnp.bfloat16), "rep").astype(jnp.float32),
        lax.psum(shard[3].astype(jnp.bfloat16), "rep").astype(jnp.float32),
    )


def attend(q_in, kv_in, weights, biases, key_mask, one_source):
    row_total, feature = q_in.shape
    head_count = feature // HEAD
    if one_source:
        packed = dot_plain(q_in, weights[:, : 3 * feature])
        q_pre = packed[:, :feature]
        k_pre = packed[:, feature : 2 * feature]
        v_pre = packed[:, 2 * feature :]
    else:
        q_pre = dot_plain(q_in, weights[:, :feature])
        packed = dot_plain(kv_in, weights[:, feature : 3 * feature])
        k_pre = packed[:, :feature]
        v_pre = packed[:, feature:]
    queries = (q_pre + biases[0]).astype(jnp.bfloat16).reshape(row_total, head_count, HEAD)
    keys_low = k_pre.astype(jnp.bfloat16).reshape(row_total, head_count, HEAD)
    values = (v_pre + biases[1]).astype(jnp.bfloat16).reshape(row_total, head_count, HEAD)
    raw_score = jnp.einsum("qhd,khd->hqk", queries, keys_low, preferred_element_type=jnp.float32)
    probs = jax.nn.softmax(jnp.where(key_mask[None], raw_score * SCORE_SCALE, NEG_FILL), axis=-1)
    probs_low = probs.astype(jnp.bfloat16)
    mixed = jnp.einsum("hqk,khd->qhd", probs_low, values, preferred_element_type=jnp.float32)
    mixed = mixed.reshape(row_total, feature).astype(jnp.bfloat16)
    branch = dot_plain(mixed, weights[:, 3 * feature :]) + biases[2]
    return (branch, (queries, keys_low, values, probs, probs_low, mixed))


def attend_back(gradient, q_in, kv_in, weights, saved, one_source):
    queries, keys_low, values, probs, probs_low, mixed = saved
    row_total, feature = q_in.shape
    head_count = feature // HEAD
    grad_bias_o = jnp.sum(gradient, axis=0)
    grad_low = gradient.astype(jnp.bfloat16)
    grad_w_o = dot_left(mixed, grad_low)
    grad_mixed = dot_right(grad_low, weights[:, 3 * feature :]).astype(jnp.bfloat16)
    grad_mixed = grad_mixed.reshape(row_total, head_count, HEAD)
    grad_probs = jnp.einsum("qhd,khd->hqk", grad_mixed, values, preferred_element_type=jnp.float32)
    grad_values = jnp.einsum(
        "hqk,qhd->khd", probs_low, grad_mixed, preferred_element_type=jnp.float32
    )
    grad_score = probs * (grad_probs - jnp.sum(grad_probs * probs, axis=-1, keepdims=True))
    grad_raw = (grad_score * SCORE_SCALE).astype(jnp.bfloat16)
    grad_query = jnp.einsum(
        "hqk,khd->qhd", grad_raw, keys_low, preferred_element_type=jnp.float32
    ).reshape(row_total, feature)
    grad_keys = jnp.einsum(
        "hqk,qhd->khd", grad_raw, queries, preferred_element_type=jnp.float32
    ).reshape(row_total, feature)
    grad_values = grad_values.reshape(row_total, feature)
    grad_bias_q = jnp.sum(grad_query, axis=0)
    grad_bias_v = jnp.sum(grad_values, axis=0)
    low_query = grad_query.astype(jnp.bfloat16)
    low_kv = jnp.concatenate(
        [grad_keys.astype(jnp.bfloat16), grad_values.astype(jnp.bfloat16)], axis=1
    )
    if one_source:
        packed = jnp.concatenate([low_query, low_kv], axis=1)
        grad_weights = jnp.concatenate([dot_left(q_in, packed), grad_w_o], axis=1)
        grad_q_in = dot_right(packed, weights[:, : 3 * feature])
        grad_kv_in = grad_q_in
    else:
        grad_weights = jnp.concatenate(
            [dot_left(q_in, low_query), dot_left(kv_in, low_kv), grad_w_o], axis=1
        )
        grad_q_in = dot_right(low_query, weights[:, :feature])
        grad_kv_in = dot_right(low_kv, weights[:, feature : 3 * feature])
    return (grad_q_in, grad_kv_in, grad_weights, (grad_bias_q, grad_bias_v, grad_bias_o))


def feed(rows_in, w_in, b_in, w_out, b_out):
    hidden = dot_plain(rows_in, w_in) + b_in
    active = gelu_exact(hidden).astype(jnp.bfloat16)
    return (dot_plain(active, w_out) + b_out, (hidden, active))


def feed_back(gradient, rows_in, w_in, w_out, saved):
    hidden, active = saved
    grad_b_out = jnp.sum(gradient, axis=0)
    grad_low = gradient.astype(jnp.bfloat16)
    grad_w_out = dot_left(active, grad_low)
    grad_active = dot_right(grad_low, w_out)
    unused, pullback = jax.vjp(gelu_exact, hidden)
    grad_hidden = pullback(grad_active)[0]
    grad_b_in = jnp.sum(grad_hidden, axis=0)
    hidden_low = grad_hidden.astype(jnp.bfloat16)
    grad_w_in = dot_left(rows_in, hidden_low)
    grad_rows = dot_right(hidden_low, w_in)
    return (grad_rows, grad_w_in, grad_b_in, grad_w_out, grad_b_out)


def per_device_any(
    enc_in,
    dec_in,
    bucket,
    enc_lengths,
    dec_lengths,
    enc_attn,
    enc_vec,
    enc_w1,
    enc_w2,
    dec_attn,
    dec_vec,
    dec_w1,
    dec_w2,
    enc_cot,
    dec_cot,
):
    row_total, feature = enc_in.shape
    enc_mask, self_mask, cross_mask = build_masks(
        bucket[0], enc_lengths[0], dec_lengths[0], row_total, enc_lengths.shape[1]
    )
    enc_weights = fetch(enc_attn, enc_vec, enc_w1, enc_w2)
    e_attn, e_vec, e_in, e_out = enc_weights
    e_rows, e_tail = unpack(e_vec, 8, feature)
    branch, e_saved_a = attend(enc_in, enc_in, e_attn, e_rows[0:3], enc_mask, True)
    e_hid_a = enc_in.astype(jnp.float32) + branch
    e_first = norm_rows(e_hid_a, e_rows[3], e_rows[4]).astype(jnp.bfloat16)
    branch, e_saved_f = feed(e_first, e_in, e_tail, e_out, e_rows[5])
    e_hid_f = e_first.astype(jnp.float32) + branch
    encoded = norm_rows(e_hid_f, e_rows[6], e_rows[7]).astype(jnp.bfloat16)
    dec_weights = fetch(dec_attn, dec_vec, dec_w1, dec_w2)
    d_attn, d_vec, d_in, d_out = dec_weights
    d_rows, d_tail = unpack(d_vec, 13, feature)
    branch, d_saved_s = attend(
        dec_in, dec_in, d_attn[:, : 4 * feature], d_rows[0:3], self_mask, True
    )
    d_hid_s = dec_in.astype(jnp.float32) + branch
    d_first = norm_rows(d_hid_s, d_rows[3], d_rows[4]).astype(jnp.bfloat16)
    branch, d_saved_c = attend(
        d_first, encoded, d_attn[:, 4 * feature :], d_rows[5:8], cross_mask, False
    )
    d_hid_c = d_first.astype(jnp.float32) + branch
    d_second = norm_rows(d_hid_c, d_rows[8], d_rows[9]).astype(jnp.bfloat16)
    branch, d_saved_f = feed(d_second, d_in, d_tail, d_out, d_rows[10])
    d_hid_f = d_second.astype(jnp.float32) + branch
    decoded = norm_rows(d_hid_f, d_rows[11], d_rows[12]).astype(jnp.bfloat16)
    dec_weights = fetch_again(dec_attn, dec_vec, dec_w1, dec_w2)
    d_attn, d_vec, d_in, d_out = dec_weights
    d_rows, d_tail = unpack(d_vec, 13, feature)
    gradient, grad_g11, grad_n12 = norm_back(
        d_hid_f, d_rows[11], d_rows[12], dec_cot.astype(jnp.float32)
    )
    grad_rows, grad_d_in, grad_d_tail, grad_d_out, grad_b10 = feed_back(
        gradient, d_second, d_in, d_out, d_saved_f
    )
    gradient, grad_g8, grad_n9 = norm_back(d_hid_c, d_rows[8], d_rows[9], gradient + grad_rows)
    grad_q_in, grad_encoded, grad_cross, cross_bias = attend_back(
        gradient, d_first, encoded, d_attn[:, 4 * feature :], d_saved_c, False
    )
    gradient, grad_g3, grad_n4 = norm_back(d_hid_s, d_rows[3], d_rows[4], gradient + grad_q_in)
    grad_self_in, unused, grad_self, self_bias = attend_back(
        gradient, dec_in, dec_in, d_attn[:, : 4 * feature], d_saved_s, True
    )
    dec_in_grad = gradient + grad_self_in
    dec_stack = jnp.stack(
        [
            self_bias[0],
            self_bias[1],
            self_bias[2],
            grad_g3,
            grad_n4,
            cross_bias[0],
            cross_bias[1],
            cross_bias[2],
            grad_g8,
            grad_n9,
            grad_b10,
            grad_g11,
            grad_n12,
        ]
    )
    dec_vec_full = jnp.concatenate([dec_stack.reshape(-1), grad_d_tail])
    dec_shards = reduce_grads(
        jnp.concatenate([grad_self, grad_cross], axis=1), dec_vec_full, grad_d_in, grad_d_out
    )
    enc_weights = fetch_again(enc_attn, enc_vec, enc_w1, enc_w2)
    e_attn, e_vec, e_in, e_out = enc_weights
    e_rows, e_tail = unpack(e_vec, 8, feature)
    gradient, grad_g6, grad_n7 = norm_back(
        e_hid_f, e_rows[6], e_rows[7], enc_cot.astype(jnp.float32) + grad_encoded
    )
    grad_rows, grad_e_in, grad_e_tail, grad_e_out, grad_b5 = feed_back(
        gradient, e_first, e_in, e_out, e_saved_f
    )
    gradient, grad_g3e, grad_n4e = norm_back(e_hid_a, e_rows[3], e_rows[4], gradient + grad_rows)
    grad_self_in, unused, grad_e_attn, enc_bias = attend_back(
        gradient, enc_in, enc_in, e_attn, e_saved_a, True
    )
    enc_in_grad = gradient + grad_self_in
    enc_stack = jnp.stack(
        [enc_bias[0], enc_bias[1], enc_bias[2], grad_g3e, grad_n4e, grad_b5, grad_g6, grad_n7]
    )
    enc_vec_full = jnp.concatenate([enc_stack.reshape(-1), grad_e_tail])
    enc_shards = reduce_grads(grad_e_attn, enc_vec_full, grad_e_in, grad_e_out)
    return (
        encoded,
        decoded,
        enc_in_grad,
        dec_in_grad,
        enc_shards[0],
        enc_shards[1],
        enc_shards[2],
        enc_shards[3],
        dec_shards[0],
        dec_shards[1],
        dec_shards[2],
        dec_shards[3],
    )


def swap(value, bit):
    return lax.ppermute(value, "fsdp", [(i, i ^ bit) for i in range(8)])


def add_low(*terms):
    total = terms[0].astype(jnp.float32)
    for term in terms[1:]:
        total = total + term.astype(jnp.float32)
    return total.astype(jnp.bfloat16)


def tile_up(rows):
    return -(-rows // ROW_TILE) * ROW_TILE


def size_of(shape):
    total = 1
    for extent in shape:
        total *= extent
    return total


class Order:
    def __init__(self):
        self.token = None
        self.waits = []

    def mark(self, *values):
        self.waits += values

    def tie(self, value):
        if self.token is None:
            return value
        value, self.token = lax.optimization_barrier((value, self.token))
        return value

    def kernel(self, body, operands, specs, outs, scratch, name, flops=0, moved=0):
        extra = self.waits + ([] if self.token is None else [self.token])
        self.waits = []
        count, skip = len(operands), len(extra)
        grant = SMALL_VMEM_BYTES if not flops and name not in WIDE else MIDDLE_VMEM_BYTES if name in MIDDLE else VMEM_BYTES
        results = pl.pallas_call(
            lambda *refs: body(*refs[:count], *refs[count + skip :]),
            out_shape=[jax.ShapeDtypeStruct(shape, dtype) for shape, dtype, spec in outs],
            in_specs=list(specs) + [ANY] * skip,
            out_specs=[spec for shape, dtype, spec in outs],
            scratch_shapes=scratch,
            compiler_params=pltpu.CompilerParams(
                vmem_limit_bytes=grant
            ),
            cost_estimate=pl.CostEstimate(flops=flops, bytes_accessed=moved, transcendentals=0),
            name=name,
        )(*operands, *extra)
        self.token = min(results, key=lambda result: result.size)
        return results


def pack_body(count, *refs):
    shards, out = refs[:count], refs[-1]
    feature = out.shape[1]
    offset = 0
    for shard in shards:
        rows, columns = shard.shape
        for block in range(columns // feature):
            out[offset : offset + rows, :] = shard[:, block * feature : (block + 1) * feature]
            offset += rows


def split_body(cut, from_x, from_y, top, lower):
    top[...] = from_x[:cut, :]
    lower[...] = from_y[cut:, :]


def vec_rows(vec_part, feature):
    rows = tile_up(-(-vec_part.shape[0] // feature))
    padded = jnp.pad(vec_part, (0, rows * feature - vec_part.shape[0]))
    return padded.reshape(rows, feature)


class Gather:
    def __init__(self, order, feature, name):
        self.order = order
        self.feature = feature
        self.name = name
        self.mine = []

    def sides(self, *shards):
        feature = self.feature
        rows = sum(shard.size for shard in shards) // feature
        (packed,) = self.order.kernel(
            functools.partial(pack_body, len(shards)),
            shards,
            [VMEM] * len(shards),
            [((rows, feature), jnp.bfloat16, VMEM)],
            [],
            self.name + "_pack",
            moved=4 * rows * feature,
        )
        self.mine = [packed, swap(packed, 2), swap(packed, 4)]

    def corners(self):
        rows, feature = self.mine[0].shape
        cut = rows // (2 * ROW_TILE) * ROW_TILE
        top, lower = self.order.kernel(
            functools.partial(split_body, cut),
            self.mine[1:3],
            [VMEM] * 2,
            [
                ((cut, feature), jnp.bfloat16, VMEM),
                ((rows - cut, feature), jnp.bfloat16, VMEM),
            ],
            [],
            self.name + "_split",
            moved=4 * rows * feature,
        )
        self.mine += [swap(top, 4), swap(lower, 2)]

    def join(self, *parts):
        rows, feature = self.mine[0].shape
        joined = self.order.kernel(
            functools.partial(join_body, parts),
            self.mine,
            [ANY] * 5,
            [((4 * count, feature), jnp.bfloat16, ANY) for first, count in parts],
            [pltpu.VMEM((4 * rows, feature), jnp.bfloat16), pltpu.SemaphoreType.DMA((5 + 4 * len(parts),))],
            self.name + "_join",
        )
        return [(part, swap(part, 1)) for part in joined]


def join_body(parts, own, from_x, from_y, top, lower, *refs):
    outs, stage, sems = refs[:-2], refs[-2], refs[-1]
    copies = []
    place = 0
    for index, source in enumerate((own, from_x, from_y, top, lower)):
        rows = source.shape[0]
        copy = pltpu.make_async_copy(source, stage.at[pl.ds(place, rows), :], sems.at[index])
        copy.start()
        copies.append(copy)
        place += rows
    block = own.shape[0]
    stores = []
    for chip in range(4):
        wait_all(copies[chip : chip + 1] if chip < 3 else copies[3:])
        for (first, count), out in zip(parts, outs):
            copy = pltpu.make_async_copy(
                stage.at[pl.ds(chip * block + first, count), :],
                out.at[pl.ds(chip * count, count), :],
                sems.at[5 + len(stores)],
            )
            copy.start()
            stores.append(copy)
    wait_all(stores)


LANES = 128


def chunk_count(length):
    return max(-(-((place * length) % LANES + length) // LANES) for place in range(8))


def vec_shards(vectors, chip_index, feature):
    parts = []
    for vector in vectors:
        length = vector.shape[0]
        blank = jnp.zeros((chunk_count(length) * LANES,), vector.dtype)
        parts.append(lax.dynamic_update_slice(blank, vector, ((chip_index * length) % LANES,)))
    return vec_rows(jnp.concatenate(parts), feature)


def vec_body(lengths, sections, table, mine, theirs, *refs):
    outs, landed, wide, sems = refs[:-3], refs[-3], refs[-2], refs[-1]
    rows = landed.shape[0] // 8
    feature = landed.shape[1]
    block = mine.shape[0] // 4
    copies = []
    for chip in range(4):
        for core, source in enumerate((mine, theirs)):
            copies.append(
                pltpu.make_async_copy(
                    source.at[pl.ds((chip + 1) * block - rows, rows), :],
                    landed.at[pl.ds(pl.multiple_of(table[2 * chip + core] * rows, ROW_TILE), rows), :],
                    sems.at[len(copies)],
                )
            )
    for copy in copies:
        copy.start()
    wait_all(copies)
    wide[...] = landed[...].astype(jnp.float32)
    per_row = feature // LANES
    outs = list(outs)
    skip = 0
    for length, section in zip(lengths, sections):
        targets = []
        for count in section:
            out = outs.pop(0)
            targets += [(out, row, lane * LANES) for row in range(count) for lane in range(per_row)]
        out = outs.pop(0)
        targets += [(out, 0, lane * LANES) for lane in range(out.shape[1] // LANES)]
        filled = set()
        for place in range(8):
            base = place * length // LANES
            used = -(-((place * length) % LANES + length) // LANES)
            for chunk in range(used):
                flat = (skip + chunk) * LANES
                row, lane = place * rows + flat // feature, flat % feature
                value = wide[row : row + 1, lane : lane + LANES]
                out, row, lane = targets[base + chunk]
                if base + chunk in filled:
                    value = value + out[row : row + 1, lane : lane + LANES]
                out[row : row + 1, lane : lane + LANES] = value
                filled.add(base + chunk)
        skip += chunk_count(length)


def gathered_vecs(order, buffers, table, rows, feature, lengths, sections):
    outs = []
    for length, section in zip(lengths, sections):
        outs += [((count, feature), jnp.float32, VMEM) for count in section]
        outs.append(((1, 8 * length - sum(section) * feature), jnp.float32, VMEM))
    return order.kernel(
        functools.partial(vec_body, lengths, sections),
        [table, *buffers],
        [SMEM] + [ANY] * 2,
        outs,
        [
            pltpu.VMEM((8 * rows, feature), jnp.bfloat16),
            pltpu.VMEM((8 * rows, feature), jnp.float32),
            pltpu.SemaphoreType.DMA((8,)),
        ],
        "vectors",
    )


class Loader:
    def __init__(self, buffers, table, sems, used=0):
        self.buffers = buffers
        self.block = buffers[0].shape[0] // 4
        self.table = table
        self.sems = sems
        self.used = used

    def unit(self, number, target, stride, first):
        rows = target.shape[1] // 8
        copies = []
        for chip in range(4):
            for core in range(2):
                offset = chip * self.block + number * rows
                place = pl.multiple_of(self.table[2 * chip + core] * stride + first, ROW_TILE)
                copy = pltpu.make_async_copy(
                    self.buffers[core].at[pl.ds(offset, rows), :],
                    target.at[pl.ds(place, rows), :],
                    self.sems.at[self.used],
                )
                copy.start()
                self.used += 1
                copies.append(copy)
        return copies

    def wide(self, number, target):
        return self.unit(number, target, target.shape[1] // 8, 0)

    def tall(self, number, target):
        rows = target.shape[1] // 8
        copies = []
        for block in range(4):
            copies += self.unit(number + block, target, 4 * rows, block * rows)
        return copies


def wait_all(copies):
    for copy in copies:
        copy.wait()


class Storer:
    def __init__(self, outs, table, slots, sems):
        self.keep, self.upper, self.lower = outs if len(outs) == 3 else (outs[0], None, outs[1])
        self.table = table
        self.slots = slots
        self.block = self.keep.shape[1] // 2
        self.sems = sems
        self.copies = []

    def add(self, source, out, row):
        copy = pltpu.make_async_copy(
            source, out.at[pl.ds(row, source.shape[0]), :], self.sems.at[len(self.copies)]
        )
        copy.start()
        self.copies.append(copy)

    def rows(self, source, stride, count, offset):
        for core in (1, 0):
            for slot in (2, 3, 0, 1):
                place = self.table[2 * self.slots[slot] + core] * stride
                block = source.at[pl.ds(pl.multiple_of(place, ROW_TILE), count), :]
                if core == 0:
                    self.add(block, self.keep, slot * self.block + offset)
                elif slot < 2 or self.upper is None:
                    self.add(block, self.lower, slot * self.block + offset)
                else:
                    self.add(block, self.upper, (slot - 2) * self.block + offset)

    def tail(self, source):
        self.add(source, self.lower, (4 if self.upper is None else 2) * self.block)
        self.add(source, self.keep, 4 * self.block)

    def finish(self):
        wait_all(self.copies)


def gradient_outs(feature, extra=0, single=False):
    rows = feature // 2
    if single:
        return [((4 * rows + extra, feature), jnp.bfloat16, ANY)] * 2
    return [((count, feature), jnp.bfloat16, ANY) for count in (4 * rows + extra, 2 * rows, 2 * rows + extra)]


def low(value):
    return value.astype(jnp.bfloat16)


def layer_norm(hidden, gain, shift):
    mean = jnp.mean(hidden, axis=-1, keepdims=True)
    centred = hidden - mean
    variance = jnp.mean(centred * centred, axis=-1, keepdims=True)
    return centred * lax.rsqrt(variance + EPSILON) * gain + shift


def layer_norm_back(hidden, gain, gradient):
    mean = jnp.mean(hidden, axis=-1, keepdims=True)
    centred = hidden - mean
    variance = jnp.mean(centred * centred, axis=-1, keepdims=True)
    scale = lax.rsqrt(variance + EPSILON)
    unit = centred * scale
    grad_gain = jnp.sum(gradient * unit, axis=0, keepdims=True)
    grad_shift = jnp.sum(gradient, axis=0, keepdims=True)
    inner = gradient * gain
    mean_inner = jnp.mean(inner, axis=-1, keepdims=True)
    mean_unit = jnp.mean(inner * unit, axis=-1, keepdims=True)
    return (scale * (inner - mean_inner - unit * mean_unit), grad_gain, grad_shift)


def key_mask(bucket, lengths, rows, segs, causal):
    span = rows // segs
    one_long = bucket[0] == 1
    query = lax.broadcasted_iota(jnp.int32, (rows, rows), 0)
    key = lax.broadcasted_iota(jnp.int32, (rows, rows), 1)
    key_row = lax.broadcasted_iota(jnp.int32, (1, rows), 1)
    limit = jnp.zeros((1, rows), jnp.int32)
    start = jnp.zeros((1, rows), jnp.int32)
    first = jnp.zeros((rows, 1), jnp.int32)
    query_col = lax.broadcasted_iota(jnp.int32, (rows, 1), 0)
    for seg in range(segs):
        inside = (key_row >= seg * span) & (key_row < (seg + 1) * span)
        limit = jnp.where(inside, seg * span + lengths[0, seg], limit)
        start = jnp.where(inside, seg * span, start)
        first = jnp.where((query_col >= seg * span) & (query_col < (seg + 1) * span), seg * span, first)
    limit = jnp.where(one_long, lengths[0, 0], limit)
    start = jnp.where(one_long, 0, start)
    first = jnp.where(one_long, 0, first)
    mask = (first == start) & (key < limit)
    if causal:
        mask = mask & (key <= query)
    return mask


def head_lanes(rows):
    return lax.broadcasted_iota(jnp.int32, (rows, PAIR), 1) < HEAD


def attn_body(
    cross, causal, first_unit, segs, table, bucket, lengths, *refs
):
    refs = list(refs)
    q_in = refs.pop(0)
    kv_in = refs.pop(0) if cross else q_in
    vec = refs.pop(0)
    buffers = [refs.pop(0) for _ in range(2)]
    hidden_out, norm_out, q_out, k_out, v_out, o_out, p_out = refs[:7]
    w_q, w_k, w_v, w_o, sems = refs[7:]
    rows, feature = q_in.shape
    load = Loader(buffers, table, sems)
    waits = [load.wide(first_unit + i, w) for i, w in enumerate((w_q, w_k, w_v, w_o))]
    mask = key_mask(bucket, lengths, rows, segs, causal)
    lanes = head_lanes(rows)
    wait_all(waits[0])
    q_out[...] = low(dot_plain(q_in[...], w_q[...]) + vec[0:1, :])
    wait_all(waits[1])
    k_out[...] = low(dot_plain(kv_in[...], w_k[...]))
    wait_all(waits[2])
    v_out[...] = low(dot_plain(kv_in[...], w_v[...]) + vec[1:2, :])
    for pair in range(feature // PAIR):
        columns = slice(pair * PAIR, (pair + 1) * PAIR)
        q_pair, k_pair, v_pair = q_out[:, columns], k_out[:, columns], v_out[:, columns]
        mixed = []
        for half in range(2):
            mine = lanes if half == 0 else ~lanes
            score = dot_right(jnp.where(mine, q_pair, jnp.zeros_like(q_pair)), k_pair)
            score = jnp.where(mask, score * SCORE_SCALE, NEG_FILL)
            power = jnp.exp(score - jnp.max(score, axis=-1, keepdims=True))
            probs = low(power / jnp.sum(power, axis=-1, keepdims=True))
            p_out[2 * pair + half] = probs
            mixed.append(dot_plain(probs, v_pair))
        o_out[:, columns] = low(jnp.where(lanes, mixed[0], mixed[1]))
    wait_all(waits[3])
    hidden = q_in[...].astype(jnp.float32) + (dot_plain(o_out[...], w_o[...]) + vec[2:3, :])
    hidden_out[...] = hidden
    norm_out[...] = low(layer_norm(hidden, vec[3:4, :], vec[4:5, :]))


def attn_forward(order, q_in, kv_in, vec, weights, ids, lengths, causal, name):
    rows, feature = q_in.shape
    sources = [q_in] + ([] if kv_in is None else [kv_in]) + [vec]
    wide = ((rows, feature), jnp.bfloat16, VMEM)
    return order.kernel(
        functools.partial(attn_body, kv_in is not None, causal, weights[1], lengths.shape[1]),
        [*ids, lengths, *sources, *weights[0]],
        [SMEM] * 3 + [VMEM] * len(sources) + [ANY] * 2,
        [((rows, feature), jnp.float32, VMEM)]
        + [wide] * 5
        + [((feature // HEAD, rows, rows), jnp.bfloat16, VMEM)],
        [pltpu.VMEM((feature, feature), jnp.bfloat16)] * 4 + [pltpu.SemaphoreType.DMA((32,))],
        name,
        8 * rows * feature * feature,
        10 * feature * feature,
    )


def gelu_parts(hidden):
    phi = 0.5 * (1.0 + lax.erf(hidden * 0.7071067811865476))
    slope = phi + hidden * (0.3989422804014327 * jnp.exp(-0.5 * hidden * hidden))
    return (hidden * phi, slope)


def feed_body(units, table, rows_in, vec, b_in, *refs):
    hidden_out, norm_out, r_out, slope_out, w_in, w_out, sems = refs[4:]
    feature = rows_in.shape[1]
    load = Loader(refs[:2], table, sems)
    waits = [load.wide(units[0] + j, w_in.at[j]) for j in range(4)]
    tail = Loader(refs[2:4], table, sems, load.used).tall(units[1], w_out)
    total = None
    for j in range(4):
        columns = slice(j * feature, (j + 1) * feature)
        wait_all(waits[j])
        hidden = dot_plain(rows_in[...], w_in[j]) + b_in[:, columns]
        active, slope = gelu_parts(hidden)
        r_out[:, columns] = low(active)
        slope_out[:, columns] = low(slope)
    wait_all(tail)
    total = dot_plain(r_out[...], w_out[...]) + vec[0:1, :]
    hidden = rows_in[...].astype(jnp.float32) + total
    hidden_out[...] = hidden
    norm_out[...] = low(layer_norm(hidden, vec[1:2, :], vec[2:3, :]))


def feed_forward(order, rows_in, vec, b_in, w_in, w_out, table, name):
    rows, feature = rows_in.shape
    width = b_in.shape[1]
    return order.kernel(
        functools.partial(feed_body, (w_in[1], w_out[1])),
        [table, rows_in, vec, b_in, *w_in[0], *w_out[0]],
        [SMEM] + [VMEM] * 3 + [ANY] * 4,
        [
            ((rows, feature), jnp.float32, VMEM),
            ((rows, feature), jnp.bfloat16, VMEM),
            ((rows, width), jnp.bfloat16, VMEM),
            ((rows, width), jnp.bfloat16, VMEM),
        ],
        [
            pltpu.VMEM((4, feature, feature), jnp.bfloat16),
            pltpu.VMEM((width, feature), jnp.bfloat16),
            pltpu.SemaphoreType.DMA((64,)),
        ],
        name,
        4 * rows * feature * width,
        8 * feature * width,
    )


def feed_back_out_body(extra, slots, table, *refs):
    refs = list(refs)
    gradient = refs.pop(0)[...].astype(jnp.float32)
    if extra:
        gradient = gradient + refs.pop(0)[...].astype(jnp.float32)
    hidden, gain, active, g_out, sums, keep, upper, lower, stage, out_sems = refs
    feature = hidden.shape[1]
    store = Storer((keep, upper, lower), table, slots, out_sems)
    gradient, grad_gain, grad_shift = layer_norm_back(hidden[...], gain[1:2, :], gradient)
    sums[0:1, :] = jnp.sum(gradient, axis=0, keepdims=True)
    sums[1:2, :] = grad_gain
    sums[2:3, :] = grad_shift
    g_out[...] = gradient
    grad_low = low(gradient)
    for j in range(4):
        columns = slice(j * feature, (j + 1) * feature)
        stage[columns, :] = low(dot_left(active[:, columns], grad_low))
    store.rows(stage, feature // 2, feature // 2, 0)
    store.finish()


def feed_back_out(order, gradients, hidden, gain, active, table, slots, name):
    rows, feature = hidden.shape
    width = active.shape[1]
    return order.kernel(
        functools.partial(feed_back_out_body, len(gradients) == 2, slots),
        [table, *gradients, hidden, gain, active],
        [SMEM] + [VMEM] * (len(gradients) + 3),
        [((rows, feature), jnp.float32, VMEM), ((3, feature), jnp.float32, VMEM), *gradient_outs(feature)],
        [pltpu.VMEM((width, feature), jnp.bfloat16), pltpu.SemaphoreType.DMA((8,))],
        name,
        2 * rows * feature * width,
        4 * feature * width,
    )


def feed_back_in_body(slots, units, table, gradient, slope, rows_in, *refs):
    total_out, bias_in, keep, upper, lower, w_in, w_out, grad_hidden, stage, sems, out_sems = refs[4:]
    feature = rows_in.shape[1]
    tail = Loader(refs[2:4], table, sems).tall(units[1], w_out)
    load = Loader(refs[:2], table, sems, len(tail))
    waits = [load.wide(units[0] + j, w_in.at[j]) for j in range(4)]
    store = Storer((keep, upper, lower), table, slots, out_sems)
    total = gradient[...]
    grad_low = low(total)
    wait_all(tail)
    for j in range(4):
        columns = slice(j * feature, (j + 1) * feature)
        hidden = dot_right(grad_low, w_out[columns, :]) * slope[:, columns].astype(jnp.float32)
        bias_in[j : j + 1, :] = jnp.sum(hidden, axis=0, keepdims=True)
        grad_hidden[:, columns] = low(hidden)
        stage[j] = low(dot_left(rows_in[...], grad_hidden[:, columns]))
        store.rows(stage.at[j], feature // 8, feature // 8, j * (feature // 8))
    for j in range(4):
        columns = slice(j * feature, (j + 1) * feature)
        wait_all(waits[j])
        total = total + dot_right(grad_hidden[:, columns], w_in[j])
    total_out[...] = total
    store.finish()


def feed_back_in(order, gradient, slope, rows_in, w_in, w_out, table, slots, name):
    rows, feature = rows_in.shape
    width = slope.shape[1]
    square = pltpu.VMEM((4, feature, feature), jnp.bfloat16)
    return order.kernel(
        functools.partial(feed_back_in_body, slots, (w_in[1], w_out[1])),
        [table, gradient, slope, rows_in, *w_in[0], *w_out[0]],
        [SMEM] + [VMEM] * 3 + [ANY] * 4,
        [((rows, feature), jnp.float32, VMEM), ((4, feature), jnp.float32, VMEM), *gradient_outs(feature)],
        [
            square,
            pltpu.VMEM((width, feature), jnp.bfloat16),
            pltpu.VMEM((rows, width), jnp.bfloat16),
            square,
            pltpu.SemaphoreType.DMA((64,)),
            pltpu.SemaphoreType.DMA((32,)),
        ],
        name,
        6 * rows * feature * width,
        6 * feature * width,
    )


def attn_back_body(cross, first_unit, others, slots, out_count, table, gradient, *refs):
    refs = list(refs)
    other_sums = [refs.pop(0) for _ in range(others)]
    hidden, gain, q_in = refs[:3]
    refs = refs[3:]
    kv_in = refs.pop(0) if cross else q_in
    queries, keys, values, mixed, probs_in = refs[:5]
    buffers = refs[5:7]
    refs = refs[7:]
    q_grad_out = refs.pop(0)
    kv_grad_out = refs.pop(0) if cross else None
    sums = refs.pop(0)
    grads = [refs.pop(0) for _ in range(out_count)]
    w_q, w_k, w_v, w_o, stage, go, gq, gk, gv, vec_low, sems, out_sems = refs
    rows, feature = hidden.shape
    unit = feature // 8
    load = Loader(buffers, table, sems)
    wait_o = load.wide(first_unit + 3, w_o)
    waits = [load.wide(first_unit + i, w) for i, w in enumerate((w_q, w_k, w_v))]
    store = Storer(grads, table, slots, out_sems)
    lanes = head_lanes(rows)
    total, grad_gain, grad_shift = layer_norm_back(hidden[...], gain[3:4, :], gradient[...])
    sums[2:3, :] = jnp.sum(total, axis=0, keepdims=True)
    sums[3:4, :] = grad_gain
    sums[4:5, :] = grad_shift
    grad_low = low(total)
    stage[3] = low(dot_left(mixed[...], grad_low))
    store.rows(stage.at[3], unit, unit, 3 * unit)
    wait_all(wait_o)
    go[...] = low(dot_right(grad_low, w_o[...]))
    for pair in range(feature // PAIR):
        columns = slice(pair * PAIR, (pair + 1) * PAIR)
        q_pair, k_pair, v_pair = queries[:, columns], keys[:, columns], values[:, columns]
        go_pair = go[:, columns]
        parts = []
        for half in range(2):
            mine = lanes if half == 0 else ~lanes
            probs_low = probs_in[2 * pair + half]
            probs = probs_low.astype(jnp.float32)
            grad_probs = dot_right(jnp.where(mine, go_pair, jnp.zeros_like(go_pair)), v_pair)
            weighted = grad_probs * probs
            row_sum = jnp.sum(weighted, axis=-1, keepdims=True)
            grad_raw = low((weighted - probs * row_sum) * SCORE_SCALE)
            parts.append(
                (
                    dot_plain(grad_raw, k_pair),
                    dot_left(grad_raw, q_pair),
                    dot_left(probs_low, go_pair),
                )
            )
        grad_q, grad_k, grad_v = (jnp.where(lanes, a, b) for a, b in zip(*parts))
        sums[0:1, columns] = jnp.sum(grad_q, axis=0, keepdims=True)
        sums[1:2, columns] = jnp.sum(grad_v, axis=0, keepdims=True)
        gq[:, columns] = low(grad_q)
        gk[:, columns] = low(grad_k)
        gv[:, columns] = low(grad_v)
    if others:
        parts = [sums[...]] + [other[...] for other in other_sums]
        count = sum(part.shape[0] for part in parts)
        parts.append(jnp.zeros((vec_low.shape[0] - count, feature), jnp.float32))
        vec_low[...] = low(jnp.concatenate(parts, axis=0))
        store.tail(vec_low)
    for index, (source, grad) in enumerate(((q_in, gq), (kv_in, gk), (kv_in, gv))):
        stage[index] = low(dot_left(source[...], grad[...]))
        store.rows(stage.at[index], unit, unit, index * unit)
    for copies in waits:
        wait_all(copies)
    total = total + dot_right(gq[...], w_q[...])
    kv_total = dot_right(gk[...], w_k[...]) + dot_right(gv[...], w_v[...])
    if cross:
        q_grad_out[...] = total
        kv_grad_out[...] = kv_total
    else:
        q_grad_out[...] = total + kv_total
    store.finish()


def attn_back(
    order, gradient, hidden, gain, q_in, kv_in, saved, weights, table, others, slots, name, single=False
):
    rows, feature = hidden.shape
    cross = kv_in is not None
    sources = [gradient, *others, hidden, gain, q_in] + ([kv_in] if cross else []) + list(saved)
    count = tile_up(5 + sum(other.shape[0] for other in others)) if others else 0
    return order.kernel(
        functools.partial(attn_back_body, cross, weights[1], len(others), slots, 2 if single else 3),
        [table, *sources, *weights[0]],
        [SMEM] + [VMEM] * len(sources) + [ANY] * 2,
        [((rows, feature), jnp.float32, VMEM)] * (1 + cross)
        + [((5, feature), jnp.float32, VMEM), *gradient_outs(feature, count, single)],
        [pltpu.VMEM((feature, feature), jnp.bfloat16)] * 4
        + [pltpu.VMEM((4, feature, feature), jnp.bfloat16)]
        + [pltpu.VMEM((rows, feature), jnp.bfloat16)] * 4
        + [pltpu.VMEM((max(count, ROW_TILE), feature), jnp.bfloat16)]
        + [pltpu.SemaphoreType.DMA((32,)), pltpu.SemaphoreType.DMA((34,))],
        name,
        16 * rows * feature * feature,
        20 * feature * feature,
    )


def combine_body(plan, count, *refs):
    inputs = refs[:count]
    outs = refs[count:-4]
    landed, summed, in_sems, out_sems = refs[-4:]
    loads = []
    place = 0
    for out, first, rows, terms in plan:
        parts = []
        for source, row in terms:
            copy = pltpu.make_async_copy(
                inputs[source].at[pl.ds(row, rows), :],
                landed.at[pl.ds(place, rows), :],
                in_sems.at[sum(len(other) for other in loads) + len(parts)],
            )
            copy.start()
            parts.append((copy, place))
            place += rows
        loads.append(parts)
    stores = []
    place = 0
    for (out, first, rows, terms), parts in zip(plan, loads):
        total = None
        for copy, start in parts:
            copy.wait()
            term = landed[start : start + rows, :].astype(jnp.float32)
            total = term if total is None else total + term
        summed[place : place + rows, :] = low(total)
        copy = pltpu.make_async_copy(
            summed.at[pl.ds(place, rows), :],
            outs[out].at[pl.ds(first, rows), :],
            out_sems.at[len(stores)],
        )
        copy.start()
        stores.append(copy)
        place += rows
    wait_all(stores)


def combine(order, name, *jobs):
    inputs, plan, outs = [], [], []
    for sizes, sums, use in jobs:
        for out, first, rows, terms in sums:
            places = []
            for array, row in terms:
                known = [index for index, other in enumerate(inputs) if other is array]
                if not known:
                    inputs.append(array)
                places.append((known[0] if known else len(inputs) - 1, row))
            plan.append((len(outs) + out, first, rows, tuple(places)))
        outs += sizes
    feature = inputs[0].shape[1]
    reads = sum(rows * len(terms) for out, first, rows, terms in plan)
    writes = sum(rows for out, first, rows, terms in plan)
    results = order.kernel(
        functools.partial(combine_body, plan, len(inputs)),
        inputs,
        [ANY] * len(inputs),
        [((rows, feature), jnp.bfloat16, ANY) for rows in outs],
        [
            pltpu.VMEM((reads, feature), jnp.bfloat16),
            pltpu.VMEM((writes, feature), jnp.bfloat16),
            pltpu.SemaphoreType.DMA((sum(len(terms) for out, first, rows, terms in plan),)),
            pltpu.SemaphoreType.DMA((len(plan),)),
        ],
        name,
    )
    for sizes, sums, use in jobs:
        use(*results[: len(sizes)])
        results = results[len(sizes) :]


OWN, X, Y, DIAGONAL = range(4)
X_FIRST = (OWN, Y, X, DIAGONAL)
Y_FIRST = (OWN, X, Y, DIAGONAL)


class Reduce:
    def __init__(self, order, outs, slots, both=False, pad=0):
        self.order = order
        self.pad = pad
        self.keep, self.upper, self.lower = outs if len(outs) == 3 else (outs[0], None, outs[1])
        self.both = both
        self.bits = (2, 4) if slots == X_FIRST else (4, 2)
        self.rows = self.keep.shape[1] // 2
        self.extra = self.keep.shape[0] - 4 * self.rows

    def cores(self):
        self.from_upper = None if self.upper is None else swap(self.order.tie(self.upper), 1)
        self.from_lower = swap(self.order.tie(self.lower), 1)

    def cores_done(self):
        self.order.mark(*(value for value in (self.from_upper, self.from_lower) if value is not None))

    def block(self, slot, first=0):
        row = slot * self.rows + first
        other = (self.from_lower, row) if slot < 2 or self.upper is None else (self.from_upper, row - 2 * self.rows)
        return ((self.keep, row), other)

    def extra_rows(self):
        return ((self.keep, 4 * self.rows), (self.from_lower, (4 if self.upper is None else 2) * self.rows))

    def first(self):
        rows, extra = self.rows, self.extra
        if not self.both:
            plan = [(0, 0, rows, self.block(2)), (0, rows, rows, self.block(3))]
            if extra:
                plan.append((0, 2 * rows, extra, self.extra_rows()))
            if self.pad:
                plan.append((0, 2 * rows + extra, self.pad, self.block(2)[:1]))
            return ([2 * rows + extra + self.pad], plan, self.first_sent)
        cut = rows // 2
        plan = [(0, 0, cut, self.block(3)), (1, 0, cut, self.block(3, cut))]
        if extra:
            plan.append((0, cut, extra, self.extra_rows()))
        return ([cut + extra, cut], plan, self.first_sent)

    def first_sent(self, *sent):
        self.sent = sent[0]
        self.landed = [swap(value, bit) for value, bit in zip(sent, (2, 4) if self.both else self.bits)]

    def second(self):
        rows, extra = self.rows, self.extra
        if not self.both:
            landed = self.landed[0]
            plan = [(0, 0, rows, self.block(1) + ((landed, rows),))]
            if extra:
                plan.append((0, rows, extra, ((self.sent, 2 * rows), (landed, 2 * rows))))
            return ([rows + extra], plan, self.second_sent)
        cut = rows // 2
        from_x, from_y = self.landed
        plan = [
            (0, 0, cut, self.block(1)),
            (0, cut, cut, self.block(1, cut) + ((from_y, 0),)),
            (1, 0, cut, self.block(2) + ((from_x, 0),)),
            (1, cut, cut, self.block(2, cut)),
        ]
        if extra:
            plan.append((1, rows, extra, ((self.sent, cut), (from_x, cut))))
        return ([rows, rows + extra], plan, self.second_sent)

    def second_sent(self, *sent):
        self.sent_last = sent[-1]
        self.last = [swap(value, bit) for value, bit in zip(sent, (2, 4) if self.both else self.bits[1:])]

    def own(self, use):
        rows, extra = self.rows, self.extra
        terms = self.block(0) + tuple((value, 0) for value in self.last)
        if not self.both:
            terms += ((self.landed[0], 0),)
        plan = [(0, 0, rows, terms)]
        if extra:
            plan.append((0, rows, extra, ((self.sent_last, rows), (self.last[-1], rows))))
        return ([rows + extra], plan, use)


def own_stack(pieces, use):
    rows = pieces[0].rows
    plan = [(0, index * rows) + piece.own(None)[1][0][2:] for index, piece in enumerate(pieces)]
    return ([len(pieces) * rows], plan, use)


class Line:
    def __init__(self, value):
        self.value = value
        self.landed = lax.ppermute(value, "rep", [(0, 1), (3, 2)])

    def part(self, first):
        return (self, first)

    def step(self, use):
        rows = self.value.shape[0]
        return ([rows], [(0, 0, rows, ((self.value, 0), (self.landed, 0)))], use)

    def middle(self):
        return self.step(self.middle_sent)

    def middle_sent(self, value):
        self.value = value
        self.landed = lax.ppermute(value, "rep", [(1, 2), (2, 1)])

    def outward(self):
        return self.step(self.outward_sent)

    def outward_sent(self, value):
        self.value = value
        self.landed = lax.ppermute(value, "rep", [(1, 0), (2, 3)])


def finish_body(parts, inner, *refs):
    wide, rest = refs[2 * len(parts)], list(refs[2 * len(parts) + 1 :])
    feature = refs[0].shape[1]
    unit = feature // 8
    for index, first in enumerate(parts):
        value, landed = refs[2 * index], refs[2 * index + 1]

        def rows(begin, count):
            mine = value[first + begin : first + begin + count, :].astype(jnp.float32)
            other = landed[first + begin : first + begin + count, :].astype(jnp.float32)
            return jnp.where(inner[0] == 1, mine, other)

        for j in range(4):
            column = (4 * index + j) * feature
            if wide.shape[0] == unit:
                wide[:, column : column + feature] = rows(j * unit, unit)
            else:
                wide[j * unit : (j + 1) * unit, :] = rows(j * unit, unit)
        if first == 0 and value.shape[0] % (4 * unit):
            rest.pop(0)[...] = rows(4 * unit, value.shape[0] - 4 * unit)


def finish(order, inner, parts, wide, name):
    operands = [inner]
    for line, first in parts:
        operands += [line.value, line.landed]
    feature = operands[1].shape[1]
    unit = feature // 8
    shape = (unit, 4 * feature * len(parts)) if wide else (4 * unit, feature)
    outs = [(shape, jnp.float32, VMEM)]
    for line, first in parts:
        rows = line.value.shape[0] % (4 * unit)
        if rows:
            outs.append(((rows, feature), jnp.float32, VMEM))
    return order.kernel(
        functools.partial(finish_body, [first for line, first in parts]),
        operands,
        [SMEM] + [VMEM] * (len(operands) - 1),
        outs,
        [],
        name,
    )


def per_device(
    enc_in,
    dec_in,
    bucket,
    enc_lengths,
    dec_lengths,
    enc_attn,
    enc_vec,
    enc_w1,
    enc_w2,
    dec_attn,
    dec_vec,
    dec_w1,
    dec_w2,
    enc_cot,
    dec_cot,
):
    feature = enc_in.shape[1]
    unit = feature // 8
    chip_index = lax.axis_index("fsdp").astype(jnp.int32)
    table = chip_index ^ jnp.arange(8, dtype=jnp.int32)
    place = lax.axis_index("rep")
    inner = ((place == 1) | (place == 2)).astype(jnp.int32).reshape(1)
    ids = (table, bucket)
    order = Order()
    mark = order.mark
    g_1, g_2, g_3, g_4 = (Gather(order, feature, "piece_" + name) for name in "1234")
    half = 4 * unit
    e_len, d_len = enc_vec.shape[0], dec_vec.shape[0]
    vec_part = vec_shards([enc_vec, dec_vec], chip_index, feature)
    g_1.sides(enc_attn, dec_attn[:, : 4 * feature], vec_part)
    g_2.sides(enc_w1, enc_w2)
    g_1.corners()
    g_2.corners()
    mark(*g_2.mine[3:])
    (attn_pair,) = g_1.join((0, 2 * half + vec_part.shape[0]))
    (e_feed,) = g_2.join((0, 2 * half))
    g_3.sides(dec_attn[:, 4 * feature :], dec_w1)
    e_attn_vec, e_feed_vec, e_tail, d_self_vec, d_cross_vec, d_feed_vec, d_tail = gathered_vecs(
        order, attn_pair, table, vec_part.shape[0], feature, (e_len, d_len), ((5, 3), (5, 5, 3))
    )
    e_hid_a, e_first, *e_saved = attn_forward(
        order, enc_in, None, e_attn_vec, (attn_pair, 0), ids, enc_lengths, False, "enc_attn"
    )
    mark(e_feed[1])
    g_4.sides(dec_w2)
    d_hid_s, d_first, *s_saved = attn_forward(
        order, dec_in, None, d_self_vec, (attn_pair, 4), ids, dec_lengths, True, "dec_self"
    )
    g_3.corners()
    e_hid_f, encoded, e_act, e_slope = feed_forward(
        order, e_first, e_feed_vec, e_tail, (e_feed, 0), (e_feed, 4), table, "enc_feed"
    )
    g_4.corners()
    cross_pair, w1_pair = g_3.join((0, half), (half, half))
    (w2_pair,) = g_4.join((0, half))
    d_hid_c, d_second, *c_saved = attn_forward(
        order, d_first, encoded, d_cross_vec, (cross_pair, 0), ids, enc_lengths, False, "dec_cross"
    )
    d_hid_f, decoded, d_act, d_slope = feed_forward(
        order, d_second, d_feed_vec, d_tail, (w1_pair, 0), (w2_pair, 0), table, "dec_feed"
    )
    gradient, d_sums_f, *outs = feed_back_out(
        order, [dec_cot], d_hid_f, d_feed_vec, d_act, table, X_FIRST, "dec_back_out"
    )
    red_0 = Reduce(order, outs, X_FIRST)
    red_0.cores()
    gradient, d_bias, *outs = feed_back_in(
        order, gradient, d_slope, d_second, (w1_pair, 0), (w2_pair, 0), table, Y_FIRST, "dec_back_in"
    )
    red_1 = Reduce(order, outs, Y_FIRST)
    red_0.cores_done()
    combine(order, "add_1", red_0.first())
    red_1.cores()
    gradient, grad_encoded, d_sums_c, *outs = attn_back(
        order, gradient, d_hid_c, d_cross_vec, d_first, encoded, c_saved, (cross_pair, 0), table, [],
        X_FIRST, "cross_back",
    )
    red_2 = Reduce(order, outs, X_FIRST)
    red_1.cores_done()
    combine(order, "add_2", red_1.first())
    red_2.cores()
    e_gradient, e_sums_f, *outs = feed_back_out(
        order, [enc_cot, grad_encoded], e_hid_f, e_feed_vec, e_act, table, Y_FIRST, "enc_back_out"
    )
    red_3 = Reduce(order, outs, Y_FIRST, pad=2 * ROW_TILE)
    combine(order, "add_3a", red_0.second())
    red_2.cores_done()
    combine(order, "add_3b", red_2.first())
    red_3.cores()
    e_gradient, e_bias, *outs = feed_back_in(
        order, e_gradient, e_slope, e_first, (e_feed, 0), (e_feed, 4), table, X_FIRST, "enc_back_in"
    )
    red_4 = Reduce(order, outs, X_FIRST)
    totals = {}

    def keep_as(key):
        return lambda value: totals.update({key: value})

    mark(*red_0.last)
    combine(order, "add_4a", red_1.second())
    red_3.cores_done()
    combine(order, "add_4b", red_3.first())
    red_4.cores()
    dec_in_grad, d_sums_s, *outs = attn_back(
        order, gradient, d_hid_s, d_self_vec, dec_in, None, s_saved, (attn_pair, 4), table,
        [d_sums_c, d_sums_f, d_bias], Y_FIRST, "self_back",
    )
    red_5 = Reduce(order, outs, Y_FIRST, True)
    combine(order, "add_5a", red_2.second())
    mark(*red_1.last)
    red_4.cores_done()
    combine(order, "add_5b", red_4.first())
    red_5.cores()
    enc_in_grad, e_sums_a, *outs = attn_back(
        order, e_gradient, e_hid_a, e_attn_vec, enc_in, None, e_saved, (attn_pair, 0), table,
        [e_sums_f, e_bias], Y_FIRST, "enc_attn_back", True,
    )
    red_6 = Reduce(order, outs, Y_FIRST, True)
    red_5.cores_done()
    mark(*red_2.last)
    combine(
        order, "add_6a", red_3.second(), red_4.second(), own_stack([red_0, red_1], keep_as("a"))
    )
    line_a = Line(totals["a"])
    red_6.cores()
    red_6.cores_done()
    mark(*red_3.last, *red_4.last)
    combine(order, "add_6b", red_5.first(), red_6.first())
    combine(order, "add_6c", own_stack([red_2, red_3], keep_as("b")), red_4.own(keep_as(4)))
    combine(order, "add_7", line_a.middle())
    mark(*red_6.landed)
    combine(order, "add_8", red_5.second())
    line_b = Line(order.tie(totals["b"]))
    line_4 = Line(order.tie(totals[4]))
    combine(order, "add_9", red_6.second(), red_5.own(keep_as(5)), line_a.outward())
    combine(order, "add_10", line_b.middle())
    combine(order, "add_11", red_6.own(keep_as(6)), line_4.middle())
    line_5 = Line(order.tie(totals[5]))
    line_6 = Line(totals[6])
    mark(line_a.landed)
    combine(order, "add_12", line_b.outward())
    (grad_d_w2,) = finish(order, inner, [line_a.part(0)], False, "out_0")
    (grad_d_w1,) = finish(order, inner, [line_a.part(half)], True, "out_1")
    combine(order, "add_13", line_4.outward(), line_5.middle(), line_6.middle())
    mark(line_b.landed)
    combine(order, "add_14", line_5.outward())
    (grad_e_w2,) = finish(order, inner, [line_b.part(half)], False, "out_3")
    (grad_e_w1,) = finish(order, inner, [line_4.part(0)], True, "out_4")
    combine(order, "add_15", line_6.outward())
    grad_d_attn, d_vec = finish(order, inner, [line_5.part(0), line_b.part(0)], True, "out_5")
    grad_e_attn, e_vec = finish(order, inner, [line_6.part(0)], True, "out_6")

    def own_part(rows, length):
        return lax.dynamic_slice(rows.reshape(-1), (chip_index * length,), (length,))

    return (
        encoded,
        decoded,
        enc_in_grad,
        dec_in_grad,
        grad_e_attn,
        own_part(e_vec, e_len),
        grad_e_w1,
        grad_e_w2,
        grad_d_attn,
        own_part(d_vec, d_len),
        grad_d_w1,
        grad_d_w2,
    )


def solution(mesh):
    in_specs = (
        P(("rep", "fsdp"), None),
        P(("rep", "fsdp"), None),
        P(("rep", "fsdp")),
        P(("rep", "fsdp"), None),
        P(("rep", "fsdp"), None),
        P("fsdp", None),
        P("fsdp"),
        P("fsdp", None),
        P("fsdp", None),
        P("fsdp", None),
        P("fsdp"),
        P("fsdp", None),
        P("fsdp", None),
        P(("rep", "fsdp"), None),
        P(("rep", "fsdp"), None),
    )
    out_specs = (
        P(("rep", "fsdp"), None),
        P(("rep", "fsdp"), None),
        P(("rep", "fsdp"), None),
        P(("rep", "fsdp"), None),
        P("fsdp", None),
        P("fsdp"),
        P("fsdp", None),
        P("fsdp", None),
        P("fsdp", None),
        P("fsdp"),
        P("fsdp", None),
        P("fsdp", None),
    )
    small = mesh.shape["fsdp"] == 8 and mesh.shape["rep"] == 4
    return jax.shard_map(
        per_device if small else per_device_any, mesh=mesh, in_specs=in_specs, out_specs=out_specs, check_vma=False
    )
```
